128 devices in a mesh: inst: 32 (over z, y, x_hi), span: 2 (over core), rad: 2 (over x_lo).
Axes of the slice: x: 4 (x_hi: 2, x_lo: 2; x = x_hi * 2 + x_lo), y: 4, z: 4, core: 2. Of those that a mesh axis runs over, the one named last changes fastest.
Arguments:
- adjoint_start: float32 [64, 5, 32, 1024], P('inst', None, 'rad', 'span'), may hold values from -6 to 6
- jac_rad: bfloat16 [64, 5, 5, 32, 1024], P('inst', None, None, 'rad', 'span'), may hold values from -2.5 to 2.5
- jac_circ: bfloat16 [64, 5, 5, 32, 1024], P('inst', None, None, 'rad', 'span'), may hold values from -2.5 to 2.5
- dissip: float32 [32, 1024], P('rad', 'span'), may hold values from 0.5 to 4
- pseudo_step: float32 [32, 1024], P('rad', 'span'), may hold values from 0.1 to 0.4
- source: float32 [64, 5, 32, 1024], P('inst', None, 'rad', 'span'), may hold values from -6 to 6
- node_cell: int32 [4096], P(('span', 'rad')), may hold values from 0 to 8191
- node_owner: int32 [4096, 1], P(('span', 'rad')), may hold values from 0 to 1; in each aligned block of 1024 rows (0 to 1023, 1024 to 2047, ...) at most 1024 rows name the same one
- node_local: int32 [4096], P(('span', 'rad')), may hold values from 0 to 31
- shape_deriv: bfloat16 [64, 5, 3, 4096], P('inst', None, None, ('span', 'rad')), may hold values from -0.119628906 to 0.119628906
Outputs:
- adjoint: float32 [64, 5, 32, 1024], P('inst', None, 'rad', 'span')
- sensitivity: float32 [3, 64], P(None, 'span')
The draws below stay inside these ranges and needn't reach their ends.
Inputs may be any that keep to these rules, and one draw needn't show every extreme that they name: `node_owner`: among the node entries of one span and rad index, no owner is named more than 1024 times.
All inputs are finite; a program needn't handle non-finite values.
Results may differ from the reference program's by a relative error of at most 0.0003.
Values sent between devices are 32-bit elements; how exact they have to be, the bound alone decides.
No kernel may reach another device: no remote copies, remote signals or barrier semaphores. Data moves between devices by JAX's collectives and lax.ppermute only.
A program may use at most 64 MiB of HBM per device.

```python
import math
import jax
import jax.numpy as jnp
import numpy as np
from jax import lax

NFLD = 5
CR = 16
CTH = 512
ITERS = 2
KD = 3
NODES = 1024
VAR_DEV = 32
NT = 64
NR = 32
NTH = 1024
NVAR = 64
NODES_ALL = 4096
CAP = 1024
N_SPAN = 2
N_RAD = 2


def place_ends(drawn, stream_key, low, largest):
    spot = [jax.random.randint(jax.random.fold_in(stream_key, axis), (), 0, length) for axis, length in enumerate(drawn.shape)]
    longest = drawn.shape.index(max(drawn.shape))
    beside = spot[:longest] + [(spot[longest] + 1) % drawn.shape[longest]] + spot[longest + 1:]
    return drawn.at[tuple(spot)].set(low).at[tuple(beside)].set(largest)


def block_levels(rng, shape, split, low, top_value):
    def one(axis_at, shards_of):
        steps = jax.random.uniform(jax.random.fold_in(jax.random.fold_in(rng, 6), axis_at), (shards_of,), jnp.float32, low / len(split), top_value / len(split))
        return jnp.repeat(jnp.exp(steps), shape[axis_at] // shards_of).reshape((-1,) + (1,) * (len(shape) - axis_at - 1))

    loudness = one(*split[0])
    for cut in split[1:]:
        loudness = loudness * one(*cut)
    return loudness


def assign_block(key, own, number, rows, amount, top, most, skew):
    order = jax.random.permutation(key, amount)
    crowded, ordinary = shares(amount, rows * top, most, skew, True), shares(amount, rows * top, most, skew, False)
    places = jnp.arange(amount)

    def named(lengths, turn):
        used = int((lengths > 0).sum())
        fixed = max(1, used // 4)
        shifted = fixed + (places - fixed + turn * (used - fixed)) % max(1, amount - fixed)
        return jnp.zeros((amount,), jnp.int32).at[order[jnp.where(places < fixed, places, shifted)]].set(jnp.asarray(lengths, jnp.int32))

    lengths = jnp.where(number % 4 == 0, named(crowded, number // 4), named(ordinary, number - number // 4 - 1))
    mixed = jax.random.permutation(jax.random.fold_in(own, 3), amount)
    source_of, taker = mixed[0:amount // 2 * 2:2], mixed[1:amount // 2 * 2:2]
    slack = jnp.minimum(lengths[source_of] - 1, most - lengths[taker]) // 2
    slack = jnp.where((source_of == order[0]) | (taker == order[0]) | (lengths[taker] == 0), 0, jnp.maximum(slack, 0))
    shifted = jax.random.randint(jax.random.fold_in(own, 4), (amount // 2,), 0, 1 << 20) % (slack + 1)
    lengths = lengths.at[source_of].add(-shifted).at[taker].add(shifted)
    labels = jnp.searchsorted(jnp.cumsum(lengths), jnp.arange(rows * top), side="right").astype(jnp.int32)
    table = labels.reshape(top, rows).T
    table = table[jax.random.permutation(jax.random.fold_in(own, 1), rows)]
    turn = jax.random.randint(jax.random.fold_in(own, 2), (rows, 1), 0, top)
    return jnp.take_along_axis(table, (jnp.arange(top)[None, :] + turn) % top, axis=1)


def shares(amount, total, reach, slope, full):
    weights = [(1 << 20) // math.isqrt(grade ** slope) + 1 for grade in range(1, amount + 1)]
    largest = reach if full else min(reach, max(-(-total // amount), total * weights[0] // sum(weights)))
    least = 1 if total - largest >= amount - 1 else 0
    given, rest = [largest] + [least] * (amount - 1), total - largest - least * (amount - 1)
    while rest > 0:
        free = [i for i in range(1, amount) if given[i] < largest] or [i for i in range(1, amount) if given[i] < reach]
        pool, left = sum([weights[i] for i in free]), rest
        for i in free:
            extra = min(reach - given[i], max(1, left * weights[i] // pool), rest)
            given[i] = given[i] + extra
            rest = rest - extra
    return np.array(given)


def normal_values(key, extent, spread, reach, cuts=(), held_as=jnp.bfloat16):
    entries = jax.random.normal(key, extent, jnp.float32) * spread
    if len(cuts) > 0:
        entries = block_levels(key, extent, cuts, -0.22, 0.18) * entries
    return jnp.clip(entries, min=-reach, max=reach).astype(held_as)


def setup_inputs(seed: int = 0) -> dict:
    arg_keys = jax.random.split(jax.random.key(seed), 11)
    adjoint_start = normal_values(arg_keys[0], (NT, NFLD, NR, NTH), 1.0, 6.0, ((0, 32), (2, 2), (3, 2)), jnp.float32)
    jac_rad = normal_values(arg_keys[1], (NT, NFLD, NFLD, NR, NTH), NFLD ** -0.5, 2.5, ((0, 32), (3, 2), (4, 2)))
    jac_circ = normal_values(arg_keys[2], (NT, NFLD, NFLD, NR, NTH), NFLD ** -0.5, 2.5, ((0, 32), (3, 2), (4, 2)))
    dissip = jnp.clip(jnp.exp(math.log(4.0) - 2.0794415 * jax.random.uniform(arg_keys[3], (NR, NTH), jnp.float32) ** block_levels(arg_keys[3], (NR, NTH), ((0, 2), (1, 2)), -0.2, 0.2)), 0.5, 4.0)
    pseudo_step = jnp.clip(jnp.exp(math.log(0.4) - 1.3862944 * jax.random.uniform(arg_keys[4], (NR, NTH), jnp.float32) ** block_levels(arg_keys[4], (NR, NTH), ((0, 2), (1, 2)), -0.2, 0.2)), 0.1, 0.4)
    source = normal_values(arg_keys[5], (NT, NFLD, NR, NTH), 1.0, 6.0, ((0, 32), (2, 2), (3, 2)), jnp.float32)
    node_cell = place_ends(jax.random.randint(arg_keys[6], (NODES_ALL,), 0, CR * CTH), jax.random.fold_in(arg_keys[6], 1), 0, (CR * CTH) - 1).astype(jnp.int32)
    node_owner_keys = jax.random.split(jax.random.fold_in(arg_keys[7], 1), NODES_ALL // NODES)
    node_owner_turns = jax.random.permutation(jax.random.fold_in(arg_keys[7], 3), NODES_ALL // NODES)
    node_owner = jax.vmap(lambda own, number: assign_block(jax.random.fold_in(arg_keys[7], 2), own, number, NODES, N_SPAN, 1, CAP, 2))(node_owner_keys, node_owner_turns).reshape((NODES_ALL, 1))
    node_local = place_ends(jax.random.randint(arg_keys[8], (NODES_ALL,), 0, VAR_DEV), jax.random.fold_in(arg_keys[8], 1), 0, VAR_DEV - 1).astype(jnp.int32)
    shape_deriv = normal_values(arg_keys[9], (NT, NFLD, KD, NODES_ALL), 0.02, 0.119628906, ((0, 32), (3, 4)))
    return dict(adjoint_start=adjoint_start, jac_rad=jac_rad, jac_circ=jac_circ, dissip=dissip, pseudo_step=pseudo_step, source=source, node_cell=node_cell, node_owner=node_owner, node_local=node_local, shape_deriv=shape_deriv)


eps_fourth = 0.0625


def spectral_table(count):
    index = jnp.arange(count, dtype=jnp.int32)
    diff = index[:, None] - index[None, :]
    safe = jnp.where(diff == 0, 1, diff).astype(jnp.float32)
    tangent = jnp.tan(jnp.pi * safe / count)
    parity = jnp.where(diff % 2 == 0, 1.0, -1.0).astype(jnp.float32)
    return jnp.where(diff == 0, 0.0, 0.5 * parity / tangent).astype(jnp.float32)


def apply_transposed(jac, vec):
    total = jac[:, 0].astype(jnp.float32) * vec[:, 0:1]
    for field in range(1, 5):
        total = total + jac[:, field].astype(jnp.float32) * vec[:, field:field + 1]
    return total


def adjoint_residual(psi, jac_rad, jac_circ, dissip, source, table):
    count = psi.shape[2]
    width = psi.shape[3]
    radial = jnp.pad(psi, ((0, 0), (0, 0), (2, 2), (0, 0)))
    circle = jnp.concatenate([psi[..., width - 2:], psi, psi[..., :2]], axis=3)
    conv = apply_transposed(jac_rad, 0.5 * (radial[:, :, 1:count + 1] - radial[:, :, 3:count + 3]))
    conv = conv + apply_transposed(jac_circ, 0.5 * (circle[..., 1:width + 1] - circle[..., 3:width + 3]))
    fourth = radial[:, :, 4:] - 4.0 * radial[:, :, 3:count + 3] + 6.0 * psi - 4.0 * radial[:, :, 1:count + 1] + radial[:, :, :count]
    fourth = fourth + circle[..., 4:] - 4.0 * circle[..., 3:width + 3] + 6.0 * psi - 4.0 * circle[..., 1:width + 1] + circle[..., :width]
    time = jnp.einsum("st,sfrc->tfrc", table, psi, precision=lax.Precision.HIGHEST)
    return conv + eps_fourth * dissip * fourth + time - source


def reference(adjoint_start, jac_rad, jac_circ, dissip, pseudo_step, source, node_cell, node_owner, node_local, shape_deriv):
    table = spectral_table(NT)
    psi = adjoint_start
    for step in range(ITERS):
        psi = psi - pseudo_step * adjoint_residual(psi, jac_rad, jac_circ, dissip, source, table)
    block = jnp.arange(NODES_ALL, dtype=jnp.int32) // NODES
    span_index = block // N_RAD
    rad_index = block % N_RAD
    row_cell = rad_index * CR + node_cell // CTH
    col_cell = span_index * CTH + node_cell % CTH
    values = psi[:, :, row_cell, col_cell]
    rows = jnp.einsum("tfn,tfkn->kn", values, shape_deriv.astype(jnp.float32), precision=lax.Precision.HIGHEST)
    variable = (node_owner[:, 0] * VAR_DEV + node_local).astype(jnp.int32)
    sensitivity = jnp.zeros((KD, NVAR), jnp.float32).at[:, variable].add(rows)
    return psi, sensitivity
```

```python
import jax
import jax.numpy as jnp
import numpy as np
from jax import lax
from jax.experimental import pallas as pl
from jax.experimental.pallas import tpu as pltpu
from jax.sharding import PartitionSpec as P

NT = 64
TD = 2
NF = 5
CR = 16
CT = 512
LT = 4
HB = 2
ROWS = 40
GRP = 8 * ROWS
NODES = 1024
VAR_DEV = 32
EPS4 = 0.0625
F32 = jnp.float32
BF = jnp.bfloat16
SWAP = [(0, 1), (1, 0)]
ALL = ("inst", "span", "rad")


def spectral_blocks():
    index = np.arange(NT)
    diff = index[:, None] - index[None, :]
    safe = np.where(diff == 0, 1, diff)
    table = np.where(diff == 0, 0.0, 0.5 * np.where(diff % 2 == 0, 1.0, -1.0) / np.tan(np.pi * safe / NT))
    order = np.concatenate([index[0::2], index[1::2]])
    apply = table.T[order][:, order].astype(np.float32)
    high = apply.astype(BF)
    low = (apply - high.astype(np.float32)).astype(BF)
    return np.concatenate([high, high, low], axis=1)


def row_of(t, what, f, h):
    return ((t * 2 + what) * NF + f) * HB + h


def lanes(q):
    return slice(128 * q, 128 * q + 128)


def local_operator(cell, edge_ref, halo_ref, pad_ref, jr_ref, jc_ref, dis, has_low, has_high, t, q):
    lane = lax.broadcasted_iota(jnp.int32, (CR, 128), 1)
    d_rad, d_circ, fourth = [], [], []
    for f in range(NF):
        tf = t * NF + f
        mid = cell(f, q)
        edge = edge_ref[tf]
        left = edge if q == 0 else cell(f, q - 1)
        right = edge if q == LT - 1 else cell(f, q + 1)
        m1 = jnp.where(lane < 1, pltpu.roll(left, 1, 1), pltpu.roll(mid, 1, 1))
        m2 = jnp.where(lane < 2, pltpu.roll(left, 2, 1), pltpu.roll(mid, 2, 1))
        p1 = jnp.where(lane >= 127, pltpu.roll(right, 127, 1), pltpu.roll(mid, 127, 1))
        p2 = jnp.where(lane >= 126, pltpu.roll(right, 126, 1), pltpu.roll(mid, 126, 1))
        halo = halo_ref[2 * tf:2 * tf + 2, lanes(q)]
        base = f * 32
        pad_ref[base + 6:base + 8, :] = halo * has_low
        pad_ref[base + 8:base + 24, :] = mid
        pad_ref[base + 24:base + 26, :] = halo * has_high
        rm2 = pad_ref[base + 6:base + 22, :]
        rm1 = pad_ref[base + 7:base + 23, :]
        rp1 = pad_ref[base + 9:base + 25, :]
        rp2 = pad_ref[base + 10:base + 26, :]
        d_circ.append(0.5 * (m1 - p1))
        d_rad.append(0.5 * (rm1 - rp1))
        fourth.append((m2 + p2) + (rm2 + rp2) - 4.0 * ((m1 + p1) + (rm1 + rp1)) + 12.0 * mid)
    out = []
    for j in range(NF):
        acc = (EPS4 * dis) * fourth[j]
        for i in range(NF):
            acc = acc + jr_ref[t, i, j, :, lanes(q)].astype(F32) * d_rad[i]
            acc = acc + jc_ref[t, i, j, :, lanes(q)].astype(F32) * d_circ[i]
        out.append(acc)
    return out


def first_kernel(rad_ref, psi_ref, edge_ref, halo_ref, jr_ref, jc_ref, dis_ref, step_ref, src_ref, x_ref, pad_ref):
    rad = rad_ref[0]
    has_low = (rad == 1).astype(F32)
    has_high = (rad == 0).astype(F32)
    for t in range(TD):
        for q in range(LT):
            cell = lambda f, qq: psi_ref[t * NF + f, :, lanes(qq)]
            res = local_operator(cell, edge_ref, halo_ref, pad_ref, jr_ref, jc_ref, dis_ref[:, lanes(q)], has_low, has_high, t, q)
            sigma = step_ref[:, lanes(q)]
            for f in range(NF):
                mid = cell(f, q)
                w = mid - sigma * (res[f] - src_ref[t * NF + f, :, lanes(q)])
                for h in range(HB):
                    x_ref[pl.ds(q * GRP + row_of(t, 0, f, h), 8, stride=ROWS), :] = mid[8 * h:8 * h + 8]
                    x_ref[pl.ds(q * GRP + row_of(t, 1, f, h), 8, stride=ROWS), :] = w[8 * h:8 * h + 8]


def time_kernel(table_ref, sig_ref, y_ref, v_ref):
    table = table_ref[...]

    def apply(x):
        high = x.astype(BF)
        low = (x - high.astype(F32)).astype(BF)
        return jnp.dot(table, jnp.concatenate([high, low, high], axis=0), preferred_element_type=F32)

    def gather(what):
        cols = []
        for f in range(NF):
            for h in range(HB):
                cols.append(jnp.concatenate(
                    [y_ref[pl.ds(row_of(t, what, f, h), 32, stride=ROWS), :] for t in range(TD)], axis=0))
        return jnp.concatenate(cols, axis=1)

    def scatter(what, value):
        for f in range(NF):
            for h in range(HB):
                for t in range(TD):
                    v_ref[pl.ds(row_of(t, what, f, h), 32, stride=ROWS), :] = value[32 * t:32 * t + 32, lanes(f * HB + h)]

    sigma = jnp.concatenate([sig_ref[0:1, :], sig_ref[1:2, :]] * NF, axis=1)
    time0 = apply(gather(0))
    scatter(0, time0)
    psi1 = gather(1) - sigma * time0
    scatter(1, apply(psi1))


def middle_kernel(rad_ref, x_ref, u_ref, step_ref, src_ref, psi_ref, base_ref, edge_ref, halo_ref):
    rad = rad_ref[0]
    lane = lax.broadcasted_iota(jnp.int32, (CR, 128), 1)
    for t in range(TD):
        for f in range(NF):
            tf = t * NF + f
            tiles = []
            for q in range(LT):
                sigma = step_ref[:, lanes(q)]

                def plane(ref, what):
                    return jnp.concatenate(
                        [ref[pl.ds(q * GRP + row_of(t, what, f, h), 8, stride=ROWS), :] for h in range(HB)], axis=0)

                psi1 = plane(x_ref, 1) - sigma * plane(u_ref, 0)
                base_ref[tf, :, lanes(q)] = psi1 - sigma * (plane(u_ref, 1) - src_ref[tf, :, lanes(q)])
                psi_ref[tf, :, lanes(q)] = psi1
                tiles.append(psi1)
                halo_ref[2 * tf:2 * tf + 2, lanes(q)] = jnp.where(rad == 0, psi1[14:16], psi1[0:2])
            edge_ref[tf] = jnp.where(lane < 64, tiles[0], tiles[3])


def last_kernel(rad_ref, psi_ref, base_ref, edge_ref, halo_ref, jr_ref, jc_ref, dis_ref, step_ref, cell_ref, owner_ref,
                local_ref, sd_ref, out_ref, sens_ref, pad_ref):
    rad = rad_ref[0]
    has_low = (rad == 1).astype(F32)
    has_high = (rad == 0).astype(F32)
    for t in range(TD):
        for q in range(LT):
            cell = lambda f, qq: psi_ref[t * NF + f, :, lanes(qq)]
            res = local_operator(cell, edge_ref, halo_ref, pad_ref, jr_ref, jc_ref, dis_ref[:, lanes(q)], has_low, has_high, t, q)
            sigma = step_ref[:, lanes(q)]
            for f in range(NF):
                out_ref[t * NF + f, :, lanes(q)] = base_ref[t * NF + f, :, lanes(q)] - sigma * res[f]
    cells = cell_ref[...]
    row, col = cells // CT, cells % CT
    pick = (lax.broadcasted_iota(jnp.int32, (CT, NODES), 0) == col).astype(F32).astype(BF)
    mask = (lax.broadcasted_iota(jnp.int32, (CR, NODES), 0) == row).astype(F32)
    acc = [jnp.zeros((CR, NODES), F32) for _ in range(3)]
    for t in range(TD):
        plane = out_ref[t * NF:(t + 1) * NF].reshape(NF * CR, CT)
        high = plane.astype(BF)
        low = (plane - high.astype(F32)).astype(BF)
        both = jnp.dot(jnp.concatenate([high, low], axis=0), pick, preferred_element_type=F32)
        value = both[:NF * CR] + both[NF * CR:]
        for f in range(NF):
            here = value[f * CR:(f + 1) * CR]
            for k in range(3):
                weight = sd_ref[t * NF + f, k:k + 1, :].astype(F32)
                acc[k] = acc[k] + here * weight
    owner = owner_ref[...]
    parts = []
    for k in range(3):
        kept = acc[k] * mask
        for s in range(2):
            parts.append(kept * (owner == s).astype(F32))
    stack = jnp.concatenate(parts, axis=0)
    high = stack.astype(BF)
    low = (stack - high.astype(F32)).astype(BF)
    label = (lax.broadcasted_iota(jnp.int32, (128, NODES), 0) % VAR_DEV == local_ref[...]).astype(F32).astype(BF)
    dims = (((1,), (1,)), ((), ()))
    total = lax.dot_general(high, label, dims, preferred_element_type=F32) + lax.dot_general(
        low, label, dims, preferred_element_type=F32)
    lane = lax.broadcasted_iota(jnp.int32, (1, 128), 1)
    line = []
    for s in range(2):
        full = jnp.zeros((1, 128), F32)
        for k in range(3):
            at = (k * 2 + s) * CR
            part = jnp.sum(total[at:at + CR], axis=0, keepdims=True)
            full = jnp.where(lane // VAR_DEV == k, part, full)
        line.append(full)
    peer = lax.broadcasted_iota(jnp.int32, (128, 128), 0)
    sens_ref[...] = jnp.where((peer // 2) % 2 == 0, line[0], line[1])


def call(kernel, outs, n_in, smem_first, scratch=()):
    specs = [pl.BlockSpec(memory_space=pltpu.VMEM)] * n_in
    if smem_first:
        specs = [pl.BlockSpec(memory_space=pltpu.SMEM)] + specs
    single = not isinstance(outs, (list, tuple))
    shapes = [outs] if single else list(outs)
    out_specs = [pl.BlockSpec(memory_space=pltpu.VMEM)] * len(shapes)
    return pl.pallas_call(
        kernel,
        out_shape=outs if single else shapes,
        in_specs=specs,
        out_specs=out_specs[0] if single else out_specs,
        scratch_shapes=list(scratch),
        compiler_params=pltpu.CompilerParams(vmem_limit_bytes=40 * 1024 * 1024),
    )


def f32(*shape):
    return jax.ShapeDtypeStruct(shape, F32)


def body(adjoint_start, jac_rad, jac_circ, dissip, pseudo_step, source, node_cell, node_owner, node_local, shape_deriv):
    me = lax.axis_index("inst")
    rad = lax.axis_index("rad")
    rad_s = rad.astype(jnp.int32).reshape(1)
    n = TD * NF
    psi0 = adjoint_start.reshape(n, CR, CT)
    src = source.reshape(n, CR, CT)
    lane = lax.broadcasted_iota(jnp.int32, (1, 1, 128), 2)
    edge = jnp.where(lane < 64, psi0[:, :, :128], psi0[:, :, 384:])
    halo = jnp.where(rad == 0, psi0[:, 14:16], psi0[:, 0:2]).reshape(2 * n, CT)
    edge = lax.ppermute(edge, "span", SWAP)
    halo = lax.ppermute(halo, "rad", SWAP)
    pad = pltpu.VMEM((NF * 32, 128), F32)
    x = call(first_kernel, f32(32 * ROWS, 128), 8, True, (pad,))(
        rad_s, psi0, edge, halo, jac_rad, jac_circ, dissip, pseudo_step, src)
    y = lax.all_to_all(x, "inst", 0, 0, tiled=True)
    sig = lax.dynamic_slice(pseudo_step.reshape(2, 8, LT, 128), (0, me % 8, me // 8, 0), (2, 1, 1, 128)).reshape(2, 128)
    v = call(time_kernel, f32(32 * ROWS, 128), 3, False)(jnp.asarray(spectral_blocks()), sig, y)
    u = lax.all_to_all(v, "inst", 0, 0, tiled=True)
    psi1, base, edge, halo = call(
        middle_kernel, (f32(n, CR, CT), f32(n, CR, CT), f32(n, CR, 128), f32(2 * n, CT)), 4, True)(
        rad_s, x, u, pseudo_step, src)
    edge = lax.ppermute(edge, "span", SWAP)
    halo = lax.ppermute(halo, "rad", SWAP)
    psi2, parts = call(last_kernel, (f32(n, CR, CT), f32(128, 128)), 12, True, (pad,))(
        rad_s, psi1, base, edge, halo, jac_rad, jac_circ, dissip, pseudo_step, node_cell.reshape(1, NODES),
        node_owner.reshape(1, NODES), node_local.reshape(1, NODES), shape_deriv.reshape(n, 3, NODES))
    got = lax.all_to_all(parts, ALL, 0, 0, tiled=True)
    sens = jnp.sum(got, axis=0)[:3 * VAR_DEV].reshape(3, VAR_DEV)
    return psi2.reshape(TD, NF, CR, CT), sens


def solution(mesh):
    in_specs = (
        P("inst", None, "rad", "span"),
        P("inst", None, None, "rad", "span"),
        P("inst", None, None, "rad", "span"),
        P("rad", "span"),
        P("rad", "span"),
        P("inst", None, "rad", "span"),
        P(("span", "rad")),
        P(("span", "rad"), None),
        P(("span", "rad")),
        P("inst", None, None, ("span", "rad")),
    )
    out_specs = (P("inst", None, "rad", "span"), P(None, "span"))
    return jax.shard_map(body, mesh=mesh, in_specs=in_specs, out_specs=out_specs, check_vma=False)
```

```python
import jax
import jax.numpy as jnp
import numpy as np
from jax import lax
from jax.experimental import pallas as pl
from jax.experimental.pallas import tpu as pltpu
from jax.sharding import PartitionSpec as P

NT = 64
TD = 2
NF = 5
CR = 16
CT = 512
LT = 4
HB = 2
ROWS = 40
GRP = 8 * ROWS
NODES = 1024
VAR_DEV = 32
EPS4 = 0.0625
F32 = jnp.float32
BF = jnp.bfloat16
SWAP = [(0, 1), (1, 0)]
ALL = ("inst", "span", "rad")


def spectral_blocks():
    index = np.arange(NT)
    diff = index[:, None] - index[None, :]
    safe = np.where(diff == 0, 1, diff)
    table = np.where(diff == 0, 0.0, 0.5 * np.where(diff % 2 == 0, 1.0, -1.0) / np.tan(np.pi * safe / NT))
    order = np.concatenate([index[0::2], index[1::2]])
    apply = table.T[order][:, order].astype(np.float32)
    high = apply.astype(BF)
    low = (apply - high.astype(np.float32)).astype(BF)
    return np.concatenate([high, high, low], axis=1)


def row_of(t, what, f, h):
    return ((t * 2 + what) * NF + f) * HB + h


def lanes(q):
    return slice(128 * q, 128 * q + 128)


def interior(cell, pad_ref, jr, jc, dis, q):
    lane = lax.broadcasted_iota(jnp.int32, (CR, 128), 1)
    none = jnp.zeros((CR, 128), F32)
    d_rad, d_circ, fourth = [], [], []
    for f in range(NF):
        mid = cell(f, q)
        left = none if q == 0 else cell(f, q - 1)
        right = none if q == LT - 1 else cell(f, q + 1)
        m1 = jnp.where(lane < 1, pltpu.roll(left, 1, 1), pltpu.roll(mid, 1, 1))
        m2 = jnp.where(lane < 2, pltpu.roll(left, 2, 1), pltpu.roll(mid, 2, 1))
        p1 = jnp.where(lane >= 127, pltpu.roll(right, 127, 1), pltpu.roll(mid, 127, 1))
        p2 = jnp.where(lane >= 126, pltpu.roll(right, 126, 1), pltpu.roll(mid, 126, 1))
        base = f * 32
        pad_ref[base + 8:base + 24, :] = mid
        rm2 = pad_ref[base + 6:base + 22, :]
        rm1 = pad_ref[base + 7:base + 23, :]
        rp1 = pad_ref[base + 9:base + 25, :]
        rp2 = pad_ref[base + 10:base + 26, :]
        d_circ.append(0.5 * (m1 - p1))
        d_rad.append(0.5 * (rm1 - rp1))
        fourth.append((m2 + p2) + (rm2 + rp2) - 4.0 * ((m1 + p1) + (rm1 + rp1)) + 12.0 * mid)
    out = []
    for j in range(NF):
        acc = (EPS4 * dis) * fourth[j]
        for i in range(NF):
            acc = acc + jr(i, j).astype(F32) * d_rad[i]
            acc = acc + jc(i, j).astype(F32) * d_circ[i]
        out.append(acc)
    return out


def clear_pad(pad_ref):
    pad_ref[...] = jnp.zeros(pad_ref.shape, F32)


def corrections(rad, edge_ref, halo_ref, jrb_ref, jce_ref, dis_ref, t):
    lane = lax.broadcasted_iota(jnp.int32, (CR, 128), 1)
    diff, fourth = [], []
    edge = edge_ref[t]
    for f in range(NF):
        turn = lambda by: pltpu.roll(edge, (by - 4 * f) % 128, 1)
        m1 = jnp.where(lane < 1, turn(1), 0.0)
        m2 = jnp.where(lane < 2, turn(2), 0.0)
        p1 = jnp.where(lane >= 127, turn(-1), 0.0)
        p2 = jnp.where(lane >= 126, turn(-2), 0.0)
        diff.append(0.5 * (m1 - p1))
        fourth.append(m2 + p2 - 4.0 * (m1 + p1))
    dis_edge = EPS4 * jnp.where(lane < 64, dis_ref[:, lanes(0)], dis_ref[:, lanes(LT - 1)])
    circ = []
    for j in range(NF):
        acc = dis_edge * fourth[j]
        for i in range(NF):
            acc = acc + jce_ref[t * NF + i, j].astype(F32) * diff[i]
        circ.append(acc)
    near_row = jnp.where(rad == 0, CR - 1, 0)
    next_row = jnp.where(rad == 0, CR - 2, 1)
    sign = jnp.where(rad == 0, -0.5, 0.5)
    first, second = [halo_ref[(2 * t + m) * NF:(2 * t + m + 1) * NF, :] for m in range(2)]
    near = jnp.where(rad == 0, first, second)
    far = jnp.where(rad == 0, second, first)
    dis_near = EPS4 * dis_ref[pl.ds(near_row, 1), :]
    dis_next = EPS4 * dis_ref[pl.ds(next_row, 1), :]
    row_a = dis_near * (far - 4.0 * near)
    for i in range(NF):
        row_a = row_a + jrb_ref[t * NF + i] * (sign * near[i:i + 1])
    row_b = dis_next * near
    riota = lax.broadcasted_iota(jnp.int32, (CR, 128), 0)

    def fix(f, q):
        out = jnp.where(riota == near_row, row_a[f:f + 1, lanes(q)], 0.0)
        out = jnp.where(riota == next_row, row_b[f:f + 1, lanes(q)], out)
        if q == 0:
            out = out + jnp.where(lane < 64, circ[f], 0.0)
        if q == LT - 1:
            out = out + jnp.where(lane >= 64, circ[f], 0.0)
        return out

    return fix


def edge_kernel(rad_ref, psi_hbm, edge_ref, halo_ref, rows_ref, left_ref, right_ref, sem):
    rad = rad_ref[0]
    start = pl.multiple_of(8 * (1 - rad), 8)
    copies = [
        pltpu.make_async_copy(psi_hbm.at[:, pl.ds(start, 8), :], rows_ref, sem.at[0]),
        pltpu.make_async_copy(psi_hbm.at[:, :, pl.ds(0, 128)], left_ref, sem.at[1]),
        pltpu.make_async_copy(psi_hbm.at[:, :, pl.ds(CT - 128, 128)], right_ref, sem.at[2]),
    ]
    for copy in copies:
        copy.start()
    copies[0].wait()
    put_halo(halo_ref, lambda tf: rows_ref[tf], rad)
    copies[1].wait()
    copies[2].wait()
    put_edge(edge_ref, lambda tf: (left_ref[tf], right_ref[tf]))


def put_edge(edge_ref, ends):
    lane = lax.broadcasted_iota(jnp.int32, (CR, 128), 1)
    for t in range(TD):
        packed = None
        for f in range(NF):
            left, right = ends(t * NF + f)
            both = jnp.where(lane < 64, left, right)
            if f == 0:
                packed = both
            else:
                packed = jnp.where((lane >= 4 * f - 2) & (lane < 4 * f + 2), pltpu.roll(both, 4 * f, 1), packed)
        edge_ref[t] = packed


def put_halo(halo_ref, tile, rad):
    for t in range(TD):
        for f in range(NF):
            rows = tile(t * NF + f)
            pair = jnp.where(rad == 0, rows[6:8], rows[0:2])
            for m in range(2):
                at = (2 * t + m) * NF + f
                halo_ref[at:at + 1] = pair[m:m + 1]


def first_kernel(rad_ref, me_ref, dis_hbm, step_hbm, cell_hbm, owner_hbm, local_hbm, psi_hbm, src_hbm, jr_hbm, jc_hbm,
                 part_ref, psi_ref, jrb_ref, jce_ref, dis_ref, step_ref, sig_ref, ids_ref,
                 src_ref, jr_ref, jc_ref, pad_ref, cell_ref, owner_ref, local_ref, sem, sem_small):
    rad = rad_ref[0]
    small = [pltpu.make_async_copy(a, b, sem_small.at[i]) for i, (a, b) in enumerate([
        (dis_hbm, dis_ref), (step_hbm, step_ref), (cell_hbm, cell_ref), (owner_hbm, owner_ref), (local_hbm, local_ref)])]
    copies = []
    for t in range(TD):
        tf = pl.ds(t * NF, NF)
        copies.append([
            pltpu.make_async_copy(psi_hbm.at[tf], psi_ref.at[tf], sem.at[t, 0]),
            pltpu.make_async_copy(jr_hbm.at[t], jr_ref.at[t], sem.at[t, 1]),
            pltpu.make_async_copy(jc_hbm.at[t], jc_ref.at[t], sem.at[t, 2]),
            pltpu.make_async_copy(src_hbm.at[tf], src_ref.at[tf], sem.at[t, 3]),
        ])
    for copy in small + copies[0] + copies[1]:
        copy.start()
    clear_pad(pad_ref)
    lane = lax.broadcasted_iota(jnp.int32, (CR, 128), 1)
    for copy in small:
        copy.wait()
    ids_ref[0:1] = cell_ref[...] % CT
    ids_ref[1:2] = cell_ref[...] // CT
    ids_ref[2:3] = owner_ref[...]
    ids_ref[3:4] = local_ref[...]
    me = me_ref[0]
    sig = jnp.zeros((2, 128), F32)
    for p in range(8):
        for q in range(LT):
            here = jnp.concatenate([step_ref[p:p + 1, lanes(q)], step_ref[p + 8:p + 9, lanes(q)]], axis=0)
            sig = jnp.where(me == 8 * q + p, here, sig)
    sig_ref[...] = sig
    for t in range(TD):
        for copy in copies[t]:
            copy.wait()
        for q in range(LT):
            cell = lambda f, qq: psi_ref[t * NF + f, :, lanes(qq)]
            jr = lambda i, j: jr_ref[t, i, j, :, lanes(q)]
            jc = lambda i, j: jc_ref[t, i, j, :, lanes(q)]
            res = interior(cell, pad_ref, jr, jc, dis_ref[:, lanes(q)], q)
            sigma = step_ref[:, lanes(q)]
            for f in range(NF):
                part_ref[t * NF + f, :, lanes(q)] = cell(f, q) - sigma * (res[f] - src_ref[t * NF + f, :, lanes(q)])
        for i in range(NF):
            for j in range(NF):
                whole = jr_ref[t, i, j].astype(F32)
                jrb_ref[t * NF + i, j:j + 1] = jnp.where(rad == 0, whole[CR - 1:CR], whole[0:1])
                jce_ref[t * NF + i, j] = jnp.where(
                    lane < 64, jc_ref[t, i, j, :, lanes(0)].astype(F32), jc_ref[t, i, j, :, lanes(LT - 1)].astype(F32)).astype(BF)


def send_kernel(rad_ref, psi_ref, part_ref, edge_ref, halo_ref, jrb_ref, jce_ref, dis_ref, step_ref, x_ref, w_ref):
    rad = rad_ref[0]
    for t in range(TD):
        fix = corrections(rad, edge_ref, halo_ref, jrb_ref, jce_ref, dis_ref, t)
        for f in range(NF):
            for q in range(LT):
                mid = psi_ref[t * NF + f, :, lanes(q)]
                w = part_ref[t * NF + f, :, lanes(q)] - step_ref[:, lanes(q)] * fix(f, q)
                w_ref[t * NF + f, :, lanes(q)] = w
                for h in range(HB):
                    x_ref[pl.ds(q * GRP + row_of(t, 0, f, h), 8, stride=ROWS), :] = mid[8 * h:8 * h + 8]
                    x_ref[pl.ds(q * GRP + row_of(t, 1, f, h), 8, stride=ROWS), :] = w[8 * h:8 * h + 8]


def time_kernel(table_ref, sig_ref, y_ref, v_ref):
    table = table_ref[...]

    def apply(x):
        high = x.astype(BF)
        low = (x - high.astype(F32)).astype(BF)
        return jnp.dot(table, jnp.concatenate([high, low, high], axis=0), preferred_element_type=F32)

    def gather(what):
        cols = []
        for f in range(NF):
            for h in range(HB):
                cols.append(jnp.concatenate(
                    [y_ref[pl.ds(row_of(t, what, f, h), 32, stride=ROWS), :] for t in range(TD)], axis=0))
        return jnp.concatenate(cols, axis=1)

    def scatter(what, value):
        for f in range(NF):
            for h in range(HB):
                for t in range(TD):
                    v_ref[pl.ds(row_of(t, what, f, h), 32, stride=ROWS), :] = value[32 * t:32 * t + 32, lanes(f * HB + h)]

    sigma = jnp.concatenate([sig_ref[0:1, :], sig_ref[1:2, :]] * NF, axis=1)
    time0 = apply(gather(0))
    scatter(0, time0)
    psi1 = gather(1) - sigma * time0
    scatter(1, apply(psi1))


def plane(ref, what, t, f, q):
    return jnp.concatenate([ref[pl.ds(q * GRP + row_of(t, what, f, h), 8, stride=ROWS), :] for h in range(HB)], axis=0)


def rim_kernel(rad_ref, w_ref, u_ref, step_ref, edge_ref, halo_ref):
    rad = rad_ref[0]

    def ends(tf):
        return [w_ref[tf, :, lanes(q)] - step_ref[:, lanes(q)] * plane(u_ref, 0, tf // NF, tf % NF, q) for q in (0, LT - 1)]

    put_edge(edge_ref, ends)
    start = pl.multiple_of(8 * (1 - rad), 8)

    def rows(tf):
        t, f = tf // NF, tf % NF
        time = jnp.concatenate(
            [u_ref[pl.ds(q * GRP + row_of(t, 0, f, 0) + (1 - rad), 8, stride=ROWS), :] for q in range(LT)], axis=1)
        return w_ref[tf, pl.ds(start, 8), :] - step_ref[pl.ds(start, 8), :] * time

    put_halo(halo_ref, rows, rad)


def middle_kernel(w_ref, u_ref, jr_ref, jc_ref, dis_ref, step_ref, src_ref, ids_ref, base_ref, pick_ref, psi_ref, pad_ref):
    clear_pad(pad_ref)
    for t in range(TD):
        for f in range(NF):
            for q in range(LT):
                psi_ref[t * NF + f, :, lanes(q)] = (
                    w_ref[t * NF + f, :, lanes(q)] - step_ref[:, lanes(q)] * plane(u_ref, 0, t, f, q))
        for q in range(LT):
            cell = lambda f, qq: psi_ref[t * NF + f, :, lanes(qq)]
            jr = lambda i, j: jr_ref[t, i, j, :, lanes(q)]
            jc = lambda i, j: jc_ref[t, i, j, :, lanes(q)]
            res = interior(cell, pad_ref, jr, jc, dis_ref[:, lanes(q)], q)
            sigma = step_ref[:, lanes(q)]
            for f in range(NF):
                base_ref[t * NF + f, :, lanes(q)] = cell(f, q) - sigma * (
                    res[f] + plane(u_ref, 1, t, f, q) - src_ref[t * NF + f, :, lanes(q)])
    col = ids_ref[0:1]
    pick_ref[...] = (lax.broadcasted_iota(jnp.int32, (CT, NODES), 0) == col).astype(F32).astype(BF)


def last_kernel(rad_ref, base_ref, edge_ref, halo_ref, jrb_ref, jce_ref, dis_ref, step_ref, pick_ref, ids_ref, sd_ref,
                 out_hbm, sens_ref, psi_ref, sem):
    rad = rad_ref[0]
    row = ids_ref[1:2]
    pick = pick_ref[...]
    mask = (lax.broadcasted_iota(jnp.int32, (CR, NODES), 0) == row).astype(F32)
    acc = [jnp.zeros((CR, NODES), F32) for _ in range(3)]
    copies = []
    for t in range(TD):
        fix = corrections(rad, edge_ref, halo_ref, jrb_ref, jce_ref, dis_ref, t)
        for f in range(NF):
            for q in range(LT):
                psi_ref[t * NF + f, :, lanes(q)] = base_ref[t * NF + f, :, lanes(q)] - step_ref[:, lanes(q)] * fix(f, q)
        tf = pl.ds(t * NF, NF)
        copies.append(pltpu.make_async_copy(psi_ref.at[tf], out_hbm.at[tf], sem.at[t]))
        copies[t].start()
    for t in range(TD):
        whole = psi_ref[t * NF:(t + 1) * NF].reshape(NF * CR, CT)
        high = whole.astype(BF)
        low = (whole - high.astype(F32)).astype(BF)
        both = jnp.dot(jnp.concatenate([high, low], axis=0), pick, preferred_element_type=F32)
        value = both[:NF * CR] + both[NF * CR:]
        for f in range(NF):
            here = value[f * CR:(f + 1) * CR]
            for k in range(3):
                weight = sd_ref[t * NF + f, k:k + 1, :].astype(F32)
                acc[k] = acc[k] + here * weight
    owner = ids_ref[2:3]
    parts = []
    for k in range(3):
        kept = acc[k] * mask
        for s in range(2):
            parts.append(kept * (owner == s).astype(F32))
    stack = jnp.concatenate(parts, axis=0)
    high = stack.astype(BF)
    low = (stack - high.astype(F32)).astype(BF)
    label = (lax.broadcasted_iota(jnp.int32, (128, NODES), 0) % VAR_DEV == ids_ref[3:4]).astype(F32).astype(BF)
    dims = (((1,), (1,)), ((), ()))
    total = lax.dot_general(high, label, dims, preferred_element_type=F32) + lax.dot_general(
        low, label, dims, preferred_element_type=F32)
    lane = lax.broadcasted_iota(jnp.int32, (1, 128), 1)
    line = []
    for s in range(2):
        full = jnp.zeros((1, 128), F32)
        for k in range(3):
            at = (k * 2 + s) * CR
            part = jnp.sum(total[at:at + CR], axis=0, keepdims=True)
            full = jnp.where(lane // VAR_DEV == k, part, full)
        line.append(full)
    peer = lax.broadcasted_iota(jnp.int32, (128, 128), 0)
    sens_ref[...] = jnp.where((peer // 2) % 2 == 0, line[0], line[1])
    for copy in copies:
        copy.wait()


VM, SM, HM = pltpu.VMEM, pltpu.SMEM, pltpu.HBM


def call(kernel, ins, outs, scratch=(), micros=1):
    return pl.pallas_call(
        kernel,
        out_shape=[shape for shape, _ in outs],
        in_specs=[pl.BlockSpec(memory_space=space) for space in ins],
        out_specs=[pl.BlockSpec(memory_space=space) for _, space in outs],
        scratch_shapes=list(scratch),
        cost_estimate=pl.CostEstimate(flops=0, bytes_accessed=int(micros * 3.0e6), transcendentals=0),
        compiler_params=pltpu.CompilerParams(vmem_limit_bytes=24 * 1024 * 1024),
    )


def f32(*shape):
    return jax.ShapeDtypeStruct(shape, F32)


def swap_halos(edge, halo):
    halo = lax.ppermute(halo, "rad", SWAP)
    edge = lax.ppermute(edge, "span", SWAP)
    return edge, halo


def body(adjoint_start, jac_rad, jac_circ, dissip, pseudo_step, source, node_cell, node_owner, node_local, shape_deriv):
    me = lax.axis_index("inst").astype(jnp.int32).reshape(1)
    rad = lax.axis_index("rad").astype(jnp.int32).reshape(1)
    n = TD * NF
    psi0 = adjoint_start.reshape(n, CR, CT)
    src = source.reshape(n, CR, CT)
    full = f32(n, CR, CT)
    line = (1, NODES)
    flat = f32(CR, CT)
    edges = [(f32(TD, CR, 128), VM), (f32(2 * n, CT), VM)]
    dma = pltpu.SemaphoreType.DMA
    pad = VM((NF * 32, 128), F32)
    held = [pltpu.with_memory_space_constraint(a, pltpu.HBM) for a in (
        dissip, pseudo_step, node_cell.reshape(line), node_owner.reshape(line), node_local.reshape(line), psi0, src, jac_rad, jac_circ)]
    edge, halo = call(edge_kernel, [SM, HM], edges,
                      [VM((n, 8, CT), F32), VM((n, CR, 128), F32), VM((n, CR, 128), F32), dma((3,))])(rad, held[5])
    edge, halo = swap_halos(edge, halo)
    part, psi, jrb, jce, dis, step, sig, ids = call(
        first_kernel, [SM, SM] + [HM] * 9,
        [(full, VM), (full, VM), (f32(n, NF, CT), VM), (jax.ShapeDtypeStruct((n, NF, CR, 128), BF), VM), (flat, VM), (flat, VM),
         (f32(2, 128), VM), (jax.ShapeDtypeStruct((8, NODES), jnp.int32), VM)],
        [VM((n, CR, CT), F32), VM(jac_rad.shape, BF), VM(jac_circ.shape, BF), pad] + [VM(line, jnp.int32)] * 3 + [dma((TD, 4)), dma((5,))],
        micros=3)(rad, me, *held)
    x, w = call(send_kernel, [SM] + [VM] * 8, [(f32(32 * ROWS, 128), VM), (full, VM)])(
        rad, psi, part, edge, halo, jrb, jce, dis, step)
    y = lax.all_to_all(x, "inst", 0, 0, tiled=True)
    v, = call(time_kernel, [VM] * 3, [(f32(32 * ROWS, 128), VM)])(jnp.asarray(spectral_blocks()), sig, y)
    u = lax.all_to_all(v, "inst", 0, 0, tiled=True)
    edge, halo = call(rim_kernel, [SM] + [VM] * 3, edges)(rad, w, u, step)
    edge, halo = swap_halos(edge, halo)
    base, pick = call(
        middle_kernel, [VM] * 8, [(full, VM), (jax.ShapeDtypeStruct((CT, NODES), BF), VM)], [VM((n, CR, CT), F32), pad],
        micros=3)(w, u, jac_rad, jac_circ, dis, step, src, ids)
    psi2, parts = call(last_kernel, [SM] + [VM] * 10, [(full, HM), (f32(128, 128), VM)], [VM((n, CR, CT), F32), dma((TD,))])(
        rad, base, edge, halo, jrb, jce, dis, step, pick, ids, shape_deriv.reshape(n, 3, NODES))
    got = lax.all_to_all(parts, ALL, 0, 0, tiled=True)
    sens = jnp.sum(got, axis=0)[:3 * VAR_DEV].reshape(3, VAR_DEV)
    return psi2.reshape(TD, NF, CR, CT), sens


def solution(mesh):
    in_specs = (
        P("inst", None, "rad", "span"),
        P("inst", None, None, "rad", "span"),
        P("inst", None, None, "rad", "span"),
        P("rad", "span"),
        P("rad", "span"),
        P("inst", None, "rad", "span"),
        P(("span", "rad")),
        P(("span", "rad"), None),
        P(("span", "rad")),
        P("inst", None, None, ("span", "rad")),
    )
    out_specs = (P("inst", None, "rad", "span"), P(None, "span"))
    return jax.shard_map(body, mesh=mesh, in_specs=in_specs, out_specs=out_specs, check_vma=False)
```

```python
import jax
import jax.numpy as jnp
import numpy as np
from jax import lax
from jax.experimental import pallas as pl
from jax.experimental.pallas import tpu as pltpu
from jax.sharding import PartitionSpec as P

NT = 64
TD = 2
NF = 5
CR = 16
CT = 512
LT = 4
HB = 2
BODY = 40
ROWS = 44
GRP = 8 * ROWS
NODES = 1024
VAR_DEV = 32
EPS4 = 0.0625
F32 = jnp.float32
BF = jnp.bfloat16
SWAP = [(0, 1), (1, 0)]
ALL = ("inst", "span", "rad")


def spectral_blocks():
    index = np.arange(NT)
    diff = index[:, None] - index[None, :]
    safe = np.where(diff == 0, 1, diff)
    table = np.where(diff == 0, 0.0, 0.5 * np.where(diff % 2 == 0, 1.0, -1.0) / np.tan(np.pi * safe / NT))
    order = np.concatenate([index[0::2], index[1::2]])
    apply = table.T[order][:, order].astype(np.float32)
    high = apply.astype(BF)
    low = (apply - high.astype(np.float32)).astype(BF)
    return np.concatenate([high, high, low], axis=1)


def row_of(t, what, f, h):
    return ((t * 2 + what) * NF + f) * HB + h


def lanes(q):
    return slice(128 * q, 128 * q + 128)


def interior(cell, pad_ref, jr, jc, dis, q):
    lane = lax.broadcasted_iota(jnp.int32, (CR, 128), 1)
    none = jnp.zeros((CR, 128), F32)
    d_rad, d_circ, fourth = [], [], []
    for f in range(NF):
        mid = cell(f, q)
        left = none if q == 0 else cell(f, q - 1)
        right = none if q == LT - 1 else cell(f, q + 1)
        m1 = jnp.where(lane < 1, pltpu.roll(left, 1, 1), pltpu.roll(mid, 1, 1))
        m2 = jnp.where(lane < 2, pltpu.roll(left, 2, 1), pltpu.roll(mid, 2, 1))
        p1 = jnp.where(lane >= 127, pltpu.roll(right, 127, 1), pltpu.roll(mid, 127, 1))
        p2 = jnp.where(lane >= 126, pltpu.roll(right, 126, 1), pltpu.roll(mid, 126, 1))
        base = f * 32
        pad_ref[base + 8:base + 24, :] = mid
        rm2 = pad_ref[base + 6:base + 22, :]
        rm1 = pad_ref[base + 7:base + 23, :]
        rp1 = pad_ref[base + 9:base + 25, :]
        rp2 = pad_ref[base + 10:base + 26, :]
        d_circ.append(0.5 * (m1 - p1))
        d_rad.append(0.5 * (rm1 - rp1))
        fourth.append((m2 + p2) + (rm2 + rp2) - 4.0 * ((m1 + p1) + (rm1 + rp1)) + 12.0 * mid)
    out = []
    for j in range(NF):
        acc = (EPS4 * dis) * fourth[j]
        for i in range(NF):
            acc = acc + jr(i, j).astype(F32) * d_rad[i]
            acc = acc + jc(i, j).astype(F32) * d_circ[i]
        out.append(acc)
    return out


def clear_pad(pad_ref):
    pad_ref[...] = jnp.zeros(pad_ref.shape, F32)


def corrections(rad, edge_ref, halo_ref, jrb_ref, jce_ref, dis_ref, t):
    lane = lax.broadcasted_iota(jnp.int32, (CR, 128), 1)
    diff, fourth = [], []
    edge = edge_ref[t]
    for f in range(NF):
        turn = lambda by: pltpu.roll(edge, (by - 4 * f) % 128, 1)
        m1 = jnp.where(lane < 1, turn(1), 0.0)
        m2 = jnp.where(lane < 2, turn(2), 0.0)
        p1 = jnp.where(lane >= 127, turn(-1), 0.0)
        p2 = jnp.where(lane >= 126, turn(-2), 0.0)
        diff.append(0.5 * (m1 - p1))
        fourth.append(m2 + p2 - 4.0 * (m1 + p1))
    dis_edge = EPS4 * jnp.where(lane < 64, dis_ref[:, lanes(0)], dis_ref[:, lanes(LT - 1)])
    circ = []
    for j in range(NF):
        acc = dis_edge * fourth[j]
        for i in range(NF):
            acc = acc + jce_ref[t * NF + i, j].astype(F32) * diff[i]
        circ.append(acc)
    near_row = jnp.where(rad == 0, CR - 1, 0)
    next_row = jnp.where(rad == 0, CR - 2, 1)
    sign = jnp.where(rad == 0, -0.5, 0.5)
    first, second = [halo_ref[(2 * t + m) * NF:(2 * t + m + 1) * NF, :] for m in range(2)]
    near = jnp.where(rad == 0, first, second)
    far = jnp.where(rad == 0, second, first)
    dis_near = EPS4 * dis_ref[pl.ds(near_row, 1), :]
    dis_next = EPS4 * dis_ref[pl.ds(next_row, 1), :]
    row_a = dis_near * (far - 4.0 * near)
    for i in range(NF):
        row_a = row_a + jrb_ref[t * NF + i] * (sign * near[i:i + 1])
    row_b = dis_next * near
    riota = lax.broadcasted_iota(jnp.int32, (CR, 128), 0)

    def fix(f, q):
        out = jnp.where(riota == near_row, row_a[f:f + 1, lanes(q)], 0.0)
        out = jnp.where(riota == next_row, row_b[f:f + 1, lanes(q)], out)
        if q == 0:
            out = out + jnp.where(lane < 64, circ[f], 0.0)
        if q == LT - 1:
            out = out + jnp.where(lane >= 64, circ[f], 0.0)
        return out

    return fix


def edge_kernel(rad_ref, psi_hbm, step_hbm, edge_ref, halo_ref, rows_ref, left_ref, right_ref, step_ref, sem):
    rad = rad_ref[0]
    start = pl.multiple_of(8 * (1 - rad), 8)
    copies = [
        pltpu.make_async_copy(psi_hbm.at[:, pl.ds(start, 8), :], rows_ref, sem.at[0]),
        pltpu.make_async_copy(psi_hbm.at[:, :, pl.ds(0, 128)], left_ref, sem.at[1]),
        pltpu.make_async_copy(psi_hbm.at[:, :, pl.ds(CT - 128, 128)], right_ref, sem.at[2]),
        pltpu.make_async_copy(step_hbm, step_ref, sem.at[3]),
    ]
    for copy in copies:
        copy.start()
    copies[0].wait()
    copies[3].wait()
    put_halo(halo_ref, lambda tf: rows_ref[tf], rad)
    halo_ref[20:22] = jnp.where(rad == 0, step_ref[CR - 2:CR], step_ref[0:2])
    halo_ref[22:24] = jnp.zeros((2, CT), F32)
    copies[1].wait()
    copies[2].wait()
    put_edge(edge_ref, lambda tf: (left_ref[tf], right_ref[tf]))
    ends = (step_ref[:, lanes(0)], step_ref[:, lanes(LT - 1)])
    edge_ref[TD] = pack_edge([ends] * NF)


def pack_edge(ends):
    lane = lax.broadcasted_iota(jnp.int32, (CR, 128), 1)
    packed = None
    for f in range(NF):
        both = jnp.where(lane < 64, ends[f][0], ends[f][1])
        if f == 0:
            packed = both
        else:
            packed = jnp.where((lane >= 4 * f - 2) & (lane < 4 * f + 2), pltpu.roll(both, 4 * f, 1), packed)
    return packed


def put_edge(edge_ref, ends):
    for t in range(TD):
        edge_ref[t] = pack_edge([ends(t * NF + f) for f in range(NF)])


def put_halo(halo_ref, tile, rad):
    for t in range(TD):
        for f in range(NF):
            rows = tile(t * NF + f)
            pair = jnp.where(rad == 0, rows[6:8], rows[0:2])
            for m in range(2):
                at = (2 * t + m) * NF + f
                halo_ref[at:at + 1] = pair[m:m + 1]


def first_kernel(rad_ref, me_ref, dis_hbm, step_hbm, cell_hbm, owner_hbm, local_hbm, psi_hbm, src_hbm, jr_hbm, jc_hbm,
                 part_ref, psi_ref, jrb_ref, jce_ref, dis_ref, step_ref, sig_ref, ids_ref,
                 src_ref, jr_ref, jc_ref, pad_ref, cell_ref, owner_ref, local_ref, sem, sem_small):
    rad = rad_ref[0]
    small = [pltpu.make_async_copy(a, b, sem_small.at[i]) for i, (a, b) in enumerate([
        (dis_hbm, dis_ref), (step_hbm, step_ref), (cell_hbm, cell_ref), (owner_hbm, owner_ref), (local_hbm, local_ref)])]
    copies = []
    for t in range(TD):
        tf = pl.ds(t * NF, NF)
        copies.append([
            pltpu.make_async_copy(psi_hbm.at[tf], psi_ref.at[tf], sem.at[t, 0]),
            pltpu.make_async_copy(jr_hbm.at[t], jr_ref.at[t], sem.at[t, 1]),
            pltpu.make_async_copy(jc_hbm.at[t], jc_ref.at[t], sem.at[t, 2]),
            pltpu.make_async_copy(src_hbm.at[tf], src_ref.at[tf], sem.at[t, 3]),
        ])
    for copy in small + copies[0] + copies[1]:
        copy.start()
    clear_pad(pad_ref)
    lane = lax.broadcasted_iota(jnp.int32, (CR, 128), 1)
    for copy in small:
        copy.wait()
    ids_ref[0:1] = cell_ref[...] % CT
    ids_ref[1:2] = cell_ref[...] // CT
    ids_ref[2:3] = owner_ref[...]
    ids_ref[3:4] = local_ref[...]
    me = me_ref[0]
    sig = jnp.zeros((2, 128), F32)
    for p in range(8):
        for q in range(LT):
            here = jnp.concatenate([step_ref[p:p + 1, lanes(q)], step_ref[p + 8:p + 9, lanes(q)]], axis=0)
            sig = jnp.where(me == 8 * q + p, here, sig)
    sig_ref[...] = sig
    for t in range(TD):
        for copy in copies[t]:
            copy.wait()
        for q in range(LT):
            cell = lambda f, qq: psi_ref[t * NF + f, :, lanes(qq)]
            jr = lambda i, j: jr_ref[t, i, j, :, lanes(q)]
            jc = lambda i, j: jc_ref[t, i, j, :, lanes(q)]
            res = interior(cell, pad_ref, jr, jc, dis_ref[:, lanes(q)], q)
            sigma = step_ref[:, lanes(q)]
            for f in range(NF):
                part_ref[t * NF + f, :, lanes(q)] = cell(f, q) - sigma * (res[f] - src_ref[t * NF + f, :, lanes(q)])
        for i in range(NF):
            for j in range(NF):
                whole = jr_ref[t, i, j].astype(F32)
                jrb_ref[t * NF + i, j:j + 1] = jnp.where(rad == 0, whole[CR - 1:CR], whole[0:1])
                jce_ref[t * NF + i, j] = jnp.where(
                    lane < 64, jc_ref[t, i, j, :, lanes(0)].astype(F32), jc_ref[t, i, j, :, lanes(LT - 1)].astype(F32)).astype(BF)


def send_kernel(rad_ref, psi_ref, part_ref, edge_ref, halo_ref, jrb_ref, jce_ref, dis_ref, step_ref, x_hbm, w_ref, w_edge_ref,
                w_halo_ref, rim_ref, x_ref, sem):
    rad = rad_ref[0]
    fixes = [corrections(rad, edge_ref, halo_ref, jrb_ref, jce_ref, dis_ref, t) for t in range(TD)]
    for t in range(TD):
        for q in range(LT):
            rim_ref[10 * q:10 * q + 10] = halo_ref[10 * t:10 * t + 10, lanes(q)]
        rim_ref[40:56] = edge_ref[t]
        rim_ref[56:64] = jnp.zeros((8, 128), F32)
        for e in range(2):
            x_ref[pl.ds(BODY + 2 * t + e, 32, stride=ROWS), :] = rim_ref[pl.ds(e, 32, stride=2), :]
    copies = []
    for q in range(LT):
        for t in range(TD):
            for f in range(NF):
                mid = psi_ref[t * NF + f, :, lanes(q)]
                w = part_ref[t * NF + f, :, lanes(q)] - step_ref[:, lanes(q)] * fixes[t](f, q)
                w_ref[t * NF + f, :, lanes(q)] = w
                for h in range(HB):
                    x_ref[pl.ds(q * GRP + row_of(t, 0, f, h), 8, stride=ROWS), :] = mid[8 * h:8 * h + 8]
                    x_ref[pl.ds(q * GRP + row_of(t, 1, f, h), 8, stride=ROWS), :] = w[8 * h:8 * h + 8]
        span = pl.ds(q * GRP, GRP)
        copies.append(pltpu.make_async_copy(x_ref.at[span], x_hbm.at[span], sem.at[q]))
        copies[q].start()
    put_edge(w_edge_ref, lambda tf: (w_ref[tf, :, lanes(0)], w_ref[tf, :, lanes(LT - 1)]))
    start = pl.multiple_of(8 * (1 - rad), 8)
    put_halo(w_halo_ref, lambda tf: w_ref[tf, pl.ds(start, 8), :], rad)
    for copy in copies:
        copy.wait()


def label_kernel(ids_ref, pick_ref, label_ref):
    pick_ref[...] = (lax.broadcasted_iota(jnp.int32, (CT, NODES), 0) == ids_ref[0:1]).astype(F32).astype(BF)
    label_ref[...] = (lax.broadcasted_iota(jnp.int32, (128, NODES), 0) % VAR_DEV == ids_ref[3:4]).astype(F32).astype(BF)


def total_kernel(got_ref, sens_ref):
    line = jnp.sum(got_ref[...], axis=0, keepdims=True)
    for k in range(3):
        sens_ref[k:k + 1, :] = pltpu.roll(line, (128 - VAR_DEV * k) % 128, 1)[:, :VAR_DEV]


def time_kernel(table_ref, sig_ref, y_ref, edge_ref, halo_ref, pick_ref, label_ref, v_ref, edge_out_ref, halo_out_ref):
    edge_out_ref[...] = edge_ref[...]
    halo_out_ref[...] = halo_ref[...]
    table = table_ref[...]

    def apply(x):
        high = x.astype(BF)
        low = (x - high.astype(F32)).astype(BF)
        return jnp.dot(table, jnp.concatenate([high, low, high], axis=0), preferred_element_type=F32)

    def row(what, m, t):
        if m < 2 * NF:
            return (t * 2 + what) * 2 * NF + m
        return BODY + 2 * t + m - 2 * NF

    def gather(what, count):
        return jnp.concatenate([jnp.concatenate(
            [y_ref[pl.ds(row(what, m, t), 32, stride=ROWS), :] for t in range(TD)], axis=0) for m in range(count)], axis=1)

    def scatter(what, value, count):
        for m in range(count):
            for t in range(TD):
                v_ref[pl.ds(row(what, m, t), 32, stride=ROWS), :] = value[32 * t:32 * t + 32, lanes(m)]

    count = 2 * NF
    sigma = jnp.concatenate([sig_ref[0:1, :], sig_ref[1:2, :]] * NF, axis=1)
    time0 = apply(gather(0, count + 2))
    scatter(0, time0, count + 2)
    psi1 = gather(1, count) - sigma * time0[:, :128 * count]
    scatter(1, apply(psi1), count)


def plane(ref, what, t, f, q):
    return jnp.concatenate([ref[pl.ds(q * GRP + row_of(t, what, f, h), 8, stride=ROWS), :] for h in range(HB)], axis=0)


def last_kernel(rad_ref, w_ref, u_ref, w_edge_ref, w_halo_ref, edge0_ref, halo0_ref, jr_ref, jc_ref, jrb_ref, jce_ref, dis_ref,
                step_ref, src_ref, ids_ref, pick_ref, label_ref, sd_ref, out_hbm, sens_ref, psi1_ref, psi_ref, edge_ref, halo_ref, rim_ref, pad_ref, sem):
    rad = rad_ref[0]
    clear_pad(pad_ref)
    for t in range(TD):
        for e in range(2):
            rim_ref[pl.ds(e, 32, stride=2), :] = u_ref[pl.ds(BODY + 2 * t + e, 32, stride=ROWS), :]
        for m in range(2):
            at = (2 * t + m) * NF
            for q in range(LT):
                halo_ref[at:at + NF, lanes(q)] = (
                    w_halo_ref[at:at + NF, lanes(q)]
                    - halo0_ref[20 + m:21 + m, lanes(q)] * rim_ref[10 * q + NF * m:10 * q + NF * m + NF])
        edge_ref[t] = w_edge_ref[t] - edge0_ref[TD] * rim_ref[40:56]
    copies = []
    for t in range(TD):
        fix = corrections(rad, edge_ref, halo_ref, jrb_ref, jce_ref, dis_ref, t)
        for f in range(NF):
            for q in range(LT):
                psi1_ref[t * NF + f, :, lanes(q)] = (
                    w_ref[t * NF + f, :, lanes(q)] - step_ref[:, lanes(q)] * plane(u_ref, 0, t, f, q))
        for q in range(LT):
            cell = lambda f, qq: psi1_ref[t * NF + f, :, lanes(qq)]
            jr = lambda i, j: jr_ref[t, i, j, :, lanes(q)]
            jc = lambda i, j: jc_ref[t, i, j, :, lanes(q)]
            res = interior(cell, pad_ref, jr, jc, dis_ref[:, lanes(q)], q)
            sigma = step_ref[:, lanes(q)]
            for f in range(NF):
                psi_ref[t * NF + f, :, lanes(q)] = cell(f, q) - sigma * (
                    res[f] + fix(f, q) + plane(u_ref, 1, t, f, q) - src_ref[t * NF + f, :, lanes(q)])
        tf = pl.ds(t * NF, NF)
        copies.append(pltpu.make_async_copy(psi_ref.at[tf], out_hbm.at[tf], sem.at[t]))
        copies[t].start()
    pick = pick_ref[...]
    mask = (lax.broadcasted_iota(jnp.int32, (CR, NODES), 0) == ids_ref[1:2]).astype(F32)
    acc = [jnp.zeros((CR, NODES), F32) for _ in range(3)]
    weights = [sd_ref[m].astype(F32) for m in range(3 * NF)]
    for t in range(TD):
        whole = psi_ref[t * NF:(t + 1) * NF].reshape(NF * CR, CT)
        high = whole.astype(BF)
        low = (whole - high.astype(F32)).astype(BF)
        both = jnp.dot(jnp.concatenate([high, low], axis=0), pick, preferred_element_type=F32)
        value = both[:NF * CR] + both[NF * CR:]
        for f in range(NF):
            here = value[f * CR:(f + 1) * CR]
            for k in range(3):
                acc[k] = acc[k] + here * weights[3 * f + k][t:t + 1]
    owner = ids_ref[2:3]
    parts = []
    for k in range(3):
        kept = acc[k] * mask
        for s in range(2):
            parts.append(kept * (owner == s).astype(F32))
    stack = jnp.concatenate(parts, axis=0)
    high = stack.astype(BF)
    low = (stack - high.astype(F32)).astype(BF)
    label = label_ref[...]
    dims = (((1,), (1,)), ((), ()))
    total = lax.dot_general(high, label, dims, preferred_element_type=F32) + lax.dot_general(
        low, label, dims, preferred_element_type=F32)
    lane = lax.broadcasted_iota(jnp.int32, (1, 128), 1)
    line = []
    for s in range(2):
        full = jnp.zeros((1, 128), F32)
        for k in range(3):
            at = (k * 2 + s) * CR
            part = jnp.sum(total[at:at + CR], axis=0, keepdims=True)
            full = jnp.where(lane // VAR_DEV == k, part, full)
        line.append(full)
    peer = lax.broadcasted_iota(jnp.int32, (128, 128), 0)
    sens_ref[...] = jnp.where((peer // 2) % 2 == 0, line[0], line[1])
    for copy in copies:
        copy.wait()


VM, SM, HM = pltpu.VMEM, pltpu.SMEM, pltpu.HBM


def call(kernel, ins, outs, scratch=(), micros=1):
    return pl.pallas_call(
        kernel,
        out_shape=[shape for shape, _ in outs],
        in_specs=[pl.BlockSpec(memory_space=space) for space in ins],
        out_specs=[pl.BlockSpec(memory_space=space) for _, space in outs],
        scratch_shapes=list(scratch),
        cost_estimate=pl.CostEstimate(flops=0, bytes_accessed=int(micros * 3.0e6), transcendentals=0),
        compiler_params=pltpu.CompilerParams(vmem_limit_bytes=24 * 1024 * 1024),
    )


def f32(*shape):
    return jax.ShapeDtypeStruct(shape, F32)


def swap_halos(edge, halo):
    halo = lax.ppermute(halo, "rad", SWAP)
    edge = lax.ppermute(edge, "span", SWAP)
    return edge, halo


def body(adjoint_start, jac_rad, jac_circ, dissip, pseudo_step, source, node_cell, node_owner, node_local, shape_deriv):
    me = lax.axis_index("inst").astype(jnp.int32).reshape(1)
    rad = lax.axis_index("rad").astype(jnp.int32).reshape(1)
    n = TD * NF
    psi0 = adjoint_start.reshape(n, CR, CT)
    src = source.reshape(n, CR, CT)
    full = f32(n, CR, CT)
    line = (1, NODES)
    flat = f32(CR, CT)
    dma = pltpu.SemaphoreType.DMA
    pad = VM((NF * 32, 128), F32)
    held = [pltpu.with_memory_space_constraint(a, pltpu.HBM) for a in (
        dissip, pseudo_step, node_cell.reshape(line), node_owner.reshape(line), node_local.reshape(line), psi0, src, jac_rad, jac_circ)]
    edge0, halo0 = call(
        edge_kernel, [SM, HM, HM], [(f32(TD + 1, CR, 128), VM), (f32(24, CT), VM)],
        [VM((n, 8, CT), F32), VM((n, CR, 128), F32), VM((n, CR, 128), F32), VM((CR, CT), F32), dma((4,))])(rad, held[5], held[1])
    edge0, halo0 = swap_halos(edge0, halo0)
    part, psi, jrb, jce, dis, step, sig, ids = call(
        first_kernel, [SM, SM] + [HM] * 9,
        [(full, VM), (full, VM), (f32(n, NF, CT), VM), (jax.ShapeDtypeStruct((n, NF, CR, 128), BF), VM), (flat, VM), (flat, VM),
         (f32(2, 128), VM), (jax.ShapeDtypeStruct((8, NODES), jnp.int32), VM)],
        [VM((n, CR, CT), F32), VM(jac_rad.shape, BF), VM(jac_circ.shape, BF), pad] + [VM(line, jnp.int32)] * 3 + [dma((TD, 4)), dma((5,))],
        micros=3)(rad, me, *held)
    rim = VM((64, 128), F32)
    x, w, w_edge, w_halo = call(
        send_kernel, [SM] + [VM] * 8, [(f32(32 * ROWS, 128), HM), (full, VM), (f32(TD, CR, 128), VM), (f32(2 * n, CT), VM)],
        [rim, VM((32 * ROWS, 128), F32), dma((LT,))])(
        rad, psi, part, edge0, halo0, jrb, jce, dis, step)
    w_edge, w_halo = swap_halos(w_edge, w_halo)
    y = lax.all_to_all(x.reshape(32 * ROWS, 1, 128), "inst", 0, 0, tiled=True).reshape(32 * ROWS, 128)
    bf16 = lambda *shape: (jax.ShapeDtypeStruct(shape, BF), VM)
    pick, label = call(label_kernel, [VM], [bf16(CT, NODES), bf16(128, NODES)])(ids)
    v, w_edge, w_halo = call(
        time_kernel, [VM] * 5 + [pl.ANY] * 2, [(f32(32 * ROWS, 128), VM), (f32(TD, CR, 128), VM), (f32(2 * n, CT), VM)])(
        jnp.asarray(spectral_blocks()), sig, y, w_edge, w_halo, pick, label)
    u = lax.all_to_all(v.reshape(32 * ROWS, 1, 128), "inst", 0, 0, tiled=True).reshape(32 * ROWS, 128)
    psi2, parts = call(
        last_kernel, [SM] + [VM] * 17, [(full, HM), (f32(128, 128), VM)],
        [VM((n, CR, CT), F32), VM((n, CR, CT), F32), VM((TD, CR, 128), F32), VM((2 * n, CT), F32), rim, pad, dma((TD,))])(
        rad, w, u, w_edge, w_halo, edge0, halo0, jac_rad, jac_circ, jrb, jce, dis, step, src, ids, pick, label,
        shape_deriv.transpose(1, 2, 0, 3).reshape(3 * NF, TD, NODES))
    got = lax.all_to_all(parts, ALL, 0, 0, tiled=True)
    sens, = call(total_kernel, [VM], [(f32(3, VAR_DEV), VM)])(got)
    return psi2.reshape(TD, NF, CR, CT), sens


def solution(mesh):
    in_specs = (
        P("inst", None, "rad", "span"),
        P("inst", None, None, "rad", "span"),
        P("inst", None, None, "rad", "span"),
        P("rad", "span"),
        P("rad", "span"),
        P("inst", None, "rad", "span"),
        P(("span", "rad")),
        P(("span", "rad"), None),
        P(("span", "rad")),
        P("inst", None, None, ("span", "rad")),
    )
    out_specs = (P("inst", None, "rad", "span"), P(None, "span"))
    return jax.shard_map(body, mesh=mesh, in_specs=in_specs, out_specs=out_specs, check_vma=False)
```

```python
import jax
import jax.numpy as jnp
import numpy as np
from jax import lax
from jax.experimental import pallas as pl
from jax.experimental.pallas import tpu as pltpu
from jax.sharding import PartitionSpec as P

NT = 64
TD = 2
NF = 5
CR = 16
CT = 512
LT = 4
HB = 2
BODY = 40
RIM = 3
ROWS = BODY + RIM
HALF = 256
GRP = 8 * ROWS
NODES = 1024
VAR_DEV = 32
EPS4 = 0.0625
F32 = jnp.float32
BF = jnp.bfloat16
SWAP = [(0, 1), (1, 0)]
ALL = ("inst", "span", "rad")


def spectral_blocks():
    index = np.arange(NT)
    diff = index[:, None] - index[None, :]
    safe = np.where(diff == 0, 1, diff)
    table = np.where(diff == 0, 0.0, 0.5 * np.where(diff % 2 == 0, 1.0, -1.0) / np.tan(np.pi * safe / NT))
    order = np.concatenate([index[0::2], index[1::2]])
    apply = table.T[order][:, order].astype(np.float32)
    high = apply.astype(BF)
    low = (apply - high.astype(np.float32)).astype(BF)
    return np.concatenate([high, high, low], axis=1)


def row_of(t, what, f, h):
    return ((t * 2 + what) * NF + f) * HB + h


def lanes(q):
    return slice(128 * q, 128 * q + 128)


def interior(cell, pad_ref, jr, jc, dis, q):
    lane = lax.broadcasted_iota(jnp.int32, (CR, 128), 1)
    none = jnp.zeros((CR, 128), F32)
    d_rad, d_circ, fourth = [], [], []
    for f in range(NF):
        mid = cell(f, q)
        left = none if q == 0 else cell(f, q - 1)
        right = none if q == LT - 1 else cell(f, q + 1)
        m1 = jnp.where(lane < 1, pltpu.roll(left, 1, 1), pltpu.roll(mid, 1, 1))
        m2 = jnp.where(lane < 2, pltpu.roll(left, 2, 1), pltpu.roll(mid, 2, 1))
        p1 = jnp.where(lane >= 127, pltpu.roll(right, 127, 1), pltpu.roll(mid, 127, 1))
        p2 = jnp.where(lane >= 126, pltpu.roll(right, 126, 1), pltpu.roll(mid, 126, 1))
        base = f * 32
        pad_ref[base + 8:base + 24, :] = mid
        rm2 = pad_ref[base + 6:base + 22, :]
        rm1 = pad_ref[base + 7:base + 23, :]
        rp1 = pad_ref[base + 9:base + 25, :]
        rp2 = pad_ref[base + 10:base + 26, :]
        d_circ.append(0.5 * (m1 - p1))
        d_rad.append(0.5 * (rm1 - rp1))
        fourth.append((m2 + p2) + (rm2 + rp2) - 4.0 * ((m1 + p1) + (rm1 + rp1)) + 12.0 * mid)
    out = []
    for j in range(NF):
        acc = (EPS4 * dis) * fourth[j]
        for i in range(NF):
            acc = acc + jr(i, j).astype(F32) * d_rad[i]
            acc = acc + jc(i, j).astype(F32) * d_circ[i]
        out.append(acc)
    return out


def clear_pad(pad_ref):
    pad_ref[...] = jnp.zeros(pad_ref.shape, F32)


def halo_rows(ref, at, count):
    return jnp.concatenate([ref[at:at + count, :], ref[20 + at:20 + at + count, :]], axis=1)


def corrections(rad, edge_ref, halo_ref, jrb_ref, jce_ref, dis_ref, t):
    lane = lax.broadcasted_iota(jnp.int32, (CR, 128), 1)
    diff, fourth = [], []
    edge = edge_ref[t]
    for f in range(NF):
        turn = lambda by: pltpu.roll(edge, (by - 4 * f) % 128, 1)
        m1 = jnp.where(lane < 1, turn(1), 0.0)
        m2 = jnp.where(lane < 2, turn(2), 0.0)
        p1 = jnp.where(lane >= 127, turn(-1), 0.0)
        p2 = jnp.where(lane >= 126, turn(-2), 0.0)
        diff.append(0.5 * (m1 - p1))
        fourth.append(m2 + p2 - 4.0 * (m1 + p1))
    dis_edge = EPS4 * jnp.where(lane < 64, dis_ref[:, lanes(0)], dis_ref[:, lanes(LT - 1)])
    circ = []
    for j in range(NF):
        acc = dis_edge * fourth[j]
        for i in range(NF):
            acc = acc + jce_ref[t * NF + i, j].astype(F32) * diff[i]
        circ.append(acc)
    near_row = jnp.where(rad == 0, CR - 1, 0)
    next_row = jnp.where(rad == 0, CR - 2, 1)
    sign = jnp.where(rad == 0, -0.5, 0.5)
    first, second = [halo_rows(halo_ref, (2 * t + m) * NF, NF) for m in range(2)]
    near = jnp.where(rad == 0, first, second)
    far = jnp.where(rad == 0, second, first)
    dis_near = EPS4 * dis_ref[pl.ds(near_row, 1), :]
    dis_next = EPS4 * dis_ref[pl.ds(next_row, 1), :]
    row_a = dis_near * (far - 4.0 * near)
    for i in range(NF):
        row_a = row_a + jrb_ref[t * NF + i] * (sign * near[i:i + 1])
    row_b = dis_next * near
    riota = lax.broadcasted_iota(jnp.int32, (CR, 128), 0)

    def fix(f, q):
        out = jnp.where(riota == near_row, row_a[f:f + 1, lanes(q)], 0.0)
        out = jnp.where(riota == next_row, row_b[f:f + 1, lanes(q)], out)
        if q == 0:
            out = out + jnp.where(lane < 64, circ[f], 0.0)
        if q == LT - 1:
            out = out + jnp.where(lane >= 64, circ[f], 0.0)
        return out

    return fix


def interior_pass(t, psi_ref, src_ref, jr_ref, jc_ref, dis_ref, step_ref, pad_ref, part_ref):
    for q in range(LT):
        cell = lambda f, qq: psi_ref[t * NF + f, :, lanes(qq)]
        jr = lambda i, j: jr_ref[t, i, j, :, lanes(q)]
        jc = lambda i, j: jc_ref[t, i, j, :, lanes(q)]
        res = interior(cell, pad_ref, jr, jc, dis_ref[:, lanes(q)], q)
        sigma = step_ref[:, lanes(q)]
        for f in range(NF):
            part_ref[t * NF + f, :, lanes(q)] = cell(f, q) - sigma * (res[f] - src_ref[t * NF + f, :, lanes(q)])


def edge_kernel(rad_ref, psi_hbm, edge_ref, halo_ref, rows_ref, left_ref, right_ref, sem):
    rad = rad_ref[0]
    start = pl.multiple_of(8 * (1 - rad), 8)
    copies = [
        pltpu.make_async_copy(psi_hbm.at[:, pl.ds(start, 8), :], rows_ref, sem.at[0]),
        pltpu.make_async_copy(psi_hbm.at[:, :, pl.ds(0, 128)], left_ref, sem.at[1]),
        pltpu.make_async_copy(psi_hbm.at[:, :, pl.ds(CT - 128, 128)], right_ref, sem.at[2]),
    ]
    for copy in copies:
        copy.start()
    copies[0].wait()
    put_halo(halo_ref, lambda tf: rows_ref[tf], rad)
    copies[1].wait()
    copies[2].wait()
    put_edge(edge_ref, lambda tf: (left_ref[tf], right_ref[tf]))


def pack_edge(ends):
    lane = lax.broadcasted_iota(jnp.int32, (CR, 128), 1)
    packed = None
    for f in range(NF):
        both = jnp.where(lane < 64, ends[f][0], ends[f][1])
        if f == 0:
            packed = both
        else:
            packed = jnp.where((lane >= 4 * f - 2) & (lane < 4 * f + 2), pltpu.roll(both, 4 * f, 1), packed)
    return packed


def put_edge(edge_ref, ends):
    for t in range(TD):
        edge_ref[t] = pack_edge([ends(t * NF + f) for f in range(NF)])


def put_halo(halo_ref, tile, rad):
    for t in range(TD):
        for f in range(NF):
            rows = tile(t * NF + f)
            pair = jnp.where(rad == 0, rows[6:8], rows[0:2])
            for m in range(2):
                put_row(halo_ref, (2 * t + m) * NF + f, pair[m:m + 1])


def put_row(halo_ref, at, row):
    halo_ref[at:at + 1] = row[:, :HALF]
    halo_ref[20 + at:21 + at] = row[:, HALF:]


def rim_of(tile, edge):
    lane = lax.broadcasted_iota(jnp.int32, (3, 128), 1)
    turned = pltpu.roll(edge, 2, 1)
    turned = jnp.concatenate([turned, jnp.zeros((8, 128), F32)], axis=0)
    dense = jnp.zeros((3, 128), F32)
    for g in range(6):
        part = turned[3 * g:3 * g + 3]
        part = pltpu.roll(part, 20 * g, 1) if g else part
        dense = jnp.where((lane >= 20 * g) & (lane < 20 * g + 20), part, dense)
    return jnp.concatenate([tile(q) for q in range(LT)] + [dense, jnp.zeros((5, 128), F32)], axis=0)


def edge_of(dense, edge_ref):
    for g in range(6):
        edge_ref[3 * g:3 * g + 3] = pltpu.roll(dense, 128 - 20 * g, 1) if g else dense
    return pltpu.roll(edge_ref[0:CR], 126, 1)


def halves(a, b):
    lane = lax.broadcasted_iota(jnp.int32, a.shape, 1)
    return jnp.where(lane < 64, a, pltpu.roll(b, 64, 1)), jnp.where(lane < 64, pltpu.roll(a, 64, 1), b)


def first_kernel(rad_ref, span_ref, me_ref, dis_hbm, step_hbm, cell_hbm, owner_hbm, local_hbm, psi_hbm, src_hbm, jr_hbm, jc_hbm,
                 part_ref, psi_ref, jrb_ref, jce_ref, dis_ref, step_ref, sig_ref, ids_ref,
                 src_ref, jr_ref, jc_ref, pad_ref, cell_ref, owner_ref, local_ref, sem, sem_small):
    rad = rad_ref[0]
    small = [pltpu.make_async_copy(a, b, sem_small.at[i]) for i, (a, b) in enumerate([
        (dis_hbm, dis_ref), (step_hbm, step_ref), (cell_hbm, cell_ref), (owner_hbm, owner_ref), (local_hbm, local_ref)])]
    copies = []
    for t in range(TD):
        tf = pl.ds(t * NF, NF)
        copies.append([
            pltpu.make_async_copy(psi_hbm.at[tf], psi_ref.at[tf], sem.at[t, 0]),
            pltpu.make_async_copy(jr_hbm.at[t], jr_ref.at[t], sem.at[t, 1]),
            pltpu.make_async_copy(jc_hbm.at[t], jc_ref.at[t], sem.at[t, 2]),
            pltpu.make_async_copy(src_hbm.at[tf], src_ref.at[tf], sem.at[t, 3]),
        ])
    for copy in small + copies[0] + copies[1]:
        copy.start()
    clear_pad(pad_ref)
    lane = lax.broadcasted_iota(jnp.int32, (CR, 128), 1)
    for copy in small:
        copy.wait()
    ids_ref[0:1] = cell_ref[...] % CT
    ids_ref[1:2] = cell_ref[...] // CT
    ids_ref[2:3] = owner_ref[...]
    ids_ref[3:4] = local_ref[...]
    me = me_ref[0]
    sig = jnp.zeros((2, 128), F32)
    for p in range(8):
        for q in range(LT):
            here = jnp.concatenate([step_ref[p:p + 1, lanes(q)], step_ref[p + 8:p + 9, lanes(q)]], axis=0)
            sig = jnp.where(me == 8 * q + p, here, sig)
    sig_ref[...] = sig
    for t in range(TD):
        for copy in copies[t]:
            copy.wait()

        @pl.when((span_ref[0] == 1) | (t == 0))
        def _():
            interior_pass(t, psi_ref, src_ref, jr_ref, jc_ref, dis_ref, step_ref, pad_ref, part_ref)

        for i in range(NF):
            for j in range(NF):
                whole = jr_ref[t, i, j].astype(F32)
                jrb_ref[t * NF + i, j:j + 1] = jnp.where(rad == 0, whole[CR - 1:CR], whole[0:1])
                jce_ref[t * NF + i, j] = jnp.where(
                    lane < 64, jc_ref[t, i, j, :, lanes(0)].astype(F32), jc_ref[t, i, j, :, lanes(LT - 1)].astype(F32)).astype(BF)


def send_kernel(rad_ref, span_ref, psi_ref, part_ref, edge_ref, halo_ref, jrb_ref, jce_ref, dis_ref, step_ref, src_hbm, jr_hbm, jc_hbm,
                x_hbm, w_ref, w_edge_ref, w_halo_ref, rim_ref, x_ref, src_ref, jr_ref, jc_ref, pad_ref, late_ref, sem, sem_in):
    rad = rad_ref[0]

    late_ref[...] = part_ref[...]

    @pl.when(span_ref[0] == 0)
    def _():
        last = pl.ds((TD - 1) * NF, NF)
        loads = [pltpu.make_async_copy(a, b, sem_in.at[i]) for i, (a, b) in enumerate(
            [(src_hbm.at[last], src_ref.at[last]), (jr_hbm.at[TD - 1], jr_ref.at[TD - 1]), (jc_hbm.at[TD - 1], jc_ref.at[TD - 1])])]
        for load in loads:
            load.start()
        clear_pad(pad_ref)
        for load in loads:
            load.wait()
        interior_pass(TD - 1, psi_ref, src_ref, jr_ref, jc_ref, dis_ref, step_ref, pad_ref, late_ref)

    fixes = [corrections(rad, edge_ref, halo_ref, jrb_ref, jce_ref, dis_ref, t) for t in range(TD)]
    rims = [rim_of(lambda q: halo_ref[20 * (q // 2) + 10 * t:20 * (q // 2) + 10 * t + 10, lanes(q % 2)], edge_ref[t])
            for t in range(TD)]
    low, high = halves(*rims)
    rim_ref[0:48] = low
    rim_ref[48:96] = high
    for e in range(RIM):
        x_ref[pl.ds(BODY + e, 32, stride=ROWS), :] = rim_ref[32 * e:32 * e + 32]
    copies = []
    for q in range(LT):
        for t in range(TD):
            for f in range(NF):
                mid = psi_ref[t * NF + f, :, lanes(q)]
                w = late_ref[t * NF + f, :, lanes(q)] - step_ref[:, lanes(q)] * fixes[t](f, q)
                w_ref[t * NF + f, :, lanes(q)] = w
                for h in range(HB):
                    x_ref[pl.ds(q * GRP + row_of(t, 0, f, h), 8, stride=ROWS), :] = mid[8 * h:8 * h + 8]
                    x_ref[pl.ds(q * GRP + row_of(t, 1, f, h), 8, stride=ROWS), :] = w[8 * h:8 * h + 8]
        span = pl.ds(q * GRP, GRP)
        copies.append(pltpu.make_async_copy(x_ref.at[span], x_hbm.at[span], sem.at[q]))
        copies[q].start()
    put_edge(w_edge_ref, lambda tf: (w_ref[tf, :, lanes(0)], w_ref[tf, :, lanes(LT - 1)]))
    start = pl.multiple_of(8 * (1 - rad), 8)
    put_halo(w_halo_ref, lambda tf: w_ref[tf, pl.ds(start, 8), :], rad)
    w_edge_ref[TD] = pack_edge([(step_ref[:, lanes(0)], step_ref[:, lanes(LT - 1)])] * NF)
    sigma = jnp.where(rad == 0, step_ref[CR - 2:CR], step_ref[0:2])
    w_halo_ref[40:42] = sigma[:, :HALF]
    w_halo_ref[42:44] = sigma[:, HALF:]
    w_halo_ref[44:48] = jnp.zeros((4, HALF), F32)
    for copy in copies:
        copy.wait()


def label_kernel(ids_ref, pick_ref, label_ref):
    pick_ref[...] = (lax.broadcasted_iota(jnp.int32, (CT, NODES), 0) == ids_ref[0:1]).astype(F32).astype(BF)
    label_ref[...] = (lax.broadcasted_iota(jnp.int32, (128, NODES), 0) % VAR_DEV == ids_ref[3:4]).astype(F32).astype(BF)


def total_kernel(got_ref, sens_ref):
    line = jnp.sum(got_ref[...], axis=0, keepdims=True)
    for k in range(3):
        sens_ref[k:k + 1, :] = pltpu.roll(line, (128 - VAR_DEV * k) % 128, 1)[:, :VAR_DEV]


def time_kernel(table_ref, sig_ref, y_ref, edge_ref, halo_ref, pick_ref, label_ref, v_ref, edge_out_ref, halo_out_ref):
    edge_out_ref[...] = edge_ref[...]
    halo_out_ref[...] = halo_ref[...]
    table = table_ref[...]

    def apply(x):
        high = x.astype(BF)
        low = (x - high.astype(F32)).astype(BF)
        return jnp.dot(table, jnp.concatenate([high, low, high], axis=0), preferred_element_type=F32)

    count = 2 * NF

    def pick(at):
        return y_ref[pl.ds(at, 32, stride=ROWS), :]

    def put(at, value):
        v_ref[pl.ds(at, 32, stride=ROWS), :] = value

    def row(what, m, t):
        return (t * 2 + what) * count + m

    def gather(what):
        return [jnp.concatenate([pick(row(what, m, t)) for t in range(TD)], axis=0) for m in range(count)]

    def scatter(what, value):
        for m in range(count):
            for t in range(TD):
                put(row(what, m, t), value[32 * t:32 * t + 32, lanes(m)])

    rims = [pick(BODY + e) for e in range(RIM)]
    rims = [jnp.concatenate(halves(rims[0], rims[1]), axis=0), jnp.concatenate([rims[2], pltpu.roll(rims[2], 64, 1)], axis=0)]
    sigma = jnp.concatenate([sig_ref[0:1, :], sig_ref[1:2, :]] * NF, axis=1)
    time0 = apply(jnp.concatenate(gather(0) + rims, axis=1))
    scatter(0, time0)
    pair, single = [time0[:, lanes(count + m)] for m in range(2)]
    for e, value in enumerate(halves(pair[:32], pair[32:]) + halves(single[:32], single[32:])[:1]):
        put(BODY + e, value)
    psi1 = jnp.concatenate(gather(1), axis=1) - sigma * time0[:, :128 * count]
    scatter(1, apply(psi1))


def plane(ref, what, t, f, q):
    return jnp.concatenate([ref[pl.ds(q * GRP + row_of(t, what, f, h), 8, stride=ROWS), :] for h in range(HB)], axis=0)


def last_kernel(rad_ref, w_ref, u_ref, w_edge_ref, w_halo_ref, jr_ref, jc_ref, jrb_ref, jce_ref, dis_ref,
                step_ref, src_ref, ids_ref, pick_ref, label_ref, sd_ref, out_hbm, sens_ref, psi1_ref, psi_ref, edge_ref, halo_ref, rim_ref, turn_ref, pad_ref, sem):
    rad = rad_ref[0]
    clear_pad(pad_ref)
    for e in range(RIM):
        rim_ref[32 * e:32 * e + 32] = u_ref[pl.ds(BODY + e, 32, stride=ROWS), :]
    rims = halves(rim_ref[0:48], rim_ref[48:96])
    for t in range(TD):
        for m in range(2):
            at = (2 * t + m) * NF
            for q in range(LT):
                side = q // 2
                here = slice(20 * side + at, 20 * side + at + NF)
                sigma = w_halo_ref[40 + 2 * side + m:41 + 2 * side + m, lanes(q % 2)]
                halo_ref[here, lanes(q % 2)] = (
                    w_halo_ref[here, lanes(q % 2)] - sigma * rims[t][10 * q + NF * m:10 * q + NF * m + NF])
        edge_ref[t] = w_edge_ref[t] - w_edge_ref[TD] * edge_of(rims[t][40:43], turn_ref)
    copies = []
    for t in range(TD):
        fix = corrections(rad, edge_ref, halo_ref, jrb_ref, jce_ref, dis_ref, t)
        for f in range(NF):
            for q in range(LT):
                psi1_ref[t * NF + f, :, lanes(q)] = (
                    w_ref[t * NF + f, :, lanes(q)] - step_ref[:, lanes(q)] * plane(u_ref, 0, t, f, q))
        for q in range(LT):
            cell = lambda f, qq: psi1_ref[t * NF + f, :, lanes(qq)]
            jr = lambda i, j: jr_ref[t, i, j, :, lanes(q)]
            jc = lambda i, j: jc_ref[t, i, j, :, lanes(q)]
            res = interior(cell, pad_ref, jr, jc, dis_ref[:, lanes(q)], q)
            sigma = step_ref[:, lanes(q)]
            for f in range(NF):
                psi_ref[t * NF + f, :, lanes(q)] = cell(f, q) - sigma * (
                    res[f] + fix(f, q) + plane(u_ref, 1, t, f, q) - src_ref[t * NF + f, :, lanes(q)])
        tf = pl.ds(t * NF, NF)
        copies.append(pltpu.make_async_copy(psi_ref.at[tf], out_hbm.at[tf], sem.at[t]))
        copies[t].start()
    pick = pick_ref[...]
    mask = (lax.broadcasted_iota(jnp.int32, (CR, NODES), 0) == ids_ref[1:2]).astype(F32)
    acc = [jnp.zeros((CR, NODES), F32) for _ in range(3)]
    weights = [sd_ref[m].astype(F32) for m in range(3 * NF)]
    for t in range(TD):
        whole = psi_ref[t * NF:(t + 1) * NF].reshape(NF * CR, CT)
        high = whole.astype(BF)
        low = (whole - high.astype(F32)).astype(BF)
        both = jnp.dot(jnp.concatenate([high, low], axis=0), pick, preferred_element_type=F32)
        value = both[:NF * CR] + both[NF * CR:]
        for f in range(NF):
            here = value[f * CR:(f + 1) * CR]
            for k in range(3):
                acc[k] = acc[k] + here * weights[3 * f + k][t:t + 1]
    owner = ids_ref[2:3]
    parts = []
    for k in range(3):
        kept = acc[k] * mask
        for s in range(2):
            parts.append(kept * (owner == s).astype(F32))
    stack = jnp.concatenate(parts, axis=0)
    high = stack.astype(BF)
    low = (stack - high.astype(F32)).astype(BF)
    label = label_ref[...]
    dims = (((1,), (1,)), ((), ()))
    total = lax.dot_general(high, label, dims, preferred_element_type=F32) + lax.dot_general(
        low, label, dims, preferred_element_type=F32)
    lane = lax.broadcasted_iota(jnp.int32, (1, 128), 1)
    line = []
    for s in range(2):
        full = jnp.zeros((1, 128), F32)
        for k in range(3):
            at = (k * 2 + s) * CR
            part = jnp.sum(total[at:at + CR], axis=0, keepdims=True)
            full = jnp.where(lane // VAR_DEV == k, part, full)
        line.append(full)
    peer = lax.broadcasted_iota(jnp.int32, (128, 128), 0)
    sens_ref[...] = jnp.where((peer // 2) % 2 == 0, line[0], line[1])
    for copy in copies:
        copy.wait()


VM, SM, HM = pltpu.VMEM, pltpu.SMEM, pltpu.HBM


def call(kernel, ins, outs, scratch=(), micros=1):
    return pl.pallas_call(
        kernel,
        out_shape=[shape for shape, _ in outs],
        in_specs=[pl.BlockSpec(memory_space=space) for space in ins],
        out_specs=[pl.BlockSpec(memory_space=space) for _, space in outs],
        scratch_shapes=list(scratch),
        cost_estimate=pl.CostEstimate(flops=0, bytes_accessed=int(micros * 3.0e6), transcendentals=0),
        compiler_params=pltpu.CompilerParams(vmem_limit_bytes=24 * 1024 * 1024),
    )


def f32(*shape):
    return jax.ShapeDtypeStruct(shape, F32)


def swap_halos(edge, halo):
    halo = lax.ppermute(halo, "rad", SWAP)
    edge = lax.ppermute(edge, "span", SWAP)
    return edge, halo


def body(adjoint_start, jac_rad, jac_circ, dissip, pseudo_step, source, node_cell, node_owner, node_local, shape_deriv):
    me = lax.axis_index("inst").astype(jnp.int32).reshape(1)
    rad = lax.axis_index("rad").astype(jnp.int32).reshape(1)
    span = lax.axis_index("span").astype(jnp.int32).reshape(1)
    n = TD * NF
    psi0 = adjoint_start.reshape(n, CR, CT)
    src = source.reshape(n, CR, CT)
    full = f32(n, CR, CT)
    line = (1, NODES)
    flat = f32(CR, CT)
    dma = pltpu.SemaphoreType.DMA
    pad = VM((NF * 32, 128), F32)
    held = [pltpu.with_memory_space_constraint(a, pltpu.HBM) for a in (
        dissip, pseudo_step, node_cell.reshape(line), node_owner.reshape(line), node_local.reshape(line), psi0, src, jac_rad, jac_circ)]
    edge0, halo0 = call(
        edge_kernel, [SM, HM], [(f32(TD, CR, 128), VM), (f32(40, HALF), VM)],
        [VM((n, 8, CT), F32), VM((n, CR, 128), F32), VM((n, CR, 128), F32), dma((3,))])(rad, held[5])
    edge0, halo0 = swap_halos(edge0, halo0)
    part, psi, jrb, jce, dis, step, sig, ids = call(
        first_kernel, [SM, SM, SM] + [HM] * 9,
        [(full, VM), (full, VM), (f32(n, NF, CT), VM), (jax.ShapeDtypeStruct((n, NF, CR, 128), BF), VM), (flat, VM), (flat, VM),
         (f32(2, 128), VM), (jax.ShapeDtypeStruct((8, NODES), jnp.int32), VM)],
        [VM((n, CR, CT), F32), VM(jac_rad.shape, BF), VM(jac_circ.shape, BF), pad] + [VM(line, jnp.int32)] * 3 + [dma((TD, 4)), dma((5,))],
        micros=3)(rad, span, me, *held)
    rim = VM((96, 128), F32)
    swapped = [(f32(TD + 1, CR, 128), VM), (f32(48, HALF), VM)]
    x, w, w_edge, w_halo = call(
        send_kernel, [SM, SM] + [VM] * 8 + [HM] * 3, [(f32(32 * ROWS, 128), HM), (full, VM)] + swapped,
        [rim, VM((32 * ROWS, 128), F32), VM((n, CR, CT), F32), VM(jac_rad.shape, BF), VM(jac_circ.shape, BF), pad, VM((n, CR, CT), F32),
         dma((LT,)), dma((3,))])(
        rad, span, psi, part, edge0, halo0, jrb, jce, dis, step, *held[6:])
    w_edge, w_halo = swap_halos(w_edge, w_halo)
    y = lax.all_to_all(x.reshape(32 * ROWS, 1, 128), "inst", 0, 0, tiled=True).reshape(32 * ROWS, 128)
    bf16 = lambda *shape: (jax.ShapeDtypeStruct(shape, BF), VM)
    pick, label = call(label_kernel, [VM], [bf16(CT, NODES), bf16(128, NODES)])(ids)
    v, w_edge, w_halo = call(
        time_kernel, [VM] * 5 + [pl.ANY] * 2, [(f32(32 * ROWS, 128), VM)] + swapped)(
        jnp.asarray(spectral_blocks()), sig, y, w_edge, w_halo, pick, label)
    u = lax.all_to_all(v.reshape(32 * ROWS, 1, 128), "inst", 0, 0, tiled=True).reshape(32 * ROWS, 128)
    psi2, parts = call(
        last_kernel, [SM] + [VM] * 15, [(full, HM), (f32(128, 128), VM)],
        [VM((n, CR, CT), F32), VM((n, CR, CT), F32), VM((TD, CR, 128), F32), VM((40, HALF), F32), rim, VM((24, 128), F32), pad, dma((TD,))])(
        rad, w, u, w_edge, w_halo, jac_rad, jac_circ, jrb, jce, dis, step, src, ids, pick, label,
        shape_deriv.transpose(1, 2, 0, 3).reshape(3 * NF, TD, NODES))
    got = lax.all_to_all(parts, ALL, 0, 0, tiled=True)
    sens, = call(total_kernel, [VM], [(f32(3, VAR_DEV), VM)])(got)
    return psi2.reshape(TD, NF, CR, CT), sens


def solution(mesh):
    in_specs = (
        P("inst", None, "rad", "span"),
        P("inst", None, None, "rad", "span"),
        P("inst", None, None, "rad", "span"),
        P("rad", "span"),
        P("rad", "span"),
        P("inst", None, "rad", "span"),
        P(("span", "rad")),
        P(("span", "rad"), None),
        P(("span", "rad")),
        P("inst", None, None, ("span", "rad")),
    )
    out_specs = (P("inst", None, "rad", "span"), P(None, "span"))
    return jax.shard_map(body, mesh=mesh, in_specs=in_specs, out_specs=out_specs, check_vma=False)
```

```python
import jax
import jax.numpy as jnp
import numpy as np
from jax import lax
from jax.experimental import pallas as pl
from jax.experimental.pallas import tpu as pltpu
from jax.sharding import PartitionSpec as P

NT = 64
TD = 2
NF = 5
CR = 16
CT = 512
LT = 4
HB = 2
BODY = 40
RIM = 3
ROWS = BODY + RIM
HALF = 256
GRP = 8 * ROWS
NODES = 1024
VAR_DEV = 32
EPS4 = 0.0625
F32 = jnp.float32
BF = jnp.bfloat16
SWAP = [(0, 1), (1, 0)]
ALL = ("inst", "span", "rad")


def spectral_blocks():
    index = np.arange(NT)
    diff = index[:, None] - index[None, :]
    safe = np.where(diff == 0, 1, diff)
    table = np.where(diff == 0, 0.0, 0.5 * np.where(diff % 2 == 0, 1.0, -1.0) / np.tan(np.pi * safe / NT))
    order = np.concatenate([index[0::2], index[1::2]])
    apply = table.T[order][:, order].astype(np.float32)
    pieces = []
    for _ in range(3):
        pieces.append(apply.astype(BF))
        apply = apply - pieces[-1].astype(np.float32)
    high, mid, low = pieces
    return np.concatenate([high, high, mid, mid, high, low], axis=1)


def split(x):
    pieces = []
    for _ in range(3):
        pieces.append(x.astype(BF))
        x = x - pieces[-1].astype(F32)
    return pieces


def pair_up(x):
    high, mid, low = split(x)
    return jnp.concatenate([high, mid, high, mid, low, high], axis=0)


def row_of(t, what, f, h):
    return ((t * 2 + what) * NF + f) * HB + h


def lanes(q):
    return slice(128 * q, 128 * q + 128)


def interior(cell, pad_ref, jr, jc, dis, q):
    lane = lax.broadcasted_iota(jnp.int32, (CR, 128), 1)
    none = jnp.zeros((CR, 128), F32)
    d_rad, d_circ, fourth = [], [], []
    for f in range(NF):
        mid = cell(f, q)
        left = none if q == 0 else cell(f, q - 1)
        right = none if q == LT - 1 else cell(f, q + 1)
        m1 = jnp.where(lane < 1, pltpu.roll(left, 1, 1), pltpu.roll(mid, 1, 1))
        m2 = jnp.where(lane < 2, pltpu.roll(left, 2, 1), pltpu.roll(mid, 2, 1))
        p1 = jnp.where(lane >= 127, pltpu.roll(right, 127, 1), pltpu.roll(mid, 127, 1))
        p2 = jnp.where(lane >= 126, pltpu.roll(right, 126, 1), pltpu.roll(mid, 126, 1))
        base = f * 32
        pad_ref[base + 8:base + 24, :] = mid
        rm2 = pad_ref[base + 6:base + 22, :]
        rm1 = pad_ref[base + 7:base + 23, :]
        rp1 = pad_ref[base + 9:base + 25, :]
        rp2 = pad_ref[base + 10:base + 26, :]
        d_circ.append(0.5 * (m1 - p1))
        d_rad.append(0.5 * (rm1 - rp1))
        fourth.append((m2 + p2) + (rm2 + rp2) - 4.0 * ((m1 + p1) + (rm1 + rp1)) + 12.0 * mid)
    out = []
    for j in range(NF):
        acc = (EPS4 * dis) * fourth[j]
        for i in range(NF):
            acc = acc + jr(i, j).astype(F32) * d_rad[i]
            acc = acc + jc(i, j).astype(F32) * d_circ[i]
        out.append(acc)
    return out


def clear_pad(pad_ref):
    pad_ref[...] = jnp.zeros(pad_ref.shape, F32)


def halo_rows(ref, at, count):
    return jnp.concatenate([ref[at:at + count, :], ref[20 + at:20 + at + count, :]], axis=1)


def corrections(rad, edge_ref, halo_ref, jrb_ref, jce_ref, dis_ref, t):
    lane = lax.broadcasted_iota(jnp.int32, (CR, 128), 1)
    diff, fourth = [], []
    edge = edge_ref[t]
    for f in range(NF):
        turn = lambda by: pltpu.roll(edge, (by - 4 * f) % 128, 1)
        m1 = jnp.where(lane < 1, turn(1), 0.0)
        m2 = jnp.where(lane < 2, turn(2), 0.0)
        p1 = jnp.where(lane >= 127, turn(-1), 0.0)
        p2 = jnp.where(lane >= 126, turn(-2), 0.0)
        diff.append(0.5 * (m1 - p1))
        fourth.append(m2 + p2 - 4.0 * (m1 + p1))
    dis_edge = EPS4 * jnp.where(lane < 64, dis_ref[:, lanes(0)], dis_ref[:, lanes(LT - 1)])
    circ = []
    for j in range(NF):
        acc = dis_edge * fourth[j]
        for i in range(NF):
            acc = acc + jce_ref[t * NF + i, j].astype(F32) * diff[i]
        circ.append(acc)
    near_row = jnp.where(rad == 0, CR - 1, 0)
    next_row = jnp.where(rad == 0, CR - 2, 1)
    sign = jnp.where(rad == 0, -0.5, 0.5)
    first, second = [halo_rows(halo_ref, (2 * t + m) * NF, NF) for m in range(2)]
    near = jnp.where(rad == 0, first, second)
    far = jnp.where(rad == 0, second, first)
    dis_near = EPS4 * dis_ref[pl.ds(near_row, 1), :]
    dis_next = EPS4 * dis_ref[pl.ds(next_row, 1), :]
    row_a = dis_near * (far - 4.0 * near)
    for i in range(NF):
        row_a = row_a + jrb_ref[t * NF + i] * (sign * near[i:i + 1])
    row_b = dis_next * near
    riota = lax.broadcasted_iota(jnp.int32, (CR, 128), 0)

    def fix(f, q):
        out = jnp.where(riota == near_row, row_a[f:f + 1, lanes(q)], 0.0)
        out = jnp.where(riota == next_row, row_b[f:f + 1, lanes(q)], out)
        if q == 0:
            out = out + jnp.where(lane < 64, circ[f], 0.0)
        if q == LT - 1:
            out = out + jnp.where(lane >= 64, circ[f], 0.0)
        return out

    return fix


def interior_pass(t, psi_ref, src_ref, jr_ref, jc_ref, dis_ref, step_ref, pad_ref, part_ref):
    for q in range(LT):
        cell = lambda f, qq: psi_ref[t * NF + f, :, lanes(qq)]
        jr = lambda i, j: jr_ref[t, i, j, :, lanes(q)]
        jc = lambda i, j: jc_ref[t, i, j, :, lanes(q)]
        res = interior(cell, pad_ref, jr, jc, dis_ref[:, lanes(q)], q)
        sigma = step_ref[:, lanes(q)]
        for f in range(NF):
            part_ref[t * NF + f, :, lanes(q)] = cell(f, q) - sigma * (res[f] - src_ref[t * NF + f, :, lanes(q)])


def edge_kernel(rad_ref, psi_hbm, edge_ref, halo_ref, rows_ref, left_ref, right_ref, sem):
    rad = rad_ref[0]
    start = pl.multiple_of(8 * (1 - rad), 8)
    copies = [
        pltpu.make_async_copy(psi_hbm.at[:, pl.ds(start, 8), :], rows_ref, sem.at[0]),
        pltpu.make_async_copy(psi_hbm.at[:, :, pl.ds(0, 128)], left_ref, sem.at[1]),
        pltpu.make_async_copy(psi_hbm.at[:, :, pl.ds(CT - 128, 128)], right_ref, sem.at[2]),
    ]
    for copy in copies:
        copy.start()
    copies[0].wait()
    put_halo(halo_ref, lambda tf: rows_ref[tf], rad)
    copies[1].wait()
    copies[2].wait()
    put_edge(edge_ref, lambda tf: (left_ref[tf], right_ref[tf]))


def pack_edge(ends):
    lane = lax.broadcasted_iota(jnp.int32, (CR, 128), 1)
    packed = None
    for f in range(NF):
        both = jnp.where(lane < 64, ends[f][0], ends[f][1])
        if f == 0:
            packed = both
        else:
            packed = jnp.where((lane >= 4 * f - 2) & (lane < 4 * f + 2), pltpu.roll(both, 4 * f, 1), packed)
    return packed


def put_edge(edge_ref, ends):
    for t in range(TD):
        edge_ref[t] = pack_edge([ends(t * NF + f) for f in range(NF)])


def put_halo(halo_ref, tile, rad):
    for t in range(TD):
        for f in range(NF):
            rows = tile(t * NF + f)
            pair = jnp.where(rad == 0, rows[6:8], rows[0:2])
            for m in range(2):
                put_row(halo_ref, (2 * t + m) * NF + f, pair[m:m + 1])


def put_row(halo_ref, at, row):
    halo_ref[at:at + 1] = row[:, :HALF]
    halo_ref[20 + at:21 + at] = row[:, HALF:]


def rim_of(tile, edge):
    lane = lax.broadcasted_iota(jnp.int32, (3, 128), 1)
    turned = pltpu.roll(edge, 2, 1)
    turned = jnp.concatenate([turned, jnp.zeros((8, 128), F32)], axis=0)
    dense = jnp.zeros((3, 128), F32)
    for g in range(6):
        part = turned[3 * g:3 * g + 3]
        part = pltpu.roll(part, 20 * g, 1) if g else part
        dense = jnp.where((lane >= 20 * g) & (lane < 20 * g + 20), part, dense)
    return jnp.concatenate([tile(q) for q in range(LT)] + [dense, jnp.zeros((5, 128), F32)], axis=0)


def edge_of(dense, edge_ref):
    for g in range(6):
        edge_ref[3 * g:3 * g + 3] = pltpu.roll(dense, 128 - 20 * g, 1) if g else dense
    return pltpu.roll(edge_ref[0:CR], 126, 1)


def halves(a, b):
    lane = lax.broadcasted_iota(jnp.int32, a.shape, 1)
    return jnp.where(lane < 64, a, pltpu.roll(b, 64, 1)), jnp.where(lane < 64, pltpu.roll(a, 64, 1), b)


def first_kernel(rad_ref, span_ref, me_ref, dis_hbm, step_hbm, cell_hbm, owner_hbm, local_hbm, psi_hbm, src_hbm, jr_hbm, jc_hbm,
                 part_ref, psi_ref, jrb_ref, jce_ref, dis_ref, step_ref, sig_ref, ids_ref,
                 src_ref, jr_ref, jc_ref, pad_ref, cell_ref, owner_ref, local_ref, sem, sem_small):
    rad = rad_ref[0]
    small = [pltpu.make_async_copy(a, b, sem_small.at[i]) for i, (a, b) in enumerate([
        (dis_hbm, dis_ref), (step_hbm, step_ref), (cell_hbm, cell_ref), (owner_hbm, owner_ref), (local_hbm, local_ref)])]
    copies = []
    for t in range(TD):
        tf = pl.ds(t * NF, NF)
        copies.append([
            pltpu.make_async_copy(psi_hbm.at[tf], psi_ref.at[tf], sem.at[t, 0]),
            pltpu.make_async_copy(jr_hbm.at[t], jr_ref.at[t], sem.at[t, 1]),
            pltpu.make_async_copy(jc_hbm.at[t], jc_ref.at[t], sem.at[t, 2]),
            pltpu.make_async_copy(src_hbm.at[tf], src_ref.at[tf], sem.at[t, 3]),
        ])
    for copy in small + copies[0] + copies[1]:
        copy.start()
    clear_pad(pad_ref)
    lane = lax.broadcasted_iota(jnp.int32, (CR, 128), 1)
    for copy in small:
        copy.wait()
    ids_ref[0:1] = cell_ref[...] % CT
    ids_ref[1:2] = cell_ref[...] // CT
    ids_ref[2:3] = owner_ref[...]
    ids_ref[3:4] = local_ref[...]
    me = me_ref[0]
    sig = jnp.zeros((2, 128), F32)
    for p in range(8):
        for q in range(LT):
            here = jnp.concatenate([step_ref[p:p + 1, lanes(q)], step_ref[p + 8:p + 9, lanes(q)]], axis=0)
            sig = jnp.where(me == 8 * q + p, here, sig)
    sig_ref[...] = sig
    for t in range(TD):
        for copy in copies[t]:
            copy.wait()

        @pl.when((span_ref[0] == 1) | (t == 0))
        def _():
            interior_pass(t, psi_ref, src_ref, jr_ref, jc_ref, dis_ref, step_ref, pad_ref, part_ref)

        for i in range(NF):
            for j in range(NF):
                whole = jr_ref[t, i, j].astype(F32)
                jrb_ref[t * NF + i, j:j + 1] = jnp.where(rad == 0, whole[CR - 1:CR], whole[0:1])
                jce_ref[t * NF + i, j] = jnp.where(
                    lane < 64, jc_ref[t, i, j, :, lanes(0)].astype(F32), jc_ref[t, i, j, :, lanes(LT - 1)].astype(F32)).astype(BF)


def send_kernel(rad_ref, span_ref, psi_ref, part_ref, edge_ref, halo_ref, jrb_ref, jce_ref, dis_ref, step_ref, src_hbm, jr_hbm, jc_hbm,
                x_hbm, w_ref, w_edge_ref, w_halo_ref, rim_ref, x_ref, src_ref, jr_ref, jc_ref, pad_ref, late_ref, sem, sem_in):
    rad = rad_ref[0]

    late_ref[...] = part_ref[...]

    @pl.when(span_ref[0] == 0)
    def _():
        last = pl.ds((TD - 1) * NF, NF)
        loads = [pltpu.make_async_copy(a, b, sem_in.at[i]) for i, (a, b) in enumerate(
            [(src_hbm.at[last], src_ref.at[last]), (jr_hbm.at[TD - 1], jr_ref.at[TD - 1]), (jc_hbm.at[TD - 1], jc_ref.at[TD - 1])])]
        for load in loads:
            load.start()
        clear_pad(pad_ref)
        for load in loads:
            load.wait()
        interior_pass(TD - 1, psi_ref, src_ref, jr_ref, jc_ref, dis_ref, step_ref, pad_ref, late_ref)

    fixes = [corrections(rad, edge_ref, halo_ref, jrb_ref, jce_ref, dis_ref, t) for t in range(TD)]
    rims = [rim_of(lambda q: halo_ref[20 * (q // 2) + 10 * t:20 * (q // 2) + 10 * t + 10, lanes(q % 2)], edge_ref[t])
            for t in range(TD)]
    low, high = halves(*rims)
    rim_ref[0:48] = low
    rim_ref[48:96] = high
    for e in range(RIM):
        x_ref[pl.ds(BODY + e, 32, stride=ROWS), :] = rim_ref[32 * e:32 * e + 32]
    copies = []
    for q in range(LT):
        for t in range(TD):
            for f in range(NF):
                mid = psi_ref[t * NF + f, :, lanes(q)]
                w = late_ref[t * NF + f, :, lanes(q)] - step_ref[:, lanes(q)] * fixes[t](f, q)
                w_ref[t * NF + f, :, lanes(q)] = w
                for h in range(HB):
                    x_ref[pl.ds(q * GRP + row_of(t, 0, f, h), 8, stride=ROWS), :] = mid[8 * h:8 * h + 8]
                    x_ref[pl.ds(q * GRP + row_of(t, 1, f, h), 8, stride=ROWS), :] = w[8 * h:8 * h + 8]
        span = pl.ds(q * GRP, GRP)
        copies.append(pltpu.make_async_copy(x_ref.at[span], x_hbm.at[span], sem.at[q]))
        copies[q].start()
    put_edge(w_edge_ref, lambda tf: (w_ref[tf, :, lanes(0)], w_ref[tf, :, lanes(LT - 1)]))
    start = pl.multiple_of(8 * (1 - rad), 8)
    put_halo(w_halo_ref, lambda tf: w_ref[tf, pl.ds(start, 8), :], rad)
    w_edge_ref[TD] = pack_edge([(step_ref[:, lanes(0)], step_ref[:, lanes(LT - 1)])] * NF)
    sigma = jnp.where(rad == 0, step_ref[CR - 2:CR], step_ref[0:2])
    w_halo_ref[40:42] = sigma[:, :HALF]
    w_halo_ref[42:44] = sigma[:, HALF:]
    w_halo_ref[44:48] = jnp.zeros((4, HALF), F32)
    for copy in copies:
        copy.wait()


def label_kernel(ids_ref, pick_ref, label_ref):
    pick_ref[...] = (lax.broadcasted_iota(jnp.int32, (CT, NODES), 0) == ids_ref[0:1]).astype(F32).astype(BF)
    label_ref[...] = (lax.broadcasted_iota(jnp.int32, (128, NODES), 0) % VAR_DEV == ids_ref[3:4]).astype(F32).astype(BF)


def total_kernel(got_ref, sens_ref):
    line = jnp.sum(got_ref[...], axis=0, keepdims=True)
    for k in range(3):
        sens_ref[k:k + 1, :] = pltpu.roll(line, (128 - VAR_DEV * k) % 128, 1)[:, :VAR_DEV]


def time_kernel(table_ref, sig_ref, y_ref, edge_ref, halo_ref, pick_ref, label_ref, v_ref, edge_out_ref, halo_out_ref):
    edge_out_ref[...] = edge_ref[...]
    halo_out_ref[...] = halo_ref[...]
    table = table_ref[...]

    def apply(x):
        return jnp.dot(table, pair_up(x), preferred_element_type=F32)

    count = 2 * NF

    def pick(at):
        return y_ref[pl.ds(at, 32, stride=ROWS), :]

    def put(at, value):
        v_ref[pl.ds(at, 32, stride=ROWS), :] = value

    def row(what, m, t):
        return (t * 2 + what) * count + m

    def gather(what):
        return [jnp.concatenate([pick(row(what, m, t)) for t in range(TD)], axis=0) for m in range(count)]

    def scatter(what, value):
        for m in range(count):
            for t in range(TD):
                put(row(what, m, t), value[32 * t:32 * t + 32, lanes(m)])

    rims = [pick(BODY + e) for e in range(RIM)]
    rims = [jnp.concatenate(halves(rims[0], rims[1]), axis=0), jnp.concatenate([rims[2], pltpu.roll(rims[2], 64, 1)], axis=0)]
    sigma = jnp.concatenate([sig_ref[0:1, :], sig_ref[1:2, :]] * NF, axis=1)
    time0 = apply(jnp.concatenate(gather(0) + rims, axis=1))
    scatter(0, time0)
    pair, single = [time0[:, lanes(count + m)] for m in range(2)]
    for e, value in enumerate(halves(pair[:32], pair[32:]) + halves(single[:32], single[32:])[:1]):
        put(BODY + e, value)
    psi1 = jnp.concatenate(gather(1), axis=1) - sigma * time0[:, :128 * count]
    scatter(1, apply(psi1))


def plane(ref, what, t, f, q):
    return jnp.concatenate([ref[pl.ds(q * GRP + row_of(t, what, f, h), 8, stride=ROWS), :] for h in range(HB)], axis=0)


def last_kernel(rad_ref, w_ref, u_ref, w_edge_ref, w_halo_ref, jr_ref, jc_ref, jrb_ref, jce_ref, dis_ref,
                step_ref, src_ref, ids_ref, pick_ref, label_ref, sd_ref, out_hbm, sens_ref, psi1_ref, psi_ref, edge_ref, halo_ref, rim_ref, turn_ref, pad_ref, sem):
    rad = rad_ref[0]
    clear_pad(pad_ref)
    for e in range(RIM):
        rim_ref[32 * e:32 * e + 32] = u_ref[pl.ds(BODY + e, 32, stride=ROWS), :]
    rims = halves(rim_ref[0:48], rim_ref[48:96])
    for t in range(TD):
        for m in range(2):
            at = (2 * t + m) * NF
            for q in range(LT):
                side = q // 2
                here = slice(20 * side + at, 20 * side + at + NF)
                sigma = w_halo_ref[40 + 2 * side + m:41 + 2 * side + m, lanes(q % 2)]
                halo_ref[here, lanes(q % 2)] = (
                    w_halo_ref[here, lanes(q % 2)] - sigma * rims[t][10 * q + NF * m:10 * q + NF * m + NF])
        edge_ref[t] = w_edge_ref[t] - w_edge_ref[TD] * edge_of(rims[t][40:43], turn_ref)
    copies = []
    for t in range(TD):
        fix = corrections(rad, edge_ref, halo_ref, jrb_ref, jce_ref, dis_ref, t)
        for f in range(NF):
            for q in range(LT):
                psi1_ref[t * NF + f, :, lanes(q)] = (
                    w_ref[t * NF + f, :, lanes(q)] - step_ref[:, lanes(q)] * plane(u_ref, 0, t, f, q))
        for q in range(LT):
            cell = lambda f, qq: psi1_ref[t * NF + f, :, lanes(qq)]
            jr = lambda i, j: jr_ref[t, i, j, :, lanes(q)]
            jc = lambda i, j: jc_ref[t, i, j, :, lanes(q)]
            res = interior(cell, pad_ref, jr, jc, dis_ref[:, lanes(q)], q)
            sigma = step_ref[:, lanes(q)]
            for f in range(NF):
                psi_ref[t * NF + f, :, lanes(q)] = cell(f, q) - sigma * (
                    res[f] + fix(f, q) + plane(u_ref, 1, t, f, q) - src_ref[t * NF + f, :, lanes(q)])
        tf = pl.ds(t * NF, NF)
        copies.append(pltpu.make_async_copy(psi_ref.at[tf], out_hbm.at[tf], sem.at[t]))
        copies[t].start()
    pick = pick_ref[...]
    mask = (lax.broadcasted_iota(jnp.int32, (CR, NODES), 0) == ids_ref[1:2]).astype(F32)
    acc = [jnp.zeros((CR, NODES), F32) for _ in range(3)]
    weights = [sd_ref[m].astype(F32) for m in range(3 * NF)]
    for t in range(TD):
        whole = psi_ref[t * NF:(t + 1) * NF].reshape(NF * CR, CT)
        got = jnp.dot(jnp.concatenate(split(whole), axis=0), pick, preferred_element_type=F32)
        value = got[:NF * CR] + got[NF * CR:2 * NF * CR] + got[2 * NF * CR:]
        for f in range(NF):
            here = value[f * CR:(f + 1) * CR]
            for k in range(3):
                acc[k] = acc[k] + here * weights[3 * f + k][t:t + 1]
    owner = ids_ref[2:3]
    parts = []
    for k in range(3):
        kept = acc[k] * mask
        for s in range(2):
            parts.append(kept * (owner == s).astype(F32))
    stack = jnp.concatenate(parts, axis=0)
    label = label_ref[...]
    dims = (((1,), (1,)), ((), ()))
    total = sum(lax.dot_general(piece, label, dims, preferred_element_type=F32) for piece in split(stack))
    lane = lax.broadcasted_iota(jnp.int32, (1, 128), 1)
    line = []
    for s in range(2):
        full = jnp.zeros((1, 128), F32)
        for k in range(3):
            at = (k * 2 + s) * CR
            part = jnp.sum(total[at:at + CR], axis=0, keepdims=True)
            full = jnp.where(lane // VAR_DEV == k, part, full)
        line.append(full)
    peer = lax.broadcasted_iota(jnp.int32, (128, 128), 0)
    sens_ref[...] = jnp.where((peer // 2) % 2 == 0, line[0], line[1])
    for copy in copies:
        copy.wait()


VM, SM, HM = pltpu.VMEM, pltpu.SMEM, pltpu.HBM


def call(kernel, ins, outs, scratch=(), micros=1):
    return pl.pallas_call(
        kernel,
        out_shape=[shape for shape, _ in outs],
        in_specs=[pl.BlockSpec(memory_space=space) for space in ins],
        out_specs=[pl.BlockSpec(memory_space=space) for _, space in outs],
        scratch_shapes=list(scratch),
        cost_estimate=pl.CostEstimate(flops=0, bytes_accessed=int(micros * 3.0e6), transcendentals=0),
        compiler_params=pltpu.CompilerParams(vmem_limit_bytes=24 * 1024 * 1024),
    )


def f32(*shape):
    return jax.ShapeDtypeStruct(shape, F32)


def swap_halos(edge, halo):
    halo = lax.ppermute(halo, "rad", SWAP)
    edge = lax.ppermute(edge, "span", SWAP)
    return edge, halo


def body(adjoint_start, jac_rad, jac_circ, dissip, pseudo_step, source, node_cell, node_owner, node_local, shape_deriv):
    me = lax.axis_index("inst").astype(jnp.int32).reshape(1)
    rad = lax.axis_index("rad").astype(jnp.int32).reshape(1)
    span = lax.axis_index("span").astype(jnp.int32).reshape(1)
    n = TD * NF
    psi0 = adjoint_start.reshape(n, CR, CT)
    src = source.reshape(n, CR, CT)
    full = f32(n, CR, CT)
    line = (1, NODES)
    flat = f32(CR, CT)
    dma = pltpu.SemaphoreType.DMA
    pad = VM((NF * 32, 128), F32)
    held = [pltpu.with_memory_space_constraint(a, pltpu.HBM) for a in (
        dissip, pseudo_step, node_cell.reshape(line), node_owner.reshape(line), node_local.reshape(line), psi0, src, jac_rad, jac_circ)]
    edge0, halo0 = call(
        edge_kernel, [SM, HM], [(f32(TD, CR, 128), VM), (f32(40, HALF), VM)],
        [VM((n, 8, CT), F32), VM((n, CR, 128), F32), VM((n, CR, 128), F32), dma((3,))])(rad, held[5])
    edge0, halo0 = swap_halos(edge0, halo0)
    part, psi, jrb, jce, dis, step, sig, ids = call(
        first_kernel, [SM, SM, SM] + [HM] * 9,
        [(full, VM), (full, VM), (f32(n, NF, CT), VM), (jax.ShapeDtypeStruct((n, NF, CR, 128), BF), VM), (flat, VM), (flat, VM),
         (f32(2, 128), VM), (jax.ShapeDtypeStruct((8, NODES), jnp.int32), VM)],
        [VM((n, CR, CT), F32), VM(jac_rad.shape, BF), VM(jac_circ.shape, BF), pad] + [VM(line, jnp.int32)] * 3 + [dma((TD, 4)), dma((5,))],
        micros=3)(rad, span, me, *held)
    rim = VM((96, 128), F32)
    swapped = [(f32(TD + 1, CR, 128), VM), (f32(48, HALF), VM)]
    x, w, w_edge, w_halo = call(
        send_kernel, [SM, SM] + [VM] * 8 + [HM] * 3, [(f32(32 * ROWS, 128), HM), (full, VM)] + swapped,
        [rim, VM((32 * ROWS, 128), F32), VM((n, CR, CT), F32), VM(jac_rad.shape, BF), VM(jac_circ.shape, BF), pad, VM((n, CR, CT), F32),
         dma((LT,)), dma((3,))])(
        rad, span, psi, part, edge0, halo0, jrb, jce, dis, step, *held[6:])
    w_edge, w_halo = swap_halos(w_edge, w_halo)
    y = lax.all_to_all(x.reshape(32 * ROWS, 1, 128), "inst", 0, 0, tiled=True).reshape(32 * ROWS, 128)
    bf16 = lambda *shape: (jax.ShapeDtypeStruct(shape, BF), VM)
    pick, label = call(label_kernel, [VM], [bf16(CT, NODES), bf16(128, NODES)])(ids)
    v, w_edge, w_halo = call(
        time_kernel, [VM] * 5 + [pl.ANY] * 2, [(f32(32 * ROWS, 128), VM)] + swapped)(
        jnp.asarray(spectral_blocks()), sig, y, w_edge, w_halo, pick, label)
    u = lax.all_to_all(v.reshape(32 * ROWS, 1, 128), "inst", 0, 0, tiled=True).reshape(32 * ROWS, 128)
    psi2, parts = call(
        last_kernel, [SM] + [VM] * 15, [(full, HM), (f32(128, 128), VM)],
        [VM((n, CR, CT), F32), VM((n, CR, CT), F32), VM((TD, CR, 128), F32), VM((40, HALF), F32), rim, VM((24, 128), F32), pad, dma((TD,))])(
        rad, w, u, w_edge, w_halo, jac_rad, jac_circ, jrb, jce, dis, step, src, ids, pick, label,
        shape_deriv.transpose(1, 2, 0, 3).reshape(3 * NF, TD, NODES))
    got = lax.all_to_all(parts, ALL, 0, 0, tiled=True)
    sens, = call(total_kernel, [VM], [(f32(3, VAR_DEV), VM)])(got)
    return psi2.reshape(TD, NF, CR, CT), sens


def solution(mesh):
    in_specs = (
        P("inst", None, "rad", "span"),
        P("inst", None, None, "rad", "span"),
        P("inst", None, None, "rad", "span"),
        P("rad", "span"),
        P("rad", "span"),
        P("inst", None, "rad", "span"),
        P(("span", "rad")),
        P(("span", "rad"), None),
        P(("span", "rad")),
        P("inst", None, None, ("span", "rad")),
    )
    out_specs = (P("inst", None, "rad", "span"), P(None, "span"))
    return jax.shard_map(body, mesh=mesh, in_specs=in_specs, out_specs=out_specs, check_vma=False)
```

```python
import jax
import jax.numpy as jnp
import numpy as np
from jax import lax
from jax.experimental import pallas as pl
from jax.experimental.pallas import tpu as pltpu
from jax.sharding import PartitionSpec as P

NT = 64
TD = 2
NF = 5
CR = 16
CT = 512
LT = 4
HB = 2
BODY = 40
RIM = 3
ROWS = BODY + RIM
HALF = 256
GRP = 8 * ROWS
NODES = 1024
VAR_DEV = 32
EPS4 = 0.0625
F32 = jnp.float32
BF = jnp.bfloat16
SWAP = [(0, 1), (1, 0)]
ALL = ("inst", "span", "rad")


def spectral_blocks():
    index = np.arange(NT)
    diff = index[:, None] - index[None, :]
    safe = np.where(diff == 0, 1, diff)
    table = np.where(diff == 0, 0.0, 0.5 * np.where(diff % 2 == 0, 1.0, -1.0) / np.tan(np.pi * safe / NT))
    order = np.concatenate([index[0::2], index[1::2]])
    apply = table.T[order][:, order].astype(np.float32)
    pieces = []
    for _ in range(3):
        pieces.append(apply.astype(BF))
        apply = apply - pieces[-1].astype(np.float32)
    high, mid, low = pieces
    return np.concatenate([high, high, mid, mid, high, low], axis=1)


def split(x):
    pieces = []
    for _ in range(3):
        pieces.append(x.astype(BF))
        x = x - pieces[-1].astype(F32)
    return pieces


def pair_up(x):
    high, mid, low = split(x)
    return jnp.concatenate([high, mid, high, mid, low, high], axis=0)


def row_of(t, what, f, h):
    return ((t * 2 + what) * NF + f) * HB + h


def lanes(q):
    return slice(128 * q, 128 * q + 128)


def interior(cell, pad_ref, jr, jc, dis, q):
    lane = lax.broadcasted_iota(jnp.int32, (CR, 128), 1)
    none = jnp.zeros((CR, 128), F32)
    d_rad, d_circ, fourth = [], [], []
    for f in range(NF):
        mid = cell(f, q)
        left = none if q == 0 else cell(f, q - 1)
        right = none if q == LT - 1 else cell(f, q + 1)
        m1 = jnp.where(lane < 1, pltpu.roll(left, 1, 1), pltpu.roll(mid, 1, 1))
        m2 = jnp.where(lane < 2, pltpu.roll(left, 2, 1), pltpu.roll(mid, 2, 1))
        p1 = jnp.where(lane >= 127, pltpu.roll(right, 127, 1), pltpu.roll(mid, 127, 1))
        p2 = jnp.where(lane >= 126, pltpu.roll(right, 126, 1), pltpu.roll(mid, 126, 1))
        base = f * 32
        pad_ref[base + 8:base + 24, :] = mid
        rm2 = pad_ref[base + 6:base + 22, :]
        rm1 = pad_ref[base + 7:base + 23, :]
        rp1 = pad_ref[base + 9:base + 25, :]
        rp2 = pad_ref[base + 10:base + 26, :]
        d_circ.append(0.5 * (m1 - p1))
        d_rad.append(0.5 * (rm1 - rp1))
        fourth.append((m2 + p2) + (rm2 + rp2) - 4.0 * ((m1 + p1) + (rm1 + rp1)) + 12.0 * mid)
    out = []
    for j in range(NF):
        acc = (EPS4 * dis) * fourth[j]
        for i in range(NF):
            acc = acc + jr(i, j).astype(F32) * d_rad[i]
            acc = acc + jc(i, j).astype(F32) * d_circ[i]
        out.append(acc)
    return out


def clear_pad(pad_ref):
    pad_ref[...] = jnp.zeros(pad_ref.shape, F32)


def halo_rows(ref, at, count):
    return jnp.concatenate([ref[at:at + count, :], ref[20 + at:20 + at + count, :]], axis=1)


def corrections(rad, edge_ref, halo_ref, jrb_ref, jce_ref, dis_ref, t):
    lane = lax.broadcasted_iota(jnp.int32, (CR, 128), 1)
    diff, fourth = [], []
    edge = edge_ref[t]
    for f in range(NF):
        turn = lambda by: pltpu.roll(edge, (by - 4 * f) % 128, 1)
        m1 = jnp.where(lane < 1, turn(1), 0.0)
        m2 = jnp.where(lane < 2, turn(2), 0.0)
        p1 = jnp.where(lane >= 127, turn(-1), 0.0)
        p2 = jnp.where(lane >= 126, turn(-2), 0.0)
        diff.append(0.5 * (m1 - p1))
        fourth.append(m2 + p2 - 4.0 * (m1 + p1))
    dis_edge = EPS4 * jnp.where(lane < 64, dis_ref[:, lanes(0)], dis_ref[:, lanes(LT - 1)])
    circ = []
    for j in range(NF):
        acc = dis_edge * fourth[j]
        for i in range(NF):
            acc = acc + jce_ref[t * NF + i, j].astype(F32) * diff[i]
        circ.append(acc)
    near_row = jnp.where(rad == 0, CR - 1, 0)
    next_row = jnp.where(rad == 0, CR - 2, 1)
    sign = jnp.where(rad == 0, -0.5, 0.5)
    first, second = [halo_rows(halo_ref, (2 * t + m) * NF, NF) for m in range(2)]
    near = jnp.where(rad == 0, first, second)
    far = jnp.where(rad == 0, second, first)
    dis_near = EPS4 * dis_ref[pl.ds(near_row, 1), :]
    dis_next = EPS4 * dis_ref[pl.ds(next_row, 1), :]
    row_a = dis_near * (far - 4.0 * near)
    for i in range(NF):
        row_a = row_a + jrb_ref[t * NF + i] * (sign * near[i:i + 1])
    row_b = dis_next * near
    riota = lax.broadcasted_iota(jnp.int32, (CR, 128), 0)

    def fix(f, q):
        out = jnp.where(riota == near_row, row_a[f:f + 1, lanes(q)], 0.0)
        out = jnp.where(riota == next_row, row_b[f:f + 1, lanes(q)], out)
        if q == 0:
            out = out + jnp.where(lane < 64, circ[f], 0.0)
        if q == LT - 1:
            out = out + jnp.where(lane >= 64, circ[f], 0.0)
        return out

    return fix


def interior_pass(t, psi_ref, src_ref, jr_ref, jc_ref, dis_ref, step_ref, pad_ref, part_ref, first=0):
    for q in range(LT):
        cell = lambda f, qq: psi_ref[t * NF + f, :, lanes(qq)]
        jr = lambda i, j: jr_ref[t, i, j, :, lanes(q)]
        jc = lambda i, j: jc_ref[t, i, j, :, lanes(q)]
        res = interior(cell, pad_ref, jr, jc, dis_ref[:, lanes(q)], q)
        sigma = step_ref[:, lanes(q)]
        for f in range(NF):
            part_ref[t * NF + f - first, :, lanes(q)] = cell(f, q) - sigma * (res[f] - src_ref[t * NF + f, :, lanes(q)])


def edge_kernel(rad_ref, psi_hbm, edge_ref, halo_ref, rows_ref, left_ref, right_ref, sem):
    rad = rad_ref[0]
    start = pl.multiple_of(8 * (1 - rad), 8)
    copies = [
        pltpu.make_async_copy(psi_hbm.at[:, pl.ds(start, 8), :], rows_ref, sem.at[0]),
        pltpu.make_async_copy(psi_hbm.at[:, :, pl.ds(0, 128)], left_ref, sem.at[1]),
        pltpu.make_async_copy(psi_hbm.at[:, :, pl.ds(CT - 128, 128)], right_ref, sem.at[2]),
    ]
    for copy in copies:
        copy.start()
    copies[0].wait()
    put_halo(halo_ref, lambda tf: rows_ref[tf], rad)
    copies[1].wait()
    copies[2].wait()
    put_edge(edge_ref, lambda tf: (left_ref[tf], right_ref[tf]))


def pack_edge(ends):
    lane = lax.broadcasted_iota(jnp.int32, (CR, 128), 1)
    packed = None
    for f in range(NF):
        both = jnp.where(lane < 64, ends[f][0], ends[f][1])
        if f == 0:
            packed = both
        else:
            packed = jnp.where((lane >= 4 * f - 2) & (lane < 4 * f + 2), pltpu.roll(both, 4 * f, 1), packed)
    return packed


def put_edge(edge_ref, ends):
    for t in range(TD):
        edge_ref[t] = pack_edge([ends(t * NF + f) for f in range(NF)])


def put_halo(halo_ref, tile, rad):
    for t in range(TD):
        for f in range(NF):
            rows = tile(t * NF + f)
            pair = jnp.where(rad == 0, rows[6:8], rows[0:2])
            for m in range(2):
                put_row(halo_ref, (2 * t + m) * NF + f, pair[m:m + 1])


def put_row(halo_ref, at, row):
    halo_ref[at:at + 1] = row[:, :HALF]
    halo_ref[20 + at:21 + at] = row[:, HALF:]


def rim_of(tile, edge):
    lane = lax.broadcasted_iota(jnp.int32, (3, 128), 1)
    turned = pltpu.roll(edge, 2, 1)
    turned = jnp.concatenate([turned, jnp.zeros((8, 128), F32)], axis=0)
    dense = jnp.zeros((3, 128), F32)
    for g in range(6):
        part = turned[3 * g:3 * g + 3]
        part = pltpu.roll(part, 20 * g, 1) if g else part
        dense = jnp.where((lane >= 20 * g) & (lane < 20 * g + 20), part, dense)
    return jnp.concatenate([tile(q) for q in range(LT)] + [dense, jnp.zeros((5, 128), F32)], axis=0)


def edge_of(dense, edge_ref):
    for g in range(6):
        edge_ref[3 * g:3 * g + 3] = pltpu.roll(dense, 128 - 20 * g, 1) if g else dense
    return pltpu.roll(edge_ref[0:CR], 126, 1)


def halves(a, b):
    lane = lax.broadcasted_iota(jnp.int32, a.shape, 1)
    return jnp.where(lane < 64, a, pltpu.roll(b, 64, 1)), jnp.where(lane < 64, pltpu.roll(a, 64, 1), b)


def first_kernel(rad_ref, span_ref, dis_hbm, step_hbm, psi_hbm, src_hbm, jr_hbm, jc_hbm,
                 part_ref, psi_ref, jrb_ref, jce_ref, dis_ref, step_ref, src_ref, jr_ref, jc_ref, pad_ref, sem, sem_small):
    rad = rad_ref[0]
    small = [pltpu.make_async_copy(a, b, sem_small.at[i]) for i, (a, b) in enumerate([
        (dis_hbm, dis_ref), (step_hbm, step_ref)])]
    copies = []
    for t in range(TD):
        tf = pl.ds(t * NF, NF)
        copies.append([
            pltpu.make_async_copy(psi_hbm.at[tf], psi_ref.at[tf], sem.at[t, 0]),
            pltpu.make_async_copy(jr_hbm.at[t], jr_ref.at[t], sem.at[t, 1]),
            pltpu.make_async_copy(jc_hbm.at[t], jc_ref.at[t], sem.at[t, 2]),
            pltpu.make_async_copy(src_hbm.at[tf], src_ref.at[tf], sem.at[t, 3]),
        ])
    for copy in small + copies[0] + copies[1]:
        copy.start()
    clear_pad(pad_ref)
    lane = lax.broadcasted_iota(jnp.int32, (CR, 128), 1)
    for copy in small:
        copy.wait()
    for t in range(TD):
        for copy in copies[t]:
            copy.wait()

        @pl.when((span_ref[0] == 1) | (t == 0))
        def _():
            interior_pass(t, psi_ref, src_ref, jr_ref, jc_ref, dis_ref, step_ref, pad_ref, part_ref)

        for i in range(NF):
            for j in range(NF):
                whole = jr_ref[t, i, j].astype(F32)
                jrb_ref[t * NF + i, j:j + 1] = jnp.where(rad == 0, whole[CR - 1:CR], whole[0:1])
                jce_ref[t * NF + i, j] = jnp.where(
                    lane < 64, jc_ref[t, i, j, :, lanes(0)].astype(F32), jc_ref[t, i, j, :, lanes(LT - 1)].astype(F32)).astype(BF)


def send_kernel(rad_ref, span_ref, psi_ref, part_ref, edge_ref, halo_ref, jrb_ref, jce_ref, dis_ref, step_ref, src_hbm, jr_hbm, jc_hbm,
                x_hbm, w_ref, w_edge_ref, w_halo_ref, rim_ref, x_ref, src_ref, jr_ref, jc_ref, pad_ref, late_ref, sem, sem_in):
    rad = rad_ref[0]


    @pl.when(span_ref[0] != 0)
    def _():
        late_ref[...] = part_ref[(TD - 1) * NF:]

    @pl.when(span_ref[0] == 0)
    def _():
        last = pl.ds((TD - 1) * NF, NF)
        loads = [pltpu.make_async_copy(a, b, sem_in.at[i]) for i, (a, b) in enumerate(
            [(src_hbm.at[last], src_ref.at[last]), (jr_hbm.at[TD - 1], jr_ref.at[TD - 1]), (jc_hbm.at[TD - 1], jc_ref.at[TD - 1])])]
        for load in loads:
            load.start()
        clear_pad(pad_ref)
        for load in loads:
            load.wait()
        interior_pass(TD - 1, psi_ref, src_ref, jr_ref, jc_ref, dis_ref, step_ref, pad_ref, late_ref, (TD - 1) * NF)

    fixes = [corrections(rad, edge_ref, halo_ref, jrb_ref, jce_ref, dis_ref, t) for t in range(TD)]
    rims = [rim_of(lambda q: halo_ref[20 * (q // 2) + 10 * t:20 * (q // 2) + 10 * t + 10, lanes(q % 2)], edge_ref[t])
            for t in range(TD)]
    low, high = halves(*rims)
    rim_ref[0:48] = low
    rim_ref[48:96] = high
    for e in range(RIM):
        x_ref[pl.ds(BODY + e, 32, stride=ROWS), :] = rim_ref[32 * e:32 * e + 32]
    copies = []
    for q in range(LT):
        for t in range(TD):
            for f in range(NF):
                mid = psi_ref[t * NF + f, :, lanes(q)]
                before = part_ref[f, :, lanes(q)] if t < TD - 1 else late_ref[f, :, lanes(q)]
                w = before - step_ref[:, lanes(q)] * fixes[t](f, q)
                w_ref[t * NF + f, :, lanes(q)] = w
                for h in range(HB):
                    x_ref[pl.ds(q * GRP + row_of(t, 0, f, h), 8, stride=ROWS), :] = mid[8 * h:8 * h + 8]
                    x_ref[pl.ds(q * GRP + row_of(t, 1, f, h), 8, stride=ROWS), :] = w[8 * h:8 * h + 8]
        span = pl.ds(q * GRP, GRP)
        copies.append(pltpu.make_async_copy(x_ref.at[span], x_hbm.at[span], sem.at[q]))
        copies[q].start()
    put_edge(w_edge_ref, lambda tf: (w_ref[tf, :, lanes(0)], w_ref[tf, :, lanes(LT - 1)]))
    start = pl.multiple_of(8 * (1 - rad), 8)
    put_halo(w_halo_ref, lambda tf: w_ref[tf, pl.ds(start, 8), :], rad)
    w_edge_ref[TD] = pack_edge([(step_ref[:, lanes(0)], step_ref[:, lanes(LT - 1)])] * NF)
    sigma = jnp.where(rad == 0, step_ref[CR - 2:CR], step_ref[0:2])
    w_halo_ref[40:42] = sigma[:, :HALF]
    w_halo_ref[42:44] = sigma[:, HALF:]
    w_halo_ref[44:48] = jnp.zeros((4, HALF), F32)
    for copy in copies:
        copy.wait()


def label_kernel(me_ref, cell_hbm, owner_hbm, local_hbm, step_ref, pick_ref, label_ref, ids_ref, sig_ref, cell_ref, owner_ref,
                 local_ref, sem):
    loads = [pltpu.make_async_copy(a, b, sem.at[i]) for i, (a, b) in enumerate(
        [(cell_hbm, cell_ref), (owner_hbm, owner_ref), (local_hbm, local_ref)])]
    for load in loads:
        load.start()
    for load in loads:
        load.wait()
    ids_ref[0:1] = cell_ref[...] % CT
    ids_ref[1:2] = cell_ref[...] // CT
    ids_ref[2:3] = owner_ref[...]
    ids_ref[3:4] = local_ref[...]
    me = me_ref[0]
    sig = jnp.zeros((2, 128), F32)
    for p in range(8):
        for q in range(LT):
            here = jnp.concatenate([step_ref[p:p + 1, lanes(q)], step_ref[p + 8:p + 9, lanes(q)]], axis=0)
            sig = jnp.where(me == 8 * q + p, here, sig)
    sig_ref[...] = sig
    pick_ref[...] = (lax.broadcasted_iota(jnp.int32, (CT, NODES), 0) == ids_ref[0:1]).astype(F32).astype(BF)
    label_ref[...] = (lax.broadcasted_iota(jnp.int32, (128, NODES), 0) % VAR_DEV == ids_ref[3:4]).astype(F32).astype(BF)


def total_kernel(got_ref, sens_ref):
    line = jnp.sum(got_ref[...], axis=0, keepdims=True)
    for k in range(3):
        sens_ref[k:k + 1, :] = pltpu.roll(line, (128 - VAR_DEV * k) % 128, 1)[:, :VAR_DEV]


def time_kernel(table_ref, sig_ref, y_ref, edge_ref, halo_ref, pick_ref, label_ref, v_ref, edge_out_ref, halo_out_ref):
    edge_out_ref[...] = edge_ref[...]
    halo_out_ref[...] = halo_ref[...]
    table = table_ref[...]

    def apply(x):
        return jnp.dot(table, pair_up(x), preferred_element_type=F32)

    count = 2 * NF

    def pick(at):
        return y_ref[pl.ds(at, 32, stride=ROWS), :]

    def put(at, value):
        v_ref[pl.ds(at, 32, stride=ROWS), :] = value

    def row(what, m, t):
        return (t * 2 + what) * count + m

    def gather(what):
        return [jnp.concatenate([pick(row(what, m, t)) for t in range(TD)], axis=0) for m in range(count)]

    def scatter(what, value):
        for m in range(count):
            for t in range(TD):
                put(row(what, m, t), value[32 * t:32 * t + 32, lanes(m)])

    rims = [pick(BODY + e) for e in range(RIM)]
    rims = [jnp.concatenate(halves(rims[0], rims[1]), axis=0), jnp.concatenate([rims[2], pltpu.roll(rims[2], 64, 1)], axis=0)]
    sigma = jnp.concatenate([sig_ref[0:1, :], sig_ref[1:2, :]] * NF, axis=1)
    time0 = apply(jnp.concatenate(gather(0) + rims, axis=1))
    scatter(0, time0)
    pair, single = [time0[:, lanes(count + m)] for m in range(2)]
    for e, value in enumerate(halves(pair[:32], pair[32:]) + halves(single[:32], single[32:])[:1]):
        put(BODY + e, value)
    psi1 = jnp.concatenate(gather(1), axis=1) - sigma * time0[:, :128 * count]
    scatter(1, apply(psi1))


def plane(ref, what, t, f, q):
    return jnp.concatenate([ref[pl.ds(q * GRP + row_of(t, what, f, h), 8, stride=ROWS), :] for h in range(HB)], axis=0)


def last_kernel(rad_ref, w_ref, u_ref, w_edge_ref, w_halo_ref, jr_ref, jc_ref, jrb_ref, jce_ref, dis_ref,
                step_ref, src_ref, ids_ref, pick_ref, label_ref, sd_ref, out_hbm, sens_ref, psi1_ref, psi_ref, edge_ref, halo_ref, rim_ref, turn_ref, pad_ref, sem):
    rad = rad_ref[0]
    clear_pad(pad_ref)
    for e in range(RIM):
        rim_ref[32 * e:32 * e + 32] = u_ref[pl.ds(BODY + e, 32, stride=ROWS), :]
    rims = halves(rim_ref[0:48], rim_ref[48:96])
    for t in range(TD):
        for m in range(2):
            at = (2 * t + m) * NF
            for q in range(LT):
                side = q // 2
                here = slice(20 * side + at, 20 * side + at + NF)
                sigma = w_halo_ref[40 + 2 * side + m:41 + 2 * side + m, lanes(q % 2)]
                halo_ref[here, lanes(q % 2)] = (
                    w_halo_ref[here, lanes(q % 2)] - sigma * rims[t][10 * q + NF * m:10 * q + NF * m + NF])
        edge_ref[t] = w_edge_ref[t] - w_edge_ref[TD] * edge_of(rims[t][40:43], turn_ref)
    copies = []
    for t in range(TD):
        fix = corrections(rad, edge_ref, halo_ref, jrb_ref, jce_ref, dis_ref, t)
        for f in range(NF):
            for q in range(LT):
                psi1_ref[t * NF + f, :, lanes(q)] = (
                    w_ref[t * NF + f, :, lanes(q)] - step_ref[:, lanes(q)] * plane(u_ref, 0, t, f, q))
        for q in range(LT):
            cell = lambda f, qq: psi1_ref[t * NF + f, :, lanes(qq)]
            jr = lambda i, j: jr_ref[t, i, j, :, lanes(q)]
            jc = lambda i, j: jc_ref[t, i, j, :, lanes(q)]
            res = interior(cell, pad_ref, jr, jc, dis_ref[:, lanes(q)], q)
            sigma = step_ref[:, lanes(q)]
            for f in range(NF):
                psi_ref[t * NF + f, :, lanes(q)] = cell(f, q) - sigma * (
                    res[f] + fix(f, q) + plane(u_ref, 1, t, f, q) - src_ref[t * NF + f, :, lanes(q)])
        tf = pl.ds(t * NF, NF)
        copies.append(pltpu.make_async_copy(psi_ref.at[tf], out_hbm.at[tf], sem.at[t]))
        copies[t].start()
    pick = pick_ref[...]
    mask = (lax.broadcasted_iota(jnp.int32, (CR, NODES), 0) == ids_ref[1:2]).astype(F32)
    acc = [jnp.zeros((CR, NODES), F32) for _ in range(3)]
    weights = [sd_ref[m].astype(F32) for m in range(3 * NF)]
    size = TD * NF * CR
    whole = psi_ref[...].reshape(size, CT)
    got = jnp.dot(jnp.concatenate(split(whole), axis=0), pick, preferred_element_type=F32)
    got = got[:size] + got[size:2 * size] + got[2 * size:]
    for t in range(TD):
        value = got[t * NF * CR:(t + 1) * NF * CR]
        for f in range(NF):
            here = value[f * CR:(f + 1) * CR]
            for k in range(3):
                acc[k] = acc[k] + here * weights[3 * f + k][t:t + 1]
    owner = ids_ref[2:3]
    parts = []
    for k in range(3):
        kept = acc[k] * mask
        for s in range(2):
            parts.append(kept * (owner == s).astype(F32))
    stack = jnp.concatenate(parts, axis=0)
    label = label_ref[...]
    dims = (((1,), (1,)), ((), ()))
    total = lax.dot_general(jnp.concatenate(split(stack), axis=0), label, dims, preferred_element_type=F32)
    count = stack.shape[0]
    total = total[:count] + total[count:2 * count] + total[2 * count:]
    lane = lax.broadcasted_iota(jnp.int32, (1, 128), 1)
    line = []
    for s in range(2):
        full = jnp.zeros((1, 128), F32)
        for k in range(3):
            at = (k * 2 + s) * CR
            part = jnp.sum(total[at:at + CR], axis=0, keepdims=True)
            full = jnp.where(lane // VAR_DEV == k, part, full)
        line.append(full)
    peer = lax.broadcasted_iota(jnp.int32, (128, 128), 0)
    sens_ref[...] = jnp.where((peer // 2) % 2 == 0, line[0], line[1])
    for copy in copies:
        copy.wait()


VM, SM, HM = pltpu.VMEM, pltpu.SMEM, pltpu.HBM


def call(kernel, ins, outs, scratch=(), micros=1):
    return pl.pallas_call(
        kernel,
        out_shape=[shape for shape, _ in outs],
        in_specs=[pl.BlockSpec(memory_space=space) for space in ins],
        out_specs=[pl.BlockSpec(memory_space=space) for _, space in outs],
        scratch_shapes=list(scratch),
        cost_estimate=pl.CostEstimate(flops=0, bytes_accessed=int(micros * 3.0e6), transcendentals=0),
        compiler_params=pltpu.CompilerParams(vmem_limit_bytes=24 * 1024 * 1024),
    )


def f32(*shape):
    return jax.ShapeDtypeStruct(shape, F32)


def swap_halos(edge, halo):
    halo = lax.ppermute(halo, "rad", SWAP)
    edge = lax.ppermute(edge, "span", SWAP)
    return edge, halo


def body(adjoint_start, jac_rad, jac_circ, dissip, pseudo_step, source, node_cell, node_owner, node_local, shape_deriv):
    me = lax.axis_index("inst").astype(jnp.int32).reshape(1)
    rad = lax.axis_index("rad").astype(jnp.int32).reshape(1)
    span = lax.axis_index("span").astype(jnp.int32).reshape(1)
    n = TD * NF
    psi0 = adjoint_start.reshape(n, CR, CT)
    src = source.reshape(n, CR, CT)
    full = f32(n, CR, CT)
    line = (1, NODES)
    flat = f32(CR, CT)
    dma = pltpu.SemaphoreType.DMA
    pad = VM((NF * 32, 128), F32)
    held = [pltpu.with_memory_space_constraint(a, pltpu.HBM) for a in (
        dissip, pseudo_step, node_cell.reshape(line), node_owner.reshape(line), node_local.reshape(line), psi0, src, jac_rad, jac_circ)]
    edge0, halo0 = call(
        edge_kernel, [SM, HM], [(f32(TD, CR, 128), VM), (f32(40, HALF), VM)],
        [VM((n, 8, CT), F32), VM((n, CR, 128), F32), VM((n, CR, 128), F32), dma((3,))])(rad, held[5])
    edge0, halo0 = swap_halos(edge0, halo0)
    part, psi, jrb, jce, dis, step = call(
        first_kernel, [SM, SM] + [HM] * 6,
        [(full, VM), (full, VM), (f32(n, NF, CT), VM), (jax.ShapeDtypeStruct((n, NF, CR, 128), BF), VM), (flat, VM), (flat, VM)],
        [VM((n, CR, CT), F32), VM(jac_rad.shape, BF), VM(jac_circ.shape, BF), pad, dma((TD, 4)), dma((2,))],
        micros=3)(rad, span, held[0], held[1], *held[5:])
    rim = VM((96, 128), F32)
    swapped = [(f32(TD + 1, CR, 128), VM), (f32(48, HALF), VM)]
    x, w, w_edge, w_halo = call(
        send_kernel, [SM, SM] + [VM] * 8 + [HM] * 3, [(f32(32 * ROWS, 128), HM), (full, VM)] + swapped,
        [rim, VM((32 * ROWS, 128), F32), VM((n, CR, CT), F32), VM(jac_rad.shape, BF), VM(jac_circ.shape, BF), pad, VM((NF, CR, CT), F32),
         dma((LT,)), dma((3,))])(
        rad, span, psi, part, edge0, halo0, jrb, jce, dis, step, *held[6:])
    w_edge, w_halo = swap_halos(w_edge, w_halo)
    y = lax.all_to_all(x.reshape(32 * ROWS, 1, 128), "inst", 0, 0, tiled=True).reshape(32 * ROWS, 128)
    bf16 = lambda *shape: (jax.ShapeDtypeStruct(shape, BF), VM)
    pick, label, ids, sig = call(
        label_kernel, [SM] + [HM] * 3 + [VM],
        [bf16(CT, NODES), bf16(128, NODES), (jax.ShapeDtypeStruct((8, NODES), jnp.int32), VM), (f32(2, 128), VM)],
        [VM(line, jnp.int32)] * 3 + [dma((3,))])(me, *held[2:5], step)
    v, w_edge, w_halo = call(
        time_kernel, [VM] * 5 + [pl.ANY] * 2, [(f32(32 * ROWS, 128), VM)] + swapped)(
        jnp.asarray(spectral_blocks()), sig, y, w_edge, w_halo, pick, label)
    u = lax.all_to_all(v.reshape(32 * ROWS, 1, 128), "inst", 0, 0, tiled=True).reshape(32 * ROWS, 128)
    psi2, parts = call(
        last_kernel, [SM] + [VM] * 15, [(full, HM), (f32(128, 128), VM)],
        [VM((n, CR, CT), F32), VM((n, CR, CT), F32), VM((TD, CR, 128), F32), VM((40, HALF), F32), rim, VM((24, 128), F32), pad, dma((TD,))])(
        rad, w, u, w_edge, w_halo, jac_rad, jac_circ, jrb, jce, dis, step, src, ids, pick, label,
        shape_deriv.transpose(1, 2, 0, 3).reshape(3 * NF, TD, NODES))
    got = lax.all_to_all(parts, ALL, 0, 0, tiled=True)
    sens, = call(total_kernel, [VM], [(f32(3, VAR_DEV), VM)])(got)
    return psi2.reshape(TD, NF, CR, CT), sens


def solution(mesh):
    in_specs = (
        P("inst", None, "rad", "span"),
        P("inst", None, None, "rad", "span"),
        P("inst", None, None, "rad", "span"),
        P("rad", "span"),
        P("rad", "span"),
        P("inst", None, "rad", "span"),
        P(("span", "rad")),
        P(("span", "rad"), None),
        P(("span", "rad")),
        P("inst", None, None, ("span", "rad")),
    )
    out_specs = (P("inst", None, "rad", "span"), P(None, "span"))
    return jax.shard_map(body, mesh=mesh, in_specs=in_specs, out_specs=out_specs, check_vma=False)
```

```python
import jax
import jax.numpy as jnp
import numpy as np
from jax import lax
from jax.experimental import pallas as pl
from jax.experimental.pallas import tpu as pltpu
from jax.sharding import PartitionSpec as P

NT = 64
TD = 2
NF = 5
CR = 16
CT = 512
LT = 4
HB = 2
BODY = 40
RIM = 3
ROWS = BODY + RIM
HALF = 256
GRP = 8 * ROWS
NODES = 1024
VAR_DEV = 32
EPS4 = 0.0625
F32 = jnp.float32
BF = jnp.bfloat16
SWAP = [(0, 1), (1, 0)]
ALL = ("inst", "span", "rad")


def spectral_blocks():
    index = np.arange(NT)
    diff = index[:, None] - index[None, :]
    safe = np.where(diff == 0, 1, diff)
    table = np.where(diff == 0, 0.0, 0.5 * np.where(diff % 2 == 0, 1.0, -1.0) / np.tan(np.pi * safe / NT))
    order = np.concatenate([index[0::2], index[1::2]])
    apply = table.T[order][:, order].astype(np.float32)
    pieces = []
    for _ in range(3):
        pieces.append(apply.astype(BF))
        apply = apply - pieces[-1].astype(np.float32)
    high, mid, _ = pieces
    return np.concatenate([high, high, mid, mid, high], axis=1)


def split(x):
    pieces = []
    for _ in range(3):
        pieces.append(x.astype(BF))
        x = x - pieces[-1].astype(F32)
    return pieces


def pair_up(x):
    high, mid, low = split(x)
    return jnp.concatenate([high, mid, high, mid, low], axis=0)


def row_of(t, what, f, h):
    return ((t * 2 + what) * NF + f) * HB + h


def lanes(q):
    return slice(128 * q, 128 * q + 128)


def interior(cell, pad_ref, jr, jc, dis, q):
    lane = lax.broadcasted_iota(jnp.int32, (CR, 128), 1)
    none = jnp.zeros((CR, 128), F32)
    d_rad, d_circ, fourth = [], [], []
    for f in range(NF):
        mid = cell(f, q)
        left = none if q == 0 else cell(f, q - 1)
        right = none if q == LT - 1 else cell(f, q + 1)
        m1 = jnp.where(lane < 1, pltpu.roll(left, 1, 1), pltpu.roll(mid, 1, 1))
        m2 = jnp.where(lane < 2, pltpu.roll(left, 2, 1), pltpu.roll(mid, 2, 1))
        p1 = jnp.where(lane >= 127, pltpu.roll(right, 127, 1), pltpu.roll(mid, 127, 1))
        p2 = jnp.where(lane >= 126, pltpu.roll(right, 126, 1), pltpu.roll(mid, 126, 1))
        base = f * 32
        pad_ref[base + 8:base + 24, :] = mid
        rm2 = pad_ref[base + 6:base + 22, :]
        rm1 = pad_ref[base + 7:base + 23, :]
        rp1 = pad_ref[base + 9:base + 25, :]
        rp2 = pad_ref[base + 10:base + 26, :]
        d_circ.append(0.5 * (m1 - p1))
        d_rad.append(0.5 * (rm1 - rp1))
        fourth.append((m2 + p2) + (rm2 + rp2) - 4.0 * ((m1 + p1) + (rm1 + rp1)) + 12.0 * mid)
    out = []
    for j in range(NF):
        acc = (EPS4 * dis) * fourth[j]
        for i in range(NF):
            acc = acc + jr(i, j).astype(F32) * d_rad[i]
            acc = acc + jc(i, j).astype(F32) * d_circ[i]
        out.append(acc)
    return out


def clear_pad(pad_ref):
    pad_ref[...] = jnp.zeros(pad_ref.shape, F32)


def halo_rows(ref, at, count):
    return jnp.concatenate([ref[at:at + count, :], ref[20 + at:20 + at + count, :]], axis=1)


def corrections(rad, edge_ref, halo_ref, jrb_ref, jce_ref, dis_ref, t):
    lane = lax.broadcasted_iota(jnp.int32, (CR, 128), 1)
    diff, fourth = [], []
    edge = edge_ref[t]
    for f in range(NF):
        turn = lambda by: pltpu.roll(edge, (by - 4 * f) % 128, 1)
        m1 = jnp.where(lane < 1, turn(1), 0.0)
        m2 = jnp.where(lane < 2, turn(2), 0.0)
        p1 = jnp.where(lane >= 127, turn(-1), 0.0)
        p2 = jnp.where(lane >= 126, turn(-2), 0.0)
        diff.append(0.5 * (m1 - p1))
        fourth.append(m2 + p2 - 4.0 * (m1 + p1))
    dis_edge = EPS4 * jnp.where(lane < 64, dis_ref[:, lanes(0)], dis_ref[:, lanes(LT - 1)])
    circ = []
    for j in range(NF):
        acc = dis_edge * fourth[j]
        for i in range(NF):
            acc = acc + jce_ref[t * NF + i, j].astype(F32) * diff[i]
        circ.append(acc)
    near_row = jnp.where(rad == 0, CR - 1, 0)
    next_row = jnp.where(rad == 0, CR - 2, 1)
    sign = jnp.where(rad == 0, -0.5, 0.5)
    first, second = [halo_rows(halo_ref, (2 * t + m) * NF, NF) for m in range(2)]
    near = jnp.where(rad == 0, first, second)
    far = jnp.where(rad == 0, second, first)
    dis_near = EPS4 * dis_ref[pl.ds(near_row, 1), :]
    dis_next = EPS4 * dis_ref[pl.ds(next_row, 1), :]
    row_a = dis_near * (far - 4.0 * near)
    for i in range(NF):
        row_a = row_a + jrb_ref[t * NF + i] * (sign * near[i:i + 1])
    row_b = dis_next * near
    riota = lax.broadcasted_iota(jnp.int32, (CR, 128), 0)

    def fix(f, q):
        out = jnp.where(riota == near_row, row_a[f:f + 1, lanes(q)], 0.0)
        out = jnp.where(riota == next_row, row_b[f:f + 1, lanes(q)], out)
        if q == 0:
            out = out + jnp.where(lane < 64, circ[f], 0.0)
        if q == LT - 1:
            out = out + jnp.where(lane >= 64, circ[f], 0.0)
        return out

    return fix


def interior_pass(t, psi_ref, src_ref, jr_ref, jc_ref, dis_ref, step_ref, pad_ref, part_ref, first=0):
    for q in range(LT):
        cell = lambda f, qq: psi_ref[t * NF + f, :, lanes(qq)]
        jr = lambda i, j: jr_ref[t, i, j, :, lanes(q)]
        jc = lambda i, j: jc_ref[t, i, j, :, lanes(q)]
        res = interior(cell, pad_ref, jr, jc, dis_ref[:, lanes(q)], q)
        sigma = step_ref[:, lanes(q)]
        for f in range(NF):
            part_ref[t * NF + f - first, :, lanes(q)] = cell(f, q) - sigma * (res[f] - src_ref[t * NF + f, :, lanes(q)])


def edge_kernel(rad_ref, psi_hbm, edge_ref, halo_ref, rows_ref, left_ref, right_ref, sem):
    rad = rad_ref[0]
    start = pl.multiple_of(8 * (1 - rad), 8)
    copies = [
        pltpu.make_async_copy(psi_hbm.at[:, pl.ds(start, 8), :], rows_ref, sem.at[0]),
        pltpu.make_async_copy(psi_hbm.at[:, :, pl.ds(0, 128)], left_ref, sem.at[1]),
        pltpu.make_async_copy(psi_hbm.at[:, :, pl.ds(CT - 128, 128)], right_ref, sem.at[2]),
    ]
    for copy in copies:
        copy.start()
    copies[0].wait()
    put_halo(halo_ref, lambda tf: rows_ref[tf], rad)
    copies[1].wait()
    copies[2].wait()
    put_edge(edge_ref, lambda tf: (left_ref[tf], right_ref[tf]))


def pack_edge(ends):
    lane = lax.broadcasted_iota(jnp.int32, (CR, 128), 1)
    packed = None
    for f in range(NF):
        both = jnp.where(lane < 64, ends[f][0], ends[f][1])
        if f == 0:
            packed = both
        else:
            packed = jnp.where((lane >= 4 * f - 2) & (lane < 4 * f + 2), pltpu.roll(both, 4 * f, 1), packed)
    return packed


def put_edge(edge_ref, ends):
    for t in range(TD):
        edge_ref[t] = pack_edge([ends(t * NF + f) for f in range(NF)])


def put_halo(halo_ref, tile, rad):
    for t in range(TD):
        for f in range(NF):
            rows = tile(t * NF + f)
            pair = jnp.where(rad == 0, rows[6:8], rows[0:2])
            for m in range(2):
                put_row(halo_ref, (2 * t + m) * NF + f, pair[m:m + 1])


def put_row(halo_ref, at, row):
    halo_ref[at:at + 1] = row[:, :HALF]
    halo_ref[20 + at:21 + at] = row[:, HALF:]


def rim_of(tile, edge):
    lane = lax.broadcasted_iota(jnp.int32, (3, 128), 1)
    turned = pltpu.roll(edge, 2, 1)
    turned = jnp.concatenate([turned, jnp.zeros((8, 128), F32)], axis=0)
    dense = jnp.zeros((3, 128), F32)
    for g in range(6):
        part = turned[3 * g:3 * g + 3]
        part = pltpu.roll(part, 20 * g, 1) if g else part
        dense = jnp.where((lane >= 20 * g) & (lane < 20 * g + 20), part, dense)
    return jnp.concatenate([tile(q) for q in range(LT)] + [dense, jnp.zeros((5, 128), F32)], axis=0)


def edge_of(dense, edge_ref):
    for g in range(6):
        edge_ref[3 * g:3 * g + 3] = pltpu.roll(dense, 128 - 20 * g, 1) if g else dense
    return pltpu.roll(edge_ref[0:CR], 126, 1)


def halves(a, b):
    lane = lax.broadcasted_iota(jnp.int32, a.shape, 1)
    return jnp.where(lane < 64, a, pltpu.roll(b, 64, 1)), jnp.where(lane < 64, pltpu.roll(a, 64, 1), b)


def first_kernel(rad_ref, span_ref, dis_hbm, step_hbm, psi_hbm, src_hbm, jr_hbm, jc_hbm,
                 part_ref, psi_ref, jrb_ref, jce_ref, dis_ref, step_ref, src_ref, jr_ref, jc_ref, pad_ref, sem, sem_small):
    rad = rad_ref[0]
    small = [pltpu.make_async_copy(a, b, sem_small.at[i]) for i, (a, b) in enumerate([
        (dis_hbm, dis_ref), (step_hbm, step_ref)])]
    copies = []
    for t in range(TD):
        tf = pl.ds(t * NF, NF)
        copies.append([
            pltpu.make_async_copy(psi_hbm.at[tf], psi_ref.at[tf], sem.at[t, 0]),
            pltpu.make_async_copy(jr_hbm.at[t], jr_ref.at[t], sem.at[t, 1]),
            pltpu.make_async_copy(jc_hbm.at[t], jc_ref.at[t], sem.at[t, 2]),
            pltpu.make_async_copy(src_hbm.at[tf], src_ref.at[tf], sem.at[t, 3]),
        ])
    for copy in small + copies[0] + copies[1]:
        copy.start()
    clear_pad(pad_ref)
    lane = lax.broadcasted_iota(jnp.int32, (CR, 128), 1)
    for copy in small:
        copy.wait()
    for t in range(TD):
        for copy in copies[t]:
            copy.wait()

        @pl.when((span_ref[0] == 1) | (t == 0))
        def _():
            interior_pass(t, psi_ref, src_ref, jr_ref, jc_ref, dis_ref, step_ref, pad_ref, part_ref)

        for i in range(NF):
            for j in range(NF):
                whole = jr_ref[t, i, j].astype(F32)
                jrb_ref[t * NF + i, j:j + 1] = jnp.where(rad == 0, whole[CR - 1:CR], whole[0:1])
                jce_ref[t * NF + i, j] = jnp.where(
                    lane < 64, jc_ref[t, i, j, :, lanes(0)].astype(F32), jc_ref[t, i, j, :, lanes(LT - 1)].astype(F32)).astype(BF)


def send_kernel(rad_ref, span_ref, psi_ref, part_ref, edge_ref, halo_ref, jrb_ref, jce_ref, dis_ref, step_ref, src_hbm, jr_hbm, jc_hbm,
                x_hbm, w_ref, w_edge_ref, w_halo_ref, rim_ref, x_ref, src_ref, jr_ref, jc_ref, pad_ref, late_ref, sem, sem_in):
    rad = rad_ref[0]


    @pl.when(span_ref[0] != 0)
    def _():
        late_ref[...] = part_ref[(TD - 1) * NF:]

    @pl.when(span_ref[0] == 0)
    def _():
        last = pl.ds((TD - 1) * NF, NF)
        loads = [pltpu.make_async_copy(a, b, sem_in.at[i]) for i, (a, b) in enumerate(
            [(src_hbm.at[last], src_ref.at[last]), (jr_hbm.at[TD - 1], jr_ref.at[TD - 1]), (jc_hbm.at[TD - 1], jc_ref.at[TD - 1])])]
        for load in loads:
            load.start()
        clear_pad(pad_ref)
        for load in loads:
            load.wait()
        interior_pass(TD - 1, psi_ref, src_ref, jr_ref, jc_ref, dis_ref, step_ref, pad_ref, late_ref, (TD - 1) * NF)

    fixes = [corrections(rad, edge_ref, halo_ref, jrb_ref, jce_ref, dis_ref, t) for t in range(TD)]
    rims = [rim_of(lambda q: halo_ref[20 * (q // 2) + 10 * t:20 * (q // 2) + 10 * t + 10, lanes(q % 2)], edge_ref[t])
            for t in range(TD)]
    low, high = halves(*rims)
    rim_ref[0:48] = low
    rim_ref[48:96] = high
    for e in range(RIM):
        x_ref[pl.ds(BODY + e, 32, stride=ROWS), :] = rim_ref[32 * e:32 * e + 32]
    copies = []
    for q in range(LT):
        for t in range(TD):
            for f in range(NF):
                mid = psi_ref[t * NF + f, :, lanes(q)]
                before = part_ref[f, :, lanes(q)] if t < TD - 1 else late_ref[f, :, lanes(q)]
                w = before - step_ref[:, lanes(q)] * fixes[t](f, q)
                w_ref[t * NF + f, :, lanes(q)] = w
                for h in range(HB):
                    x_ref[pl.ds(q * GRP + row_of(t, 0, f, h), 8, stride=ROWS), :] = mid[8 * h:8 * h + 8]
                    x_ref[pl.ds(q * GRP + row_of(t, 1, f, h), 8, stride=ROWS), :] = w[8 * h:8 * h + 8]
        span = pl.ds(q * GRP, GRP)
        copies.append(pltpu.make_async_copy(x_ref.at[span], x_hbm.at[span], sem.at[q]))
        copies[q].start()
    put_edge(w_edge_ref, lambda tf: (w_ref[tf, :, lanes(0)], w_ref[tf, :, lanes(LT - 1)]))
    start = pl.multiple_of(8 * (1 - rad), 8)
    put_halo(w_halo_ref, lambda tf: w_ref[tf, pl.ds(start, 8), :], rad)
    w_edge_ref[TD] = pack_edge([(step_ref[:, lanes(0)], step_ref[:, lanes(LT - 1)])] * NF)
    sigma = jnp.where(rad == 0, step_ref[CR - 2:CR], step_ref[0:2])
    w_halo_ref[40:42] = sigma[:, :HALF]
    w_halo_ref[42:44] = sigma[:, HALF:]
    w_halo_ref[44:48] = jnp.zeros((4, HALF), F32)
    for copy in copies:
        copy.wait()


def label_kernel(me_ref, cell_hbm, owner_hbm, local_hbm, step_ref, pick_ref, label_ref, ids_ref, sig_ref, cell_ref, owner_ref,
                 local_ref, sem):
    loads = [pltpu.make_async_copy(a, b, sem.at[i]) for i, (a, b) in enumerate(
        [(cell_hbm, cell_ref), (owner_hbm, owner_ref), (local_hbm, local_ref)])]
    for load in loads:
        load.start()
    for load in loads:
        load.wait()
    ids_ref[0:1] = cell_ref[...] % CT
    ids_ref[1:2] = cell_ref[...] // CT
    ids_ref[2:3] = owner_ref[...]
    ids_ref[3:4] = local_ref[...]
    me = me_ref[0]
    sig = jnp.zeros((2, 128), F32)
    for p in range(8):
        for q in range(LT):
            here = jnp.concatenate([step_ref[p:p + 1, lanes(q)], step_ref[p + 8:p + 9, lanes(q)]], axis=0)
            sig = jnp.where(me == 8 * q + p, here, sig)
    sig_ref[...] = sig
    pick_ref[...] = (lax.broadcasted_iota(jnp.int32, (CT, NODES), 0) == ids_ref[0:1]).astype(F32).astype(BF)
    label_ref[...] = (lax.broadcasted_iota(jnp.int32, (128, NODES), 0) % VAR_DEV == ids_ref[3:4]).astype(F32).astype(BF)


def total_kernel(got_ref, sens_ref):
    line = jnp.sum(got_ref[...], axis=0, keepdims=True)
    for k in range(3):
        sens_ref[k:k + 1, :] = pltpu.roll(line, (128 - VAR_DEV * k) % 128, 1)[:, :VAR_DEV]


def time_kernel(table_ref, sig_ref, y_ref, edge_ref, halo_ref, pick_ref, label_ref, v_ref, edge_out_ref, halo_out_ref):
    edge_out_ref[...] = edge_ref[...]
    halo_out_ref[...] = halo_ref[...]
    table = table_ref[...]

    def apply(x):
        return jnp.dot(table, pair_up(x), preferred_element_type=F32)

    count = 2 * NF

    def pick(at):
        return y_ref[pl.ds(at, 32, stride=ROWS), :]

    def put(at, value):
        v_ref[pl.ds(at, 32, stride=ROWS), :] = value

    def row(what, m, t):
        return (t * 2 + what) * count + m

    def gather(what):
        return [jnp.concatenate([pick(row(what, m, t)) for t in range(TD)], axis=0) for m in range(count)]

    def scatter(what, value):
        for m in range(count):
            for t in range(TD):
                put(row(what, m, t), value[32 * t:32 * t + 32, lanes(m)])

    rims = [pick(BODY + e) for e in range(RIM)]
    rims = [jnp.concatenate(halves(rims[0], rims[1]), axis=0), jnp.concatenate([rims[2], pltpu.roll(rims[2], 64, 1)], axis=0)]
    sigma = jnp.concatenate([sig_ref[0:1, :], sig_ref[1:2, :]] * NF, axis=1)
    time0 = apply(jnp.concatenate(gather(0) + rims, axis=1))
    scatter(0, time0)
    pair, single = [time0[:, lanes(count + m)] for m in range(2)]
    for e, value in enumerate(halves(pair[:32], pair[32:]) + halves(single[:32], single[32:])[:1]):
        put(BODY + e, value)
    psi1 = jnp.concatenate(gather(1), axis=1) - sigma * time0[:, :128 * count]
    scatter(1, apply(psi1))


def plane(ref, what, t, f, q):
    return jnp.concatenate([ref[pl.ds(q * GRP + row_of(t, what, f, h), 8, stride=ROWS), :] for h in range(HB)], axis=0)


def last_kernel(rad_ref, w_ref, u_ref, w_edge_ref, w_halo_ref, jr_ref, jc_ref, jrb_ref, jce_ref, dis_ref,
                step_ref, src_ref, ids_ref, pick_ref, label_ref, sd_ref, out_hbm, sens_ref, psi1_ref, psi_ref, edge_ref, halo_ref, rim_ref, turn_ref, pad_ref, sem):
    rad = rad_ref[0]
    clear_pad(pad_ref)
    for e in range(RIM):
        rim_ref[32 * e:32 * e + 32] = u_ref[pl.ds(BODY + e, 32, stride=ROWS), :]
    rims = halves(rim_ref[0:48], rim_ref[48:96])
    for t in range(TD):
        for m in range(2):
            at = (2 * t + m) * NF
            for q in range(LT):
                side = q // 2
                here = slice(20 * side + at, 20 * side + at + NF)
                sigma = w_halo_ref[40 + 2 * side + m:41 + 2 * side + m, lanes(q % 2)]
                halo_ref[here, lanes(q % 2)] = (
                    w_halo_ref[here, lanes(q % 2)] - sigma * rims[t][10 * q + NF * m:10 * q + NF * m + NF])
        edge_ref[t] = w_edge_ref[t] - w_edge_ref[TD] * edge_of(rims[t][40:43], turn_ref)
    copies = []
    for t in range(TD):
        fix = corrections(rad, edge_ref, halo_ref, jrb_ref, jce_ref, dis_ref, t)
        for f in range(NF):
            for q in range(LT):
                psi1_ref[t * NF + f, :, lanes(q)] = (
                    w_ref[t * NF + f, :, lanes(q)] - step_ref[:, lanes(q)] * plane(u_ref, 0, t, f, q))
        for q in range(LT):
            cell = lambda f, qq: psi1_ref[t * NF + f, :, lanes(qq)]
            jr = lambda i, j: jr_ref[t, i, j, :, lanes(q)]
            jc = lambda i, j: jc_ref[t, i, j, :, lanes(q)]
            res = interior(cell, pad_ref, jr, jc, dis_ref[:, lanes(q)], q)
            sigma = step_ref[:, lanes(q)]
            for f in range(NF):
                psi_ref[t * NF + f, :, lanes(q)] = cell(f, q) - sigma * (
                    res[f] + fix(f, q) + plane(u_ref, 1, t, f, q) - src_ref[t * NF + f, :, lanes(q)])
        tf = pl.ds(t * NF, NF)
        copies.append(pltpu.make_async_copy(psi_ref.at[tf], out_hbm.at[tf], sem.at[t]))
        copies[t].start()
    pick = pick_ref[...]
    mask = (lax.broadcasted_iota(jnp.int32, (CR, NODES), 0) == ids_ref[1:2]).astype(F32)
    acc = [jnp.zeros((CR, NODES), F32) for _ in range(3)]
    weights = [sd_ref[m].astype(F32) for m in range(3 * NF)]
    size = TD * NF * CR
    whole = psi_ref[...].reshape(size, CT)
    got = jnp.dot(jnp.concatenate(split(whole), axis=0), pick, preferred_element_type=F32)
    got = got[:size] + got[size:2 * size] + got[2 * size:]
    for t in range(TD):
        value = got[t * NF * CR:(t + 1) * NF * CR]
        for f in range(NF):
            here = value[f * CR:(f + 1) * CR]
            for k in range(3):
                acc[k] = acc[k] + here * weights[3 * f + k][t:t + 1]
    owner = ids_ref[2:3]
    parts = []
    for k in range(3):
        kept = acc[k] * mask
        for s in range(2):
            parts.append(kept * (owner == s).astype(F32))
    stack = jnp.concatenate(parts, axis=0)
    label = label_ref[...]
    dims = (((1,), (1,)), ((), ()))
    total = lax.dot_general(jnp.concatenate(split(stack), axis=0), label, dims, preferred_element_type=F32)
    count = stack.shape[0]
    total = total[:count] + total[count:2 * count] + total[2 * count:]
    lane = lax.broadcasted_iota(jnp.int32, (1, 128), 1)
    line = []
    for s in range(2):
        full = jnp.zeros((1, 128), F32)
        for k in range(3):
            at = (k * 2 + s) * CR
            part = jnp.sum(total[at:at + CR], axis=0, keepdims=True)
            full = jnp.where(lane // VAR_DEV == k, part, full)
        line.append(full)
    peer = lax.broadcasted_iota(jnp.int32, (128, 128), 0)
    sens_ref[...] = jnp.where((peer // 2) % 2 == 0, line[0], line[1])
    for copy in copies:
        copy.wait()


VM, SM, HM = pltpu.VMEM, pltpu.SMEM, pltpu.HBM


def call(kernel, ins, outs, scratch=(), micros=1):
    return pl.pallas_call(
        kernel,
        out_shape=[shape for shape, _ in outs],
        in_specs=[pl.BlockSpec(memory_space=space) for space in ins],
        out_specs=[pl.BlockSpec(memory_space=space) for _, space in outs],
        scratch_shapes=list(scratch),
        cost_estimate=pl.CostEstimate(flops=0, bytes_accessed=int(micros * 3.0e6), transcendentals=0),
        compiler_params=pltpu.CompilerParams(vmem_limit_bytes=24 * 1024 * 1024),
    )


def f32(*shape):
    return jax.ShapeDtypeStruct(shape, F32)


def swap_halos(edge, halo):
    halo = lax.ppermute(halo, "rad", SWAP)
    edge = lax.ppermute(edge, "span", SWAP)
    return edge, halo


def body(adjoint_start, jac_rad, jac_circ, dissip, pseudo_step, source, node_cell, node_owner, node_local, shape_deriv):
    me = lax.axis_index("inst").astype(jnp.int32).reshape(1)
    rad = lax.axis_index("rad").astype(jnp.int32).reshape(1)
    span = lax.axis_index("span").astype(jnp.int32).reshape(1)
    n = TD * NF
    psi0 = adjoint_start.reshape(n, CR, CT)
    src = source.reshape(n, CR, CT)
    full = f32(n, CR, CT)
    line = (1, NODES)
    flat = f32(CR, CT)
    dma = pltpu.SemaphoreType.DMA
    pad = VM((NF * 32, 128), F32)
    held = [pltpu.with_memory_space_constraint(a, pltpu.HBM) for a in (
        dissip, pseudo_step, node_cell.reshape(line), node_owner.reshape(line), node_local.reshape(line), psi0, src, jac_rad, jac_circ)]
    edge0, halo0 = call(
        edge_kernel, [SM, HM], [(f32(TD, CR, 128), VM), (f32(40, HALF), VM)],
        [VM((n, 8, CT), F32), VM((n, CR, 128), F32), VM((n, CR, 128), F32), dma((3,))])(rad, held[5])
    edge0, halo0 = swap_halos(edge0, halo0)
    part, psi, jrb, jce, dis, step = call(
        first_kernel, [SM, SM] + [HM] * 6,
        [(full, VM), (full, VM), (f32(n, NF, CT), VM), (jax.ShapeDtypeStruct((n, NF, CR, 128), BF), VM), (flat, VM), (flat, VM)],
        [VM((n, CR, CT), F32), VM(jac_rad.shape, BF), VM(jac_circ.shape, BF), pad, dma((TD, 4)), dma((2,))],
        micros=3)(rad, span, held[0], held[1], *held[5:])
    rim = VM((96, 128), F32)
    swapped = [(f32(TD + 1, CR, 128), VM), (f32(48, HALF), VM)]
    x, w, w_edge, w_halo = call(
        send_kernel, [SM, SM] + [VM] * 8 + [HM] * 3, [(f32(32 * ROWS, 128), HM), (full, VM)] + swapped,
        [rim, VM((32 * ROWS, 128), F32), VM((n, CR, CT), F32), VM(jac_rad.shape, BF), VM(jac_circ.shape, BF), pad, VM((NF, CR, CT), F32),
         dma((LT,)), dma((3,))])(
        rad, span, psi, part, edge0, halo0, jrb, jce, dis, step, *held[6:])
    w_edge, w_halo = swap_halos(w_edge, w_halo)
    y = lax.all_to_all(x.reshape(32 * ROWS, 1, 128), "inst", 0, 0, tiled=True).reshape(32 * ROWS, 128)
    bf16 = lambda *shape: (jax.ShapeDtypeStruct(shape, BF), VM)
    pick, label, ids, sig = call(
        label_kernel, [SM] + [HM] * 3 + [VM],
        [bf16(CT, NODES), bf16(128, NODES), (jax.ShapeDtypeStruct((8, NODES), jnp.int32), VM), (f32(2, 128), VM)],
        [VM(line, jnp.int32)] * 3 + [dma((3,))], micros=40)(me, *held[2:5], step)
    v, w_edge, w_halo = call(
        time_kernel, [VM] * 5 + [pl.ANY] * 2, [(f32(32 * ROWS, 128), VM)] + swapped)(
        jnp.asarray(spectral_blocks()), sig, y, w_edge, w_halo, pick, label)
    u = lax.all_to_all(v.reshape(32 * ROWS, 1, 128), "inst", 0, 0, tiled=True).reshape(32 * ROWS, 128)
    psi2, parts = call(
        last_kernel, [SM] + [VM] * 15, [(full, HM), (f32(128, 128), VM)],
        [VM((n, CR, CT), F32), VM((n, CR, CT), F32), VM((TD, CR, 128), F32), VM((40, HALF), F32), rim, VM((24, 128), F32), pad, dma((TD,))])(
        rad, w, u, w_edge, w_halo, jac_rad, jac_circ, jrb, jce, dis, step, src, ids, pick, label,
        shape_deriv.transpose(1, 2, 0, 3).reshape(3 * NF, TD, NODES))
    got = lax.all_to_all(parts, ALL, 0, 0, tiled=True)
    sens, = call(total_kernel, [VM], [(f32(3, VAR_DEV), VM)])(got)
    return psi2.reshape(TD, NF, CR, CT), sens


def solution(mesh):
    in_specs = (
        P("inst", None, "rad", "span"),
        P("inst", None, None, "rad", "span"),
        P("inst", None, None, "rad", "span"),
        P("rad", "span"),
        P("rad", "span"),
        P("inst", None, "rad", "span"),
        P(("span", "rad")),
        P(("span", "rad"), None),
        P(("span", "rad")),
        P("inst", None, None, ("span", "rad")),
    )
    out_specs = (P("inst", None, "rad", "span"), P(None, "span"))
    return jax.shard_map(body, mesh=mesh, in_specs=in_specs, out_specs=out_specs, check_vma=False)
```

```python
import jax
import jax.numpy as jnp
import numpy as np
from jax import lax
from jax.experimental import pallas as pl
from jax.experimental.pallas import tpu as pltpu
from jax.sharding import PartitionSpec as P

NT = 64
TD = 2
NF = 5
CR = 16
CT = 512
LT = 4
HB = 2
BODY = 40
RIM = 3
ROWS = BODY + RIM
HALF = 256
GRP = 8 * ROWS
NODES = 1024
VAR_DEV = 32
EPS4 = 0.0625
F32 = jnp.float32
BF = jnp.bfloat16
SWAP = [(0, 1), (1, 0)]
ALL = ("inst", "span", "rad")


def spectral_blocks():
    index = np.arange(NT)
    diff = index[:, None] - index[None, :]
    safe = np.where(diff == 0, 1, diff)
    table = np.where(diff == 0, 0.0, 0.5 * np.where(diff % 2 == 0, 1.0, -1.0) / np.tan(np.pi * safe / NT))
    order = np.concatenate([index[0::2], index[1::2]])
    apply = table.T[order][:, order].astype(np.float32)
    pieces = []
    for _ in range(3):
        pieces.append(apply.astype(BF))
        apply = apply - pieces[-1].astype(np.float32)
    high, mid, _ = pieces
    return np.concatenate([high, high, mid, mid, high], axis=1)


def split(x):
    pieces = []
    for _ in range(3):
        pieces.append(x.astype(BF))
        x = x - pieces[-1].astype(F32)
    return pieces


def pair_up(x):
    high, mid, low = split(x)
    return jnp.concatenate([high, mid, high, mid, low], axis=0)


def row_of(t, what, f, h):
    return ((t * 2 + what) * NF + f) * HB + h


def lanes(q):
    return slice(128 * q, 128 * q + 128)


def interior(cell, pad_ref, jr, jc, dis, q):
    lane = lax.broadcasted_iota(jnp.int32, (CR, 128), 1)
    none = jnp.zeros((CR, 128), F32)
    d_rad, d_circ, fourth = [], [], []
    for f in range(NF):
        mid = cell(f, q)
        left = none if q == 0 else cell(f, q - 1)
        right = none if q == LT - 1 else cell(f, q + 1)
        m1 = jnp.where(lane < 1, pltpu.roll(left, 1, 1), pltpu.roll(mid, 1, 1))
        m2 = jnp.where(lane < 2, pltpu.roll(left, 2, 1), pltpu.roll(mid, 2, 1))
        p1 = jnp.where(lane >= 127, pltpu.roll(right, 127, 1), pltpu.roll(mid, 127, 1))
        p2 = jnp.where(lane >= 126, pltpu.roll(right, 126, 1), pltpu.roll(mid, 126, 1))
        base = f * 32
        pad_ref[base + 8:base + 24, :] = mid
        rm2 = pad_ref[base + 6:base + 22, :]
        rm1 = pad_ref[base + 7:base + 23, :]
        rp1 = pad_ref[base + 9:base + 25, :]
        rp2 = pad_ref[base + 10:base + 26, :]
        d_circ.append(0.5 * (m1 - p1))
        d_rad.append(0.5 * (rm1 - rp1))
        fourth.append((m2 + p2) + (rm2 + rp2) - 4.0 * ((m1 + p1) + (rm1 + rp1)) + 12.0 * mid)
    out = []
    for j in range(NF):
        acc = (EPS4 * dis) * fourth[j]
        for i in range(NF):
            acc = acc + jr(i, j).astype(F32) * d_rad[i]
            acc = acc + jc(i, j).astype(F32) * d_circ[i]
        out.append(acc)
    return out


def clear_pad(pad_ref):
    pad_ref[...] = jnp.zeros(pad_ref.shape, F32)


def halo_rows(ref, at, count):
    return jnp.concatenate([ref[at:at + count, :], ref[20 + at:20 + at + count, :]], axis=1)


def corrections(rad, edge_ref, halo_ref, jrb_ref, jce_ref, dis_ref, t):
    lane = lax.broadcasted_iota(jnp.int32, (CR, 128), 1)
    diff, fourth = [], []
    edge = edge_ref[t]
    for f in range(NF):
        turn = lambda by: pltpu.roll(edge, (by - 4 * f) % 128, 1)
        m1 = jnp.where(lane < 1, turn(1), 0.0)
        m2 = jnp.where(lane < 2, turn(2), 0.0)
        p1 = jnp.where(lane >= 127, turn(-1), 0.0)
        p2 = jnp.where(lane >= 126, turn(-2), 0.0)
        diff.append(0.5 * (m1 - p1))
        fourth.append(m2 + p2 - 4.0 * (m1 + p1))
    dis_edge = EPS4 * jnp.where(lane < 64, dis_ref[:, lanes(0)], dis_ref[:, lanes(LT - 1)])
    circ = []
    for j in range(NF):
        acc = dis_edge * fourth[j]
        for i in range(NF):
            acc = acc + jce_ref[t * NF + i, j].astype(F32) * diff[i]
        circ.append(acc)
    near_row = jnp.where(rad == 0, CR - 1, 0)
    next_row = jnp.where(rad == 0, CR - 2, 1)
    sign = jnp.where(rad == 0, -0.5, 0.5)
    first, second = [halo_rows(halo_ref, (2 * t + m) * NF, NF) for m in range(2)]
    near = jnp.where(rad == 0, first, second)
    far = jnp.where(rad == 0, second, first)
    dis_near = EPS4 * dis_ref[pl.ds(near_row, 1), :]
    dis_next = EPS4 * dis_ref[pl.ds(next_row, 1), :]
    row_a = dis_near * (far - 4.0 * near)
    for i in range(NF):
        row_a = row_a + jrb_ref[t * NF + i] * (sign * near[i:i + 1])
    row_b = dis_next * near
    riota = lax.broadcasted_iota(jnp.int32, (CR, 128), 0)

    def fix(f, q):
        out = jnp.where(riota == near_row, row_a[f:f + 1, lanes(q)], 0.0)
        out = jnp.where(riota == next_row, row_b[f:f + 1, lanes(q)], out)
        if q == 0:
            out = out + jnp.where(lane < 64, circ[f], 0.0)
        if q == LT - 1:
            out = out + jnp.where(lane >= 64, circ[f], 0.0)
        return out

    return fix


def interior_pass(t, psi_ref, src_ref, jr_ref, jc_ref, dis_ref, step_ref, pad_ref, part_ref, first=0):
    for q in range(LT):
        cell = lambda f, qq: psi_ref[t * NF + f, :, lanes(qq)]
        jr = lambda i, j: jr_ref[t, i, j, :, lanes(q)]
        jc = lambda i, j: jc_ref[t, i, j, :, lanes(q)]
        res = interior(cell, pad_ref, jr, jc, dis_ref[:, lanes(q)], q)
        sigma = step_ref[:, lanes(q)]
        for f in range(NF):
            part_ref[t * NF + f - first, :, lanes(q)] = cell(f, q) - sigma * (res[f] - src_ref[t * NF + f, :, lanes(q)])


def edge_kernel(rad_ref, psi_hbm, edge_ref, halo_ref, rows_ref, left_ref, right_ref, sem):
    rad = rad_ref[0]
    start = pl.multiple_of(8 * (1 - rad), 8)
    copies = [
        pltpu.make_async_copy(psi_hbm.at[:, pl.ds(start, 8), :], rows_ref, sem.at[0]),
        pltpu.make_async_copy(psi_hbm.at[:, :, pl.ds(0, 128)], left_ref, sem.at[1]),
        pltpu.make_async_copy(psi_hbm.at[:, :, pl.ds(CT - 128, 128)], right_ref, sem.at[2]),
    ]
    for copy in copies:
        copy.start()
    copies[0].wait()
    put_halo(halo_ref, lambda tf: rows_ref[tf], rad)
    copies[1].wait()
    copies[2].wait()
    put_edge(edge_ref, lambda tf: (left_ref[tf], right_ref[tf]))


def pack_edge(ends):
    lane = lax.broadcasted_iota(jnp.int32, (CR, 128), 1)
    packed = None
    for f in range(NF):
        both = jnp.where(lane < 64, ends[f][0], ends[f][1])
        if f == 0:
            packed = both
        else:
            packed = jnp.where((lane >= 4 * f - 2) & (lane < 4 * f + 2), pltpu.roll(both, 4 * f, 1), packed)
    return packed


def put_edge(edge_ref, ends):
    for t in range(TD):
        edge_ref[t] = pack_edge([ends(t * NF + f) for f in range(NF)])


def put_halo(halo_ref, tile, rad):
    for t in range(TD):
        for f in range(NF):
            rows = tile(t * NF + f)
            pair = jnp.where(rad == 0, rows[6:8], rows[0:2])
            for m in range(2):
                put_row(halo_ref, (2 * t + m) * NF + f, pair[m:m + 1])


def put_row(halo_ref, at, row):
    halo_ref[at:at + 1] = row[:, :HALF]
    halo_ref[20 + at:21 + at] = row[:, HALF:]


def rim_of(tile, edge):
    lane = lax.broadcasted_iota(jnp.int32, (3, 128), 1)
    turned = pltpu.roll(edge, 2, 1)
    turned = jnp.concatenate([turned, jnp.zeros((8, 128), F32)], axis=0)
    dense = jnp.zeros((3, 128), F32)
    for g in range(6):
        part = turned[3 * g:3 * g + 3]
        part = pltpu.roll(part, 20 * g, 1) if g else part
        dense = jnp.where((lane >= 20 * g) & (lane < 20 * g + 20), part, dense)
    return jnp.concatenate([tile(q) for q in range(LT)] + [dense, jnp.zeros((5, 128), F32)], axis=0)


def edge_of(dense, edge_ref):
    for g in range(6):
        edge_ref[3 * g:3 * g + 3] = pltpu.roll(dense, 128 - 20 * g, 1) if g else dense
    return pltpu.roll(edge_ref[0:CR], 126, 1)


def halves(a, b):
    lane = lax.broadcasted_iota(jnp.int32, a.shape, 1)
    return jnp.where(lane < 64, a, pltpu.roll(b, 64, 1)), jnp.where(lane < 64, pltpu.roll(a, 64, 1), b)


def first_kernel(rad_ref, span_ref, dis_hbm, step_hbm, psi_hbm, src_hbm, jr_hbm, jc_hbm,
                 part_ref, psi_ref, jrb_ref, jce_ref, dis_ref, step_ref, src_ref, jr_ref, jc_ref, pad_ref, sem, sem_small):
    rad = rad_ref[0]
    small = [pltpu.make_async_copy(a, b, sem_small.at[i]) for i, (a, b) in enumerate([
        (dis_hbm, dis_ref), (step_hbm, step_ref)])]
    copies = []
    for t in range(TD):
        tf = pl.ds(t * NF, NF)
        copies.append([
            pltpu.make_async_copy(psi_hbm.at[tf], psi_ref.at[tf], sem.at[t, 0]),
            pltpu.make_async_copy(jr_hbm.at[t], jr_ref.at[t], sem.at[t, 1]),
            pltpu.make_async_copy(jc_hbm.at[t], jc_ref.at[t], sem.at[t, 2]),
            pltpu.make_async_copy(src_hbm.at[tf], src_ref.at[tf], sem.at[t, 3]),
        ])
    for copy in small + copies[0] + copies[1]:
        copy.start()
    clear_pad(pad_ref)
    lane = lax.broadcasted_iota(jnp.int32, (CR, 128), 1)
    for copy in small:
        copy.wait()
    for t in range(TD):
        for copy in copies[t]:
            copy.wait()

        @pl.when((span_ref[0] == 1) | (t == 0))
        def _():
            interior_pass(t, psi_ref, src_ref, jr_ref, jc_ref, dis_ref, step_ref, pad_ref, part_ref)

        for i in range(NF):
            for j in range(NF):
                whole = jr_ref[t, i, j].astype(F32)
                jrb_ref[t * NF + i, j:j + 1] = jnp.where(rad == 0, whole[CR - 1:CR], whole[0:1])
                jce_ref[t * NF + i, j] = jnp.where(
                    lane < 64, jc_ref[t, i, j, :, lanes(0)].astype(F32), jc_ref[t, i, j, :, lanes(LT - 1)].astype(F32)).astype(BF)


def send_kernel(rad_ref, span_ref, psi_ref, part_ref, edge_ref, halo_ref, jrb_ref, jce_ref, dis_ref, step_ref, src_hbm, jr_hbm, jc_hbm,
                x_hbm, w_ref, w_edge_ref, w_halo_ref, rim_ref, x_ref, src_ref, jr_ref, jc_ref, pad_ref, late_ref, sem, sem_in):
    rad = rad_ref[0]


    @pl.when(span_ref[0] != 0)
    def _():
        late_ref[...] = part_ref[(TD - 1) * NF:]

    @pl.when(span_ref[0] == 0)
    def _():
        last = pl.ds((TD - 1) * NF, NF)
        loads = [pltpu.make_async_copy(a, b, sem_in.at[i]) for i, (a, b) in enumerate(
            [(src_hbm.at[last], src_ref.at[last]), (jr_hbm.at[TD - 1], jr_ref.at[TD - 1]), (jc_hbm.at[TD - 1], jc_ref.at[TD - 1])])]
        for load in loads:
            load.start()
        clear_pad(pad_ref)
        for load in loads:
            load.wait()
        interior_pass(TD - 1, psi_ref, src_ref, jr_ref, jc_ref, dis_ref, step_ref, pad_ref, late_ref, (TD - 1) * NF)

    fixes = [corrections(rad, edge_ref, halo_ref, jrb_ref, jce_ref, dis_ref, t) for t in range(TD)]
    rims = [rim_of(lambda q: halo_ref[20 * (q // 2) + 10 * t:20 * (q // 2) + 10 * t + 10, lanes(q % 2)], edge_ref[t])
            for t in range(TD)]
    low, high = halves(*rims)
    rim_ref[0:48] = low
    rim_ref[48:96] = high
    for e in range(RIM):
        x_ref[pl.ds(BODY + e, 32, stride=ROWS), :] = rim_ref[32 * e:32 * e + 32]
    copies = []
    for q in range(LT):
        for t in range(TD):
            for f in range(NF):
                mid = psi_ref[t * NF + f, :, lanes(q)]
                before = part_ref[f, :, lanes(q)] if t < TD - 1 else late_ref[f, :, lanes(q)]
                w = before - step_ref[:, lanes(q)] * fixes[t](f, q)
                w_ref[t * NF + f, :, lanes(q)] = w
                for h in range(HB):
                    x_ref[pl.ds(q * GRP + row_of(t, 0, f, h), 8, stride=ROWS), :] = mid[8 * h:8 * h + 8]
                    x_ref[pl.ds(q * GRP + row_of(t, 1, f, h), 8, stride=ROWS), :] = w[8 * h:8 * h + 8]
        span = pl.ds(q * GRP, GRP)
        copies.append(pltpu.make_async_copy(x_ref.at[span], x_hbm.at[span], sem.at[q]))
        copies[q].start()
    put_edge(w_edge_ref, lambda tf: (w_ref[tf, :, lanes(0)], w_ref[tf, :, lanes(LT - 1)]))
    start = pl.multiple_of(8 * (1 - rad), 8)
    put_halo(w_halo_ref, lambda tf: w_ref[tf, pl.ds(start, 8), :], rad)
    w_edge_ref[TD] = pack_edge([(step_ref[:, lanes(0)], step_ref[:, lanes(LT - 1)])] * NF)
    sigma = jnp.where(rad == 0, step_ref[CR - 2:CR], step_ref[0:2])
    w_halo_ref[40:42] = sigma[:, :HALF]
    w_halo_ref[42:44] = sigma[:, HALF:]
    w_halo_ref[44:48] = jnp.zeros((4, HALF), F32)
    for copy in copies:
        copy.wait()


def label_kernel(me_ref, cell_hbm, owner_hbm, local_hbm, step_ref, pick_ref, label_ref, ids_ref, sig_ref, cell_ref, owner_ref,
                 local_ref, sem):
    loads = [pltpu.make_async_copy(a, b, sem.at[i]) for i, (a, b) in enumerate(
        [(cell_hbm, cell_ref), (owner_hbm, owner_ref), (local_hbm, local_ref)])]
    for load in loads:
        load.start()
    for load in loads:
        load.wait()
    ids_ref[0:1] = cell_ref[...] % CT
    ids_ref[1:2] = cell_ref[...] // CT
    ids_ref[2:3] = owner_ref[...]
    ids_ref[3:4] = local_ref[...]
    me = me_ref[0]
    sig = jnp.zeros((2, 128), F32)
    for p in range(8):
        for q in range(LT):
            here = jnp.concatenate([step_ref[p:p + 1, lanes(q)], step_ref[p + 8:p + 9, lanes(q)]], axis=0)
            sig = jnp.where(me == 8 * q + p, here, sig)
    sig_ref[...] = sig
    pick_ref[...] = (lax.broadcasted_iota(jnp.int32, (CT, NODES), 0) == ids_ref[0:1]).astype(F32).astype(BF)
    label_ref[...] = (lax.broadcasted_iota(jnp.int32, (128, NODES), 0) % VAR_DEV == ids_ref[3:4]).astype(F32).astype(BF)


def total_kernel(got_ref, sens_hbm, sens_ref, sem):
    line = jnp.sum(got_ref[...], axis=0, keepdims=True)
    for k in range(3):
        sens_ref[k:k + 1, :] = pltpu.roll(line, (128 - VAR_DEV * k) % 128, 1)[:, :VAR_DEV]
    copy = pltpu.make_async_copy(sens_ref, sens_hbm, sem)
    copy.start()
    copy.wait()


def time_kernel(table_ref, sig_ref, y_ref, edge_ref, halo_ref, pick_ref, label_ref, v_ref, edge_out_ref, halo_out_ref):
    edge_out_ref[...] = edge_ref[...]
    halo_out_ref[...] = halo_ref[...]
    table = table_ref[...]

    def apply(x):
        return jnp.dot(table, pair_up(x), preferred_element_type=F32)

    count = 2 * NF

    def pick(at):
        return y_ref[pl.ds(at, 32, stride=ROWS), :]

    def put(at, value):
        v_ref[pl.ds(at, 32, stride=ROWS), :] = value

    def row(what, m, t):
        return (t * 2 + what) * count + m

    def gather(what):
        return [jnp.concatenate([pick(row(what, m, t)) for t in range(TD)], axis=0) for m in range(count)]

    def scatter(what, value):
        for m in range(count):
            for t in range(TD):
                put(row(what, m, t), value[32 * t:32 * t + 32, lanes(m)])

    rims = [pick(BODY + e) for e in range(RIM)]
    rims = [jnp.concatenate(halves(rims[0], rims[1]), axis=0), jnp.concatenate([rims[2], pltpu.roll(rims[2], 64, 1)], axis=0)]
    sigma = jnp.concatenate([sig_ref[0:1, :], sig_ref[1:2, :]] * NF, axis=1)
    time0 = apply(jnp.concatenate(gather(0) + rims, axis=1))
    scatter(0, time0)
    pair, single = [time0[:, lanes(count + m)] for m in range(2)]
    for e, value in enumerate(halves(pair[:32], pair[32:]) + halves(single[:32], single[32:])[:1]):
        put(BODY + e, value)
    psi1 = jnp.concatenate(gather(1), axis=1) - sigma * time0[:, :128 * count]
    scatter(1, apply(psi1))


def plane(ref, what, t, f, q):
    return jnp.concatenate([ref[pl.ds(q * GRP + row_of(t, what, f, h), 8, stride=ROWS), :] for h in range(HB)], axis=0)


def last_kernel(rad_ref, w_ref, u_ref, w_edge_ref, w_halo_ref, jr_ref, jc_ref, jrb_ref, jce_ref, dis_ref,
                step_ref, src_ref, ids_ref, pick_ref, label_ref, sd_ref, out_hbm, sens_ref, psi1_ref, psi_ref, edge_ref, halo_ref, rim_ref, turn_ref, pad_ref, sem):
    rad = rad_ref[0]
    clear_pad(pad_ref)
    for e in range(RIM):
        rim_ref[32 * e:32 * e + 32] = u_ref[pl.ds(BODY + e, 32, stride=ROWS), :]
    rims = halves(rim_ref[0:48], rim_ref[48:96])
    for t in range(TD):
        for m in range(2):
            at = (2 * t + m) * NF
            for q in range(LT):
                side = q // 2
                here = slice(20 * side + at, 20 * side + at + NF)
                sigma = w_halo_ref[40 + 2 * side + m:41 + 2 * side + m, lanes(q % 2)]
                halo_ref[here, lanes(q % 2)] = (
                    w_halo_ref[here, lanes(q % 2)] - sigma * rims[t][10 * q + NF * m:10 * q + NF * m + NF])
        edge_ref[t] = w_edge_ref[t] - w_edge_ref[TD] * edge_of(rims[t][40:43], turn_ref)
    copies = []
    for t in range(TD):
        fix = corrections(rad, edge_ref, halo_ref, jrb_ref, jce_ref, dis_ref, t)
        for f in range(NF):
            for q in range(LT):
                psi1_ref[t * NF + f, :, lanes(q)] = (
                    w_ref[t * NF + f, :, lanes(q)] - step_ref[:, lanes(q)] * plane(u_ref, 0, t, f, q))
        for q in range(LT):
            cell = lambda f, qq: psi1_ref[t * NF + f, :, lanes(qq)]
            jr = lambda i, j: jr_ref[t, i, j, :, lanes(q)]
            jc = lambda i, j: jc_ref[t, i, j, :, lanes(q)]
            res = interior(cell, pad_ref, jr, jc, dis_ref[:, lanes(q)], q)
            sigma = step_ref[:, lanes(q)]
            for f in range(NF):
                psi_ref[t * NF + f, :, lanes(q)] = cell(f, q) - sigma * (
                    res[f] + fix(f, q) + plane(u_ref, 1, t, f, q) - src_ref[t * NF + f, :, lanes(q)])
        tf = pl.ds(t * NF, NF)
        copies.append(pltpu.make_async_copy(psi_ref.at[tf], out_hbm.at[tf], sem.at[t]))
        copies[t].start()
    pick = pick_ref[...]
    mask = (lax.broadcasted_iota(jnp.int32, (CR, NODES), 0) == ids_ref[1:2]).astype(F32)
    acc = [jnp.zeros((CR, NODES), F32) for _ in range(3)]
    weights = [sd_ref[m].astype(F32) for m in range(3 * NF)]
    size = TD * NF * CR
    whole = psi_ref[...].reshape(size, CT)
    got = jnp.dot(jnp.concatenate(split(whole), axis=0), pick, preferred_element_type=F32)
    got = got[:size] + got[size:2 * size] + got[2 * size:]
    for t in range(TD):
        value = got[t * NF * CR:(t + 1) * NF * CR]
        for f in range(NF):
            here = value[f * CR:(f + 1) * CR]
            for k in range(3):
                acc[k] = acc[k] + here * weights[3 * f + k][t:t + 1]
    owner = ids_ref[2:3]
    parts = []
    for k in range(3):
        kept = acc[k] * mask
        for s in range(2):
            parts.append(kept * (owner == s).astype(F32))
    stack = jnp.concatenate(parts, axis=0)
    label = label_ref[...]
    dims = (((1,), (1,)), ((), ()))
    total = lax.dot_general(jnp.concatenate(split(stack), axis=0), label, dims, preferred_element_type=F32)
    count = stack.shape[0]
    total = total[:count] + total[count:2 * count] + total[2 * count:]
    lane = lax.broadcasted_iota(jnp.int32, (1, 128), 1)
    line = []
    for s in range(2):
        full = jnp.zeros((1, 128), F32)
        for k in range(3):
            at = (k * 2 + s) * CR
            part = jnp.sum(total[at:at + CR], axis=0, keepdims=True)
            full = jnp.where(lane // VAR_DEV == k, part, full)
        line.append(full)
    peer = lax.broadcasted_iota(jnp.int32, (128, 128), 0)
    sens_ref[...] = jnp.where((peer // 2) % 2 == 0, line[0], line[1])
    for copy in copies:
        copy.wait()


VM, SM, HM = pltpu.VMEM, pltpu.SMEM, pltpu.HBM


def call(kernel, ins, outs, scratch=(), micros=1):
    return pl.pallas_call(
        kernel,
        out_shape=[shape for shape, _ in outs],
        in_specs=[pl.BlockSpec(memory_space=space) for space in ins],
        out_specs=[pl.BlockSpec(memory_space=space) for _, space in outs],
        scratch_shapes=list(scratch),
        cost_estimate=pl.CostEstimate(flops=0, bytes_accessed=int(micros * 3.0e6), transcendentals=0),
        compiler_params=pltpu.CompilerParams(vmem_limit_bytes=24 * 1024 * 1024),
    )


def f32(*shape):
    return jax.ShapeDtypeStruct(shape, F32)


def swap_halos(edge, halo):
    halo = lax.ppermute(halo, "rad", SWAP)
    edge = lax.ppermute(edge, "span", SWAP)
    return edge, halo


def body(adjoint_start, jac_rad, jac_circ, dissip, pseudo_step, source, node_cell, node_owner, node_local, shape_deriv):
    me = lax.axis_index("inst").astype(jnp.int32).reshape(1)
    rad = lax.axis_index("rad").astype(jnp.int32).reshape(1)
    span = lax.axis_index("span").astype(jnp.int32).reshape(1)
    n = TD * NF
    psi0 = adjoint_start.reshape(n, CR, CT)
    src = source.reshape(n, CR, CT)
    full = f32(n, CR, CT)
    line = (1, NODES)
    flat = f32(CR, CT)
    dma = pltpu.SemaphoreType.DMA
    pad = VM((NF * 32, 128), F32)
    held = [pltpu.with_memory_space_constraint(a, pltpu.HBM) for a in (
        dissip, pseudo_step, node_cell.reshape(line), node_owner.reshape(line), node_local.reshape(line), psi0, src, jac_rad, jac_circ)]
    edge0, halo0 = call(
        edge_kernel, [SM, HM], [(f32(TD, CR, 128), VM), (f32(40, HALF), VM)],
        [VM((n, 8, CT), F32), VM((n, CR, 128), F32), VM((n, CR, 128), F32), dma((3,))])(rad, held[5])
    edge0, halo0 = swap_halos(edge0, halo0)
    part, psi, jrb, jce, dis, step = call(
        first_kernel, [SM, SM] + [HM] * 6,
        [(full, VM), (full, VM), (f32(n, NF, CT), VM), (jax.ShapeDtypeStruct((n, NF, CR, 128), BF), VM), (flat, VM), (flat, VM)],
        [VM((n, CR, CT), F32), VM(jac_rad.shape, BF), VM(jac_circ.shape, BF), pad, dma((TD, 4)), dma((2,))],
        micros=3)(rad, span, held[0], held[1], *held[5:])
    rim = VM((96, 128), F32)
    swapped = [(f32(TD + 1, CR, 128), VM), (f32(48, HALF), VM)]
    x, w, w_edge, w_halo = call(
        send_kernel, [SM, SM] + [VM] * 8 + [HM] * 3, [(f32(32 * ROWS, 128), HM), (full, VM)] + swapped,
        [rim, VM((32 * ROWS, 128), F32), VM((n, CR, CT), F32), VM(jac_rad.shape, BF), VM(jac_circ.shape, BF), pad, VM((NF, CR, CT), F32),
         dma((LT,)), dma((3,))])(
        rad, span, psi, part, edge0, halo0, jrb, jce, dis, step, *held[6:])
    w_edge, w_halo = swap_halos(w_edge, w_halo)
    y = lax.all_to_all(x.reshape(32 * ROWS, 1, 128), "inst", 0, 0, tiled=True).reshape(32 * ROWS, 128)
    bf16 = lambda *shape: (jax.ShapeDtypeStruct(shape, BF), VM)
    pick, label, ids, sig = call(
        label_kernel, [SM] + [HM] * 3 + [VM],
        [bf16(CT, NODES), bf16(128, NODES), (jax.ShapeDtypeStruct((8, NODES), jnp.int32), VM), (f32(2, 128), VM)],
        [VM(line, jnp.int32)] * 3 + [dma((3,))], micros=40)(me, *held[2:5], step)
    v, w_edge, w_halo = call(
        time_kernel, [VM] * 5 + [pl.ANY] * 2, [(f32(32 * ROWS, 128), VM)] + swapped)(
        jnp.asarray(spectral_blocks()), sig, y, w_edge, w_halo, pick, label)
    u = lax.all_to_all(v.reshape(32 * ROWS, 1, 128), "inst", 0, 0, tiled=True).reshape(32 * ROWS, 128)
    psi2, parts = call(
        last_kernel, [SM] + [VM] * 15, [(full, HM), (f32(128, 128), VM)],
        [VM((n, CR, CT), F32), VM((n, CR, CT), F32), VM((TD, CR, 128), F32), VM((40, HALF), F32), rim, VM((24, 128), F32), pad, dma((TD,))])(
        rad, w, u, w_edge, w_halo, jac_rad, jac_circ, jrb, jce, dis, step, src, ids, pick, label,
        shape_deriv.transpose(1, 2, 0, 3).reshape(3 * NF, TD, NODES))
    got = lax.all_to_all(parts, ALL, 0, 0, tiled=True)
    sens, = call(total_kernel, [VM], [(f32(3, VAR_DEV), HM)], [VM((3, VAR_DEV), F32), dma])(got)
    return psi2.reshape(TD, NF, CR, CT), sens


def solution(mesh):
    in_specs = (
        P("inst", None, "rad", "span"),
        P("inst", None, None, "rad", "span"),
        P("inst", None, None, "rad", "span"),
        P("rad", "span"),
        P("rad", "span"),
        P("inst", None, "rad", "span"),
        P(("span", "rad")),
        P(("span", "rad"), None),
        P(("span", "rad")),
        P("inst", None, None, ("span", "rad")),
    )
    out_specs = (P("inst", None, "rad", "span"), P(None, "span"))
    return jax.shard_map(body, mesh=mesh, in_specs=in_specs, out_specs=out_specs, check_vma=False)
```

```python
import jax
import jax.numpy as jnp
import numpy as np
from jax import lax
from jax.experimental import pallas as pl
from jax.experimental.pallas import tpu as pltpu
from jax.sharding import PartitionSpec as P

NT = 64
TD = 2
NF = 5
CR = 16
CT = 512
LT = 4
HB = 2
BODY = 40
RIM = 3
ROWS = BODY + RIM
HALF = 256
GRP = 8 * ROWS
NODES = 1024
VAR_DEV = 32
EPS4 = 0.0625
F32 = jnp.float32
BF = jnp.bfloat16
SWAP = [(0, 1), (1, 0)]
ALL = ("inst", "span", "rad")


def spectral_blocks():
    index = np.arange(NT)
    diff = index[:, None] - index[None, :]
    safe = np.where(diff == 0, 1, diff)
    table = np.where(diff == 0, 0.0, 0.5 * np.where(diff % 2 == 0, 1.0, -1.0) / np.tan(np.pi * safe / NT))
    order = np.concatenate([index[0::2], index[1::2]])
    apply = table.T[order][:, order].astype(np.float32)
    pieces = []
    for _ in range(3):
        pieces.append(apply.astype(BF))
        apply = apply - pieces[-1].astype(np.float32)
    high, mid, _ = pieces
    return np.concatenate([high, high, mid, mid, high], axis=1)


def split(x):
    pieces = []
    for _ in range(3):
        pieces.append(x.astype(BF))
        x = x - pieces[-1].astype(F32)
    return pieces


def pair_up(x):
    high, mid, low = split(x)
    return jnp.concatenate([high, mid, high, mid, low], axis=0)


def row_of(t, what, f, h):
    return ((t * 2 + what) * NF + f) * HB + h


def lanes(q):
    return slice(128 * q, 128 * q + 128)


def interior(cell, pad_ref, jr, jc, dis, q):
    lane = lax.broadcasted_iota(jnp.int32, (CR, 128), 1)
    none = jnp.zeros((CR, 128), F32)
    d_rad, d_circ, fourth = [], [], []
    for f in range(NF):
        mid = cell(f, q)
        left = none if q == 0 else cell(f, q - 1)
        right = none if q == LT - 1 else cell(f, q + 1)
        m1 = jnp.where(lane < 1, pltpu.roll(left, 1, 1), pltpu.roll(mid, 1, 1))
        m2 = jnp.where(lane < 2, pltpu.roll(left, 2, 1), pltpu.roll(mid, 2, 1))
        p1 = jnp.where(lane >= 127, pltpu.roll(right, 127, 1), pltpu.roll(mid, 127, 1))
        p2 = jnp.where(lane >= 126, pltpu.roll(right, 126, 1), pltpu.roll(mid, 126, 1))
        base = f * 32
        pad_ref[base + 8:base + 24, :] = mid
        rm2 = pad_ref[base + 6:base + 22, :]
        rm1 = pad_ref[base + 7:base + 23, :]
        rp1 = pad_ref[base + 9:base + 25, :]
        rp2 = pad_ref[base + 10:base + 26, :]
        d_circ.append(0.5 * (m1 - p1))
        d_rad.append(0.5 * (rm1 - rp1))
        fourth.append((m2 + p2) + (rm2 + rp2) - 4.0 * ((m1 + p1) + (rm1 + rp1)) + 12.0 * mid)
    out = []
    for j in range(NF):
        acc = (EPS4 * dis) * fourth[j]
        for i in range(NF):
            acc = acc + jr(i, j).astype(F32) * d_rad[i]
            acc = acc + jc(i, j).astype(F32) * d_circ[i]
        out.append(acc)
    return out


def clear_pad(pad_ref):
    for f in range(NF):
        for at in (32 * f, 32 * f + 24):
            pad_ref[at:at + 8, :] = jnp.zeros((8, 128), F32)


def halo_rows(ref, at, count):
    return jnp.concatenate([ref[at:at + count, :], ref[20 + at:20 + at + count, :]], axis=1)


def corrections(rad, edge_ref, halo_ref, jrb_ref, jce_ref, dis_ref, t):
    lane = lax.broadcasted_iota(jnp.int32, (CR, 128), 1)
    diff, fourth = [], []
    edge = edge_ref[t]
    for f in range(NF):
        turn = lambda by: pltpu.roll(edge, (by - 4 * f) % 128, 1)
        m1 = jnp.where(lane < 1, turn(1), 0.0)
        m2 = jnp.where(lane < 2, turn(2), 0.0)
        p1 = jnp.where(lane >= 127, turn(-1), 0.0)
        p2 = jnp.where(lane >= 126, turn(-2), 0.0)
        diff.append(0.5 * (m1 - p1))
        fourth.append(m2 + p2 - 4.0 * (m1 + p1))
    dis_edge = EPS4 * jnp.where(lane < 64, dis_ref[:, lanes(0)], dis_ref[:, lanes(LT - 1)])
    circ = []
    for j in range(NF):
        acc = dis_edge * fourth[j]
        for i in range(NF):
            acc = acc + jce_ref[t * NF + i, j].astype(F32) * diff[i]
        circ.append(acc)
    near_row = jnp.where(rad == 0, CR - 1, 0)
    next_row = jnp.where(rad == 0, CR - 2, 1)
    sign = jnp.where(rad == 0, -0.5, 0.5)
    first, second = [halo_rows(halo_ref, (2 * t + m) * NF, NF) for m in range(2)]
    near = jnp.where(rad == 0, first, second)
    far = jnp.where(rad == 0, second, first)
    dis_near = EPS4 * dis_ref[pl.ds(near_row, 1), :]
    dis_next = EPS4 * dis_ref[pl.ds(next_row, 1), :]
    row_a = dis_near * (far - 4.0 * near)
    for i in range(NF):
        row_a = row_a + jrb_ref[t * NF + i] * (sign * near[i:i + 1])
    row_b = dis_next * near
    riota = lax.broadcasted_iota(jnp.int32, (CR, 128), 0)

    def fix(f, q):
        out = jnp.where(riota == near_row, row_a[f:f + 1, lanes(q)], 0.0)
        out = jnp.where(riota == next_row, row_b[f:f + 1, lanes(q)], out)
        if q == 0:
            out = out + jnp.where(lane < 64, circ[f], 0.0)
        if q == LT - 1:
            out = out + jnp.where(lane >= 64, circ[f], 0.0)
        return out

    return fix


def interior_pass(t, psi_ref, src_ref, jr_ref, jc_ref, dis_ref, step_ref, pad_ref, part_ref, first=0):
    for q in range(LT):
        cell = lambda f, qq: psi_ref[t * NF + f, :, lanes(qq)]
        jr = lambda i, j: jr_ref[t, i, j, :, lanes(q)]
        jc = lambda i, j: jc_ref[t, i, j, :, lanes(q)]
        res = interior(cell, pad_ref, jr, jc, dis_ref[:, lanes(q)], q)
        sigma = step_ref[:, lanes(q)]
        for f in range(NF):
            part_ref[t * NF + f - first, :, lanes(q)] = cell(f, q) - sigma * (res[f] - src_ref[t * NF + f, :, lanes(q)])


def edge_kernel(rad_ref, psi_hbm, edge_ref, halo_ref, rows_ref, left_ref, right_ref, sem):
    rad = rad_ref[0]
    start = pl.multiple_of(8 * (1 - rad), 8)
    copies = [
        pltpu.make_async_copy(psi_hbm.at[:, pl.ds(start, 8), :], rows_ref, sem.at[0]),
        pltpu.make_async_copy(psi_hbm.at[:, :, pl.ds(0, 128)], left_ref, sem.at[1]),
        pltpu.make_async_copy(psi_hbm.at[:, :, pl.ds(CT - 128, 128)], right_ref, sem.at[2]),
    ]
    for copy in copies:
        copy.start()
    copies[0].wait()
    put_halo(halo_ref, lambda tf: rows_ref[tf], rad)
    copies[1].wait()
    copies[2].wait()
    put_edge(edge_ref, lambda tf: (left_ref[tf], right_ref[tf]))


def pack_edge(ends):
    lane = lax.broadcasted_iota(jnp.int32, (CR, 128), 1)
    packed = None
    for f in range(NF):
        both = jnp.where(lane < 64, ends[f][0], ends[f][1])
        if f == 0:
            packed = both
        else:
            packed = jnp.where((lane >= 4 * f - 2) & (lane < 4 * f + 2), pltpu.roll(both, 4 * f, 1), packed)
    return packed


def put_edge(edge_ref, ends):
    for t in range(TD):
        edge_ref[t] = pack_edge([ends(t * NF + f) for f in range(NF)])


def put_halo(halo_ref, tile, rad):
    for t in range(TD):
        for f in range(NF):
            rows = tile(t * NF + f)
            pair = jnp.where(rad == 0, rows[6:8], rows[0:2])
            for m in range(2):
                put_row(halo_ref, (2 * t + m) * NF + f, pair[m:m + 1])


def put_row(halo_ref, at, row):
    halo_ref[at:at + 1] = row[:, :HALF]
    halo_ref[20 + at:21 + at] = row[:, HALF:]


def rim_of(tile, edge):
    lane = lax.broadcasted_iota(jnp.int32, (3, 128), 1)
    turned = pltpu.roll(edge, 2, 1)
    turned = jnp.concatenate([turned, jnp.zeros((8, 128), F32)], axis=0)
    dense = jnp.zeros((3, 128), F32)
    for g in range(6):
        part = turned[3 * g:3 * g + 3]
        part = pltpu.roll(part, 20 * g, 1) if g else part
        dense = jnp.where((lane >= 20 * g) & (lane < 20 * g + 20), part, dense)
    return jnp.concatenate([tile(q) for q in range(LT)] + [dense, jnp.zeros((5, 128), F32)], axis=0)


def edge_of(dense, edge_ref):
    for g in range(6):
        edge_ref[3 * g:3 * g + 3] = pltpu.roll(dense, 128 - 20 * g, 1) if g else dense
    return pltpu.roll(edge_ref[0:CR], 126, 1)


def halves(a, b):
    lane = lax.broadcasted_iota(jnp.int32, a.shape, 1)
    return jnp.where(lane < 64, a, pltpu.roll(b, 64, 1)), jnp.where(lane < 64, pltpu.roll(a, 64, 1), b)


def first_kernel(rad_ref, span_ref, dis_hbm, step_hbm, psi_hbm, src_hbm, jr_hbm, jc_hbm,
                 part_ref, psi_ref, jrb_ref, jce_ref, dis_ref, step_ref, src_ref, jr_ref, jc_ref, pad_ref, sem, sem_small):
    rad = rad_ref[0]
    small = [pltpu.make_async_copy(a, b, sem_small.at[i]) for i, (a, b) in enumerate([
        (dis_hbm, dis_ref), (step_hbm, step_ref)])]
    copies = []
    for t in range(TD):
        tf = pl.ds(t * NF, NF)
        copies.append([
            pltpu.make_async_copy(psi_hbm.at[tf], psi_ref.at[tf], sem.at[t, 0]),
            pltpu.make_async_copy(jr_hbm.at[t], jr_ref.at[t], sem.at[t, 1]),
            pltpu.make_async_copy(jc_hbm.at[t], jc_ref.at[t], sem.at[t, 2]),
            pltpu.make_async_copy(src_hbm.at[tf], src_ref.at[tf], sem.at[t, 3]),
        ])
    for copy in small + copies[0] + copies[1]:
        copy.start()
    clear_pad(pad_ref)
    lane = lax.broadcasted_iota(jnp.int32, (CR, 128), 1)
    for copy in small:
        copy.wait()
    for t in range(TD):
        for copy in copies[t]:
            copy.wait()

        @pl.when((span_ref[0] == 1) | (t == 0))
        def _():
            interior_pass(t, psi_ref, src_ref, jr_ref, jc_ref, dis_ref, step_ref, pad_ref, part_ref)

        for i in range(NF):
            for j in range(NF):
                whole = jr_ref[t, i, j].astype(F32)
                jrb_ref[t * NF + i, j:j + 1] = jnp.where(rad == 0, whole[CR - 1:CR], whole[0:1])
                jce_ref[t * NF + i, j] = jnp.where(
                    lane < 64, jc_ref[t, i, j, :, lanes(0)].astype(F32), jc_ref[t, i, j, :, lanes(LT - 1)].astype(F32)).astype(BF)


def send_kernel(rad_ref, span_ref, psi_ref, part_ref, edge_ref, halo_ref, jrb_ref, jce_ref, dis_ref, step_ref, src_hbm, jr_hbm, jc_hbm,
                x_hbm, w_ref, w_edge_ref, w_halo_ref, rim_ref, x_ref, src_ref, jr_ref, jc_ref, pad_ref, late_ref, sem, sem_in):
    rad = rad_ref[0]


    @pl.when(span_ref[0] != 0)
    def _():
        late_ref[...] = part_ref[(TD - 1) * NF:]

    @pl.when(span_ref[0] == 0)
    def _():
        last = pl.ds((TD - 1) * NF, NF)
        loads = [pltpu.make_async_copy(a, b, sem_in.at[i]) for i, (a, b) in enumerate(
            [(src_hbm.at[last], src_ref.at[last]), (jr_hbm.at[TD - 1], jr_ref.at[TD - 1]), (jc_hbm.at[TD - 1], jc_ref.at[TD - 1])])]
        for load in loads:
            load.start()
        clear_pad(pad_ref)
        for load in loads:
            load.wait()
        interior_pass(TD - 1, psi_ref, src_ref, jr_ref, jc_ref, dis_ref, step_ref, pad_ref, late_ref, (TD - 1) * NF)

    fixes = [corrections(rad, edge_ref, halo_ref, jrb_ref, jce_ref, dis_ref, t) for t in range(TD)]
    rims = [rim_of(lambda q: halo_ref[20 * (q // 2) + 10 * t:20 * (q // 2) + 10 * t + 10, lanes(q % 2)], edge_ref[t])
            for t in range(TD)]
    low, high = halves(*rims)
    rim_ref[0:48] = low
    rim_ref[48:96] = high
    for e in range(RIM):
        x_ref[pl.ds(BODY + e, 32, stride=ROWS), :] = rim_ref[32 * e:32 * e + 32]
    copies = []
    for q in range(LT):
        for t in range(TD):
            for f in range(NF):
                mid = psi_ref[t * NF + f, :, lanes(q)]
                before = part_ref[f, :, lanes(q)] if t < TD - 1 else late_ref[f, :, lanes(q)]
                w = before - step_ref[:, lanes(q)] * fixes[t](f, q)
                w_ref[t * NF + f, :, lanes(q)] = w
                for h in range(HB):
                    x_ref[pl.ds(q * GRP + row_of(t, 0, f, h), 8, stride=ROWS), :] = mid[8 * h:8 * h + 8]
                    x_ref[pl.ds(q * GRP + row_of(t, 1, f, h), 8, stride=ROWS), :] = w[8 * h:8 * h + 8]
        span = pl.ds(q * GRP, GRP)
        copies.append(pltpu.make_async_copy(x_ref.at[span], x_hbm.at[span], sem.at[q]))
        copies[q].start()
    put_edge(w_edge_ref, lambda tf: (w_ref[tf, :, lanes(0)], w_ref[tf, :, lanes(LT - 1)]))
    start = pl.multiple_of(8 * (1 - rad), 8)
    put_halo(w_halo_ref, lambda tf: w_ref[tf, pl.ds(start, 8), :], rad)
    w_edge_ref[TD] = pack_edge([(step_ref[:, lanes(0)], step_ref[:, lanes(LT - 1)])] * NF)
    sigma = jnp.where(rad == 0, step_ref[CR - 2:CR], step_ref[0:2])
    w_halo_ref[40:42] = sigma[:, :HALF]
    w_halo_ref[42:44] = sigma[:, HALF:]
    w_halo_ref[44:48] = jnp.zeros((4, HALF), F32)
    for copy in copies:
        copy.wait()


def label_kernel(me_ref, cell_hbm, owner_hbm, local_hbm, step_ref, pick_ref, label_ref, ids_ref, sig_ref, cell_ref, owner_ref,
                 local_ref, sem):
    loads = [pltpu.make_async_copy(a, b, sem.at[i]) for i, (a, b) in enumerate(
        [(cell_hbm, cell_ref), (owner_hbm, owner_ref), (local_hbm, local_ref)])]
    for load in loads:
        load.start()
    for load in loads:
        load.wait()
    ids_ref[0:1] = cell_ref[...] % CT
    ids_ref[1:2] = cell_ref[...] // CT
    ids_ref[2:3] = owner_ref[...]
    ids_ref[3:4] = local_ref[...]
    me = me_ref[0]
    sig = jnp.zeros((2, 128), F32)
    for p in range(8):
        for q in range(LT):
            here = jnp.concatenate([step_ref[p:p + 1, lanes(q)], step_ref[p + 8:p + 9, lanes(q)]], axis=0)
            sig = jnp.where(me == 8 * q + p, here, sig)
    sig_ref[...] = sig
    pick_ref[...] = (lax.broadcasted_iota(jnp.int32, (CT, NODES), 0) == ids_ref[0:1]).astype(F32).astype(BF)
    label_ref[...] = (lax.broadcasted_iota(jnp.int32, (128, NODES), 0) % VAR_DEV == ids_ref[3:4]).astype(F32).astype(BF)


def total_kernel(got_ref, sens_ref):
    line = jnp.sum(got_ref[...], axis=0, keepdims=True)
    for k in range(3):
        sens_ref[k:k + 1, :] = pltpu.roll(line, (128 - VAR_DEV * k) % 128, 1)[:, :VAR_DEV]


def time_kernel(table_ref, sig_ref, y_ref, edge_ref, halo_ref, pick_ref, label_ref, v_ref, edge_out_ref, halo_out_ref):
    edge_out_ref[...] = edge_ref[...]
    halo_out_ref[...] = halo_ref[...]
    table = table_ref[...]

    def apply(x):
        return jnp.dot(table, pair_up(x), preferred_element_type=F32)

    count = 2 * NF

    def pick(at):
        return y_ref[pl.ds(at, 32, stride=ROWS), :]

    def put(at, value):
        v_ref[pl.ds(at, 32, stride=ROWS), :] = value

    def row(what, m, t):
        return (t * 2 + what) * count + m

    def gather(what):
        return [jnp.concatenate([pick(row(what, m, t)) for t in range(TD)], axis=0) for m in range(count)]

    def scatter(what, value):
        for m in range(count):
            for t in range(TD):
                put(row(what, m, t), value[32 * t:32 * t + 32, lanes(m)])

    rims = [pick(BODY + e) for e in range(RIM)]
    rims = [jnp.concatenate(halves(rims[0], rims[1]), axis=0), jnp.concatenate([rims[2], pltpu.roll(rims[2], 64, 1)], axis=0)]
    sigma = jnp.concatenate([sig_ref[0:1, :], sig_ref[1:2, :]] * NF, axis=1)
    time0 = apply(jnp.concatenate(gather(0) + rims, axis=1))
    scatter(0, time0)
    pair, single = [time0[:, lanes(count + m)] for m in range(2)]
    for e, value in enumerate(halves(pair[:32], pair[32:]) + halves(single[:32], single[32:])[:1]):
        put(BODY + e, value)
    psi1 = jnp.concatenate(gather(1), axis=1) - sigma * time0[:, :128 * count]
    scatter(1, apply(psi1))


def plane(ref, what, t, f, q):
    return jnp.concatenate([ref[pl.ds(q * GRP + row_of(t, what, f, h), 8, stride=ROWS), :] for h in range(HB)], axis=0)


def last_kernel(rad_ref, w_ref, u_ref, w_edge_ref, w_halo_ref, jr_ref, jc_ref, jrb_ref, jce_ref, dis_ref,
                step_ref, src_ref, ids_ref, pick_ref, label_ref, sd_ref, out_hbm, sens_ref, psi1_ref, psi_ref, edge_ref, halo_ref, rim_ref, turn_ref, pad_ref, sem):
    rad = rad_ref[0]
    clear_pad(pad_ref)
    for e in range(RIM):
        rim_ref[32 * e:32 * e + 32] = u_ref[pl.ds(BODY + e, 32, stride=ROWS), :]
    rims = halves(rim_ref[0:48], rim_ref[48:96])
    for t in range(TD):
        for m in range(2):
            at = (2 * t + m) * NF
            for q in range(LT):
                side = q // 2
                here = slice(20 * side + at, 20 * side + at + NF)
                sigma = w_halo_ref[40 + 2 * side + m:41 + 2 * side + m, lanes(q % 2)]
                halo_ref[here, lanes(q % 2)] = (
                    w_halo_ref[here, lanes(q % 2)] - sigma * rims[t][10 * q + NF * m:10 * q + NF * m + NF])
        edge_ref[t] = w_edge_ref[t] - w_edge_ref[TD] * edge_of(rims[t][40:43], turn_ref)
    copies = []
    for t in range(TD):
        fix = corrections(rad, edge_ref, halo_ref, jrb_ref, jce_ref, dis_ref, t)
        for f in range(NF):
            for q in range(LT):
                psi1_ref[t * NF + f, :, lanes(q)] = (
                    w_ref[t * NF + f, :, lanes(q)] - step_ref[:, lanes(q)] * plane(u_ref, 0, t, f, q))
        for q in range(LT):
            cell = lambda f, qq: psi1_ref[t * NF + f, :, lanes(qq)]
            jr = lambda i, j: jr_ref[t, i, j, :, lanes(q)]
            jc = lambda i, j: jc_ref[t, i, j, :, lanes(q)]
            res = interior(cell, pad_ref, jr, jc, dis_ref[:, lanes(q)], q)
            sigma = step_ref[:, lanes(q)]
            for f in range(NF):
                psi_ref[t * NF + f, :, lanes(q)] = cell(f, q) - sigma * (
                    res[f] + fix(f, q) + plane(u_ref, 1, t, f, q) - src_ref[t * NF + f, :, lanes(q)])
        tf = pl.ds(t * NF, NF)
        copies.append(pltpu.make_async_copy(psi_ref.at[tf], out_hbm.at[tf], sem.at[t]))
        copies[t].start()
    pick = pick_ref[...]
    mask = (lax.broadcasted_iota(jnp.int32, (CR, NODES), 0) == ids_ref[1:2]).astype(F32)
    acc = [jnp.zeros((CR, NODES), F32) for _ in range(3)]
    weights = [sd_ref[m].astype(F32) for m in range(3 * NF)]
    size = TD * NF * CR
    whole = psi_ref[...].reshape(size, CT)
    got = jnp.dot(jnp.concatenate(split(whole), axis=0), pick, preferred_element_type=F32)
    got = got[:size] + got[size:2 * size] + got[2 * size:]
    for t in range(TD):
        value = got[t * NF * CR:(t + 1) * NF * CR]
        for f in range(NF):
            here = value[f * CR:(f + 1) * CR]
            for k in range(3):
                acc[k] = acc[k] + here * weights[3 * f + k][t:t + 1]
    owner = ids_ref[2:3]
    parts = []
    for k in range(3):
        kept = acc[k] * mask
        for s in range(2):
            parts.append(kept * (owner == s).astype(F32))
    stack = jnp.concatenate(parts, axis=0)
    label = label_ref[...]
    dims = (((1,), (1,)), ((), ()))
    total = lax.dot_general(jnp.concatenate(split(stack), axis=0), label, dims, preferred_element_type=F32)
    count = stack.shape[0]
    total = total[:count] + total[count:2 * count] + total[2 * count:]
    lane = lax.broadcasted_iota(jnp.int32, (1, 128), 1)
    line = []
    for s in range(2):
        full = jnp.zeros((1, 128), F32)
        for k in range(3):
            at = (k * 2 + s) * CR
            part = jnp.sum(total[at:at + CR], axis=0, keepdims=True)
            full = jnp.where(lane // VAR_DEV == k, part, full)
        line.append(full)
    peer = lax.broadcasted_iota(jnp.int32, (128, 128), 0)
    sens_ref[...] = jnp.where((peer // 2) % 2 == 0, line[0], line[1])
    for copy in copies:
        copy.wait()


VM, SM, HM = pltpu.VMEM, pltpu.SMEM, pltpu.HBM


def call(kernel, ins, outs, scratch=(), micros=1):
    return pl.pallas_call(
        kernel,
        out_shape=[shape for shape, _ in outs],
        in_specs=[pl.BlockSpec(memory_space=space) for space in ins],
        out_specs=[pl.BlockSpec(memory_space=space) for _, space in outs],
        scratch_shapes=list(scratch),
        cost_estimate=pl.CostEstimate(flops=0, bytes_accessed=int(micros * 3.0e6), transcendentals=0),
        compiler_params=pltpu.CompilerParams(vmem_limit_bytes=24 * 1024 * 1024),
    )


def f32(*shape):
    return jax.ShapeDtypeStruct(shape, F32)


def swap_halos(edge, halo):
    halo = lax.ppermute(halo, "rad", SWAP)
    edge = lax.ppermute(edge, "span", SWAP)
    return edge, halo


def body(adjoint_start, jac_rad, jac_circ, dissip, pseudo_step, source, node_cell, node_owner, node_local, shape_deriv):
    me = lax.axis_index("inst").astype(jnp.int32).reshape(1)
    rad = lax.axis_index("rad").astype(jnp.int32).reshape(1)
    span = lax.axis_index("span").astype(jnp.int32).reshape(1)
    n = TD * NF
    psi0 = adjoint_start.reshape(n, CR, CT)
    src = source.reshape(n, CR, CT)
    full = f32(n, CR, CT)
    line = (1, NODES)
    flat = f32(CR, CT)
    dma = pltpu.SemaphoreType.DMA
    pad = VM((NF * 32, 128), F32)
    held = [pltpu.with_memory_space_constraint(a, pltpu.HBM) for a in (
        dissip, pseudo_step, node_cell.reshape(line), node_owner.reshape(line), node_local.reshape(line), psi0, src, jac_rad, jac_circ)]
    edge0, halo0 = call(
        edge_kernel, [SM, HM], [(f32(TD, CR, 128), VM), (f32(40, HALF), VM)],
        [VM((n, 8, CT), F32), VM((n, CR, 128), F32), VM((n, CR, 128), F32), dma((3,))])(rad, held[5])
    edge0, halo0 = swap_halos(edge0, halo0)
    part, psi, jrb, jce, dis, step = call(
        first_kernel, [SM, SM] + [HM] * 6,
        [(full, VM), (full, VM), (f32(n, NF, CT), VM), (jax.ShapeDtypeStruct((n, NF, CR, 128), BF), VM), (flat, VM), (flat, VM)],
        [VM((n, CR, CT), F32), VM(jac_rad.shape, BF), VM(jac_circ.shape, BF), pad, dma((TD, 4)), dma((2,))],
        micros=3)(rad, span, held[0], held[1], *held[5:])
    rim = VM((96, 128), F32)
    swapped = [(f32(TD + 1, CR, 128), VM), (f32(48, HALF), VM)]
    x, w, w_edge, w_halo = call(
        send_kernel, [SM, SM] + [VM] * 8 + [HM] * 3, [(f32(32 * ROWS, 128), HM), (full, VM)] + swapped,
        [rim, VM((32 * ROWS, 128), F32), VM((n, CR, CT), F32), VM(jac_rad.shape, BF), VM(jac_circ.shape, BF), pad, VM((NF, CR, CT), F32),
         dma((LT,)), dma((3,))])(
        rad, span, psi, part, edge0, halo0, jrb, jce, dis, step, *held[6:])
    w_edge, w_halo = swap_halos(w_edge, w_halo)
    y = lax.all_to_all(x.reshape(32 * ROWS, 1, 128), "inst", 0, 0, tiled=True).reshape(32 * ROWS, 128)
    bf16 = lambda *shape: (jax.ShapeDtypeStruct(shape, BF), VM)
    pick, label, ids, sig = call(
        label_kernel, [SM] + [HM] * 3 + [VM],
        [bf16(CT, NODES), bf16(128, NODES), (jax.ShapeDtypeStruct((8, NODES), jnp.int32), VM), (f32(2, 128), VM)],
        [VM(line, jnp.int32)] * 3 + [dma((3,))], micros=40)(me, *held[2:5], step)
    v, w_edge, w_halo = call(
        time_kernel, [VM] * 5 + [pl.ANY] * 2, [(f32(32 * ROWS, 128), VM)] + swapped)(
        jnp.asarray(spectral_blocks()), sig, y, w_edge, w_halo, pick, label)
    u = lax.all_to_all(v.reshape(32 * ROWS, 1, 128), "inst", 0, 0, tiled=True).reshape(32 * ROWS, 128)
    psi2, parts = call(
        last_kernel, [SM] + [VM] * 15, [(full, HM), (f32(128, 128), VM)],
        [VM((n, CR, CT), F32), VM((n, CR, CT), F32), VM((TD, CR, 128), F32), VM((40, HALF), F32), rim, VM((24, 128), F32), pad, dma((TD,))])(
        rad, w, u, w_edge, w_halo, jac_rad, jac_circ, jrb, jce, dis, step, src, ids, pick, label,
        shape_deriv.transpose(1, 2, 0, 3).reshape(3 * NF, TD, NODES))
    got = lax.all_to_all(parts, ALL, 0, 0, tiled=True)
    sens, = call(total_kernel, [VM], [(f32(3, VAR_DEV), VM)])(got)
    return psi2.reshape(TD, NF, CR, CT), sens


def solution(mesh):
    in_specs = (
        P("inst", None, "rad", "span"),
        P("inst", None, None, "rad", "span"),
        P("inst", None, None, "rad", "span"),
        P("rad", "span"),
        P("rad", "span"),
        P("inst", None, "rad", "span"),
        P(("span", "rad")),
        P(("span", "rad"), None),
        P(("span", "rad")),
        P("inst", None, None, ("span", "rad")),
    )
    out_specs = (P("inst", None, "rad", "span"), P(None, "span"))
    return jax.shard_map(body, mesh=mesh, in_specs=in_specs, out_specs=out_specs, check_vma=False)
```
